32 devices in a mesh: row: 4 (over x, core), col: 2 (over y), exp: 4 (over z).
Axes of the slice: x: 2, y: 2, z: 4, core: 2. Of those that a mesh axis runs over, the one named last changes fastest.
Arguments:
- layer_input: bfloat16 [5120, 2048], P(('row', 'exp'), 'col'), may hold values from -6 to 6
- lengths: int32 [4, 3], P('exp'), may hold values from 1 to 1024, 1280 in all within a row
- routes: int32 [2, 2560, 6], P('col', ('row', 'exp')), may hold values from 0 to 15, all different within a row; in each aligned block of 160 rows (0 to 159, 160 to 319, ..., all dimensions but the last counted through in order) at most 90 rows name the same one
- norm1_gain: float32 [2048], replicated, may hold values from 0.5 to 1.5
- w_query: bfloat16 [2048, 3072], P('col', 'row'), may hold values from -0.125 to 0.125
- w_latent: bfloat16 [2, 1024, 576], P('col', 'row'), may hold values from -0.125 to 0.125
- latent_gain: float32 [512], replicated, may hold values from 0.5 to 1.5
- w_kv: bfloat16 [512, 4096], P(None, ('row', 'col')), may hold values from -0.25 to 0.25
- w_out: bfloat16 [2048, 2048], P('row', 'col'), may hold values from -2 to 2
- norm2_gain: float32 [2048], replicated, may hold values from 0.5 to 1.5
- shared_gate: bfloat16 [2048, 2816], P('col', 'row'), may hold values from -0.125 to 0.125
- shared_up: bfloat16 [2048, 2816], P('col', 'row'), may hold values from -0.125 to 0.125
- shared_down: bfloat16 [2816, 2048], P('row', 'col'), may hold values from -0.21875 to 0.21875
- router: bfloat16 [2048, 16], replicated, may hold values from -0.0625 to 0.0625
- expert_gate: bfloat16 [16, 2048, 1408], P(('row', 'exp'), None, 'col'), may hold values from -0.125 to 0.125
- expert_up: bfloat16 [16, 2048, 1408], P(('row', 'exp'), None, 'col'), may hold values from -0.125 to 0.125
- expert_down: bfloat16 [16, 2048, 1408], P(('row', 'exp'), None, 'col'), may hold values from -0.4375 to 0.4375
- cotangent: bfloat16 [5120, 2048], P(('row', 'exp'), 'col'), may hold values from -6 to 6
Outputs:
- layer_output: bfloat16 [5120, 2048], P(('row', 'exp'), 'col')
- input_grad: float32 [5120, 2048], P(('row', 'exp'), 'col')
- norm1_gain_grad: float32 [2048], replicated
- w_query_grad: float32 [2048, 3072], P('col', 'row')
- w_latent_grad: float32 [2, 1024, 576], P('col', 'row')
- latent_gain_grad: float32 [512], replicated
- w_kv_grad: float32 [512, 4096], P(None, ('row', 'col'))
- w_out_grad: float32 [2048, 2048], P('row', 'col')
- norm2_gain_grad: float32 [2048], replicated
- shared_gate_grad: float32 [2048, 2816], P('col', 'row')
- shared_up_grad: float32 [2048, 2816], P('col', 'row')
- shared_down_grad: float32 [2816, 2048], P('row', 'col')
- router_grad: float32 [2048, 16], replicated
- expert_gate_grad: float32 [16, 2048, 1408], P(('row', 'exp'), None, 'col')
- expert_up_grad: float32 [16, 2048, 1408], P(('row', 'exp'), None, 'col')
- expert_down_grad: float32 [16, 2048, 1408], P(('row', 'exp'), None, 'col')
The draws below stay inside these ranges and needn't reach their ends.
Inputs may be any that keep to these rules, and one draw needn't show every extreme that they name: `routes`: each row of a token names 6 different experts. In the rows of one device (aligned blocks of 160 rows of the second dimension, for each first index) no expert is named more than 90 times, a bound that some block reaches. `lengths`: each row sums to 1280, and its largest entry is exactly 1024.
All inputs are finite; a program needn't handle non-finite values.
Results may differ from the reference program's by a relative error of at most 0.02.
Values may be sent and summed in bfloat16 or wider, within the bound.
A program may use at most 320 MiB of HBM per device.

```python
import math
import jax
import jax.numpy as jnp
import numpy as np
from jax import lax

D = 2048
H = 16
QK_NOPE = 128
ROPE = 64
KV_RANK = 512
V_DIM = 128
FF_E = 1408
SHARED = 2
TOPK = 6
TOK_DEV = 160
SEQS = 3
GROUPS = 4
GROUP_TOK = 1280
TOKENS = 5120
EXPERTS = 16
SEQ_MOST = 1024
CAP = 90
N_COL = 2
DEVICES = 32


def block_levels(key, shape, pieces, smallest, top_value):
    factor_of = 1.0
    for dim, parts in pieces:
        draws = jax.random.uniform(jax.random.fold_in(jax.random.fold_in(key, 6), dim), (parts,), jnp.float32, smallest / len(pieces), top_value / len(pieces))
        factor_of = factor_of * jnp.repeat(jnp.exp(draws), shape[dim] // parts).reshape((-1,) + (1,) * (len(shape) - 1 - dim))
    return factor_of


def split_up(amount, total, bound, slope):
    portions = [(1 << 20) // math.isqrt(standing ** slope) + 1 for standing in range(2, amount + 1)]
    spare, given = total - bound - (amount - 1), [1] * (amount - 1)
    while spare > 0:
        movable = [i for i in range(amount - 1) if given[i] < bound]
        mass, left = sum([portions[i] for i in movable]), spare
        for i in movable:
            more = min(bound - given[i], max(1, left * portions[i] // mass), spare)
            given[i] = given[i] + more
            spare = spare - more
    return np.array([bound] + given)


def uneven_parts(key, number_of, total, reach, lean):
    if number_of == 2:
        one = jax.random.randint(key, (), max(1, total - reach), min(reach, total - 1) + 1)
        return jnp.stack([one, total - one])
    tallies = jnp.asarray(split_up(number_of, total, reach, lean), jnp.int32)
    pairs = (number_of - 1) // 2
    donor, receiver = tallies[1:1 + 2 * pairs:2], tallies[2:2 + 2 * pairs:2]
    margin = jnp.minimum(donor - 1, reach - receiver)
    shifted = jax.random.randint(jax.random.fold_in(key, 1), (pairs,), 0, 1 << 20) % (margin + 1)
    tallies = tallies.at[1:1 + 2 * pairs:2].set(donor - shifted).at[2:2 + 2 * pairs:2].set(receiver + shifted)
    return tallies[jax.random.permutation(jax.random.fold_in(key, 2), number_of)]


def routed_block(key, own, number, rows, number_of, top, reach, slope):
    sequence = jax.random.permutation(key, number_of)
    crowded, common = portions_of(number_of, rows * top, reach, slope, True), portions_of(number_of, rows * top, reach, slope, False)
    places = jnp.arange(number_of)

    def named(tallies, turn):
        used = int((tallies > 0).sum())
        fixed = max(1, used // 4)
        moved = fixed + (places - fixed + turn * (used - fixed)) % max(1, number_of - fixed)
        return jnp.zeros((number_of,), jnp.int32).at[sequence[jnp.where(places < fixed, places, moved)]].set(jnp.asarray(tallies, jnp.int32))

    tallies = jnp.where(number % 4 == 0, named(crowded, number // 4), named(common, number - number // 4 - 1))
    mixed = jax.random.permutation(jax.random.fold_in(own, 3), number_of)
    donor, sink = mixed[0:number_of // 2 * 2:2], mixed[1:number_of // 2 * 2:2]
    room = jnp.minimum(tallies[donor] - 1, reach - tallies[sink]) // 2
    room = jnp.where((donor == sequence[0]) | (sink == sequence[0]) | (tallies[sink] == 0), 0, jnp.maximum(room, 0))
    moved = jax.random.randint(jax.random.fold_in(own, 4), (number_of // 2,), 0, 1 << 20) % (room + 1)
    tallies = tallies.at[donor].add(-moved).at[sink].add(moved)
    members = jnp.searchsorted(jnp.cumsum(tallies), jnp.arange(rows * top), side="right").astype(jnp.int32)
    listing = members.reshape(top, rows).T
    listing = listing[jax.random.permutation(jax.random.fold_in(own, 1), rows)]
    turn = jax.random.randint(jax.random.fold_in(own, 2), (rows, 1), 0, top)
    return jnp.take_along_axis(listing, (jnp.arange(top)[None, :] + turn) % top, axis=1)


def portions_of(amount, total, most, skew, full):
    loads = [(1 << 20) // math.isqrt(rank ** skew) + 1 for rank in range(1, amount + 1)]
    largest = most if full else min(most, max(-(-total // amount), total * loads[0] // sum(loads)))
    least = 1 if total - largest >= amount - 1 else 0
    holding, rest = [largest] + [least] * (amount - 1), total - largest - least * (amount - 1)
    while rest > 0:
        free = [i for i in range(1, amount) if holding[i] < largest] or [i for i in range(1, amount) if holding[i] < most]
        pool, remaining = sum([loads[i] for i in free]), rest
        for i in free:
            extra = min(most - holding[i], max(1, remaining * loads[i] // pool), rest)
            holding[i] = holding[i] + extra
            rest = rest - extra
    return np.array(holding)


def gaussian(key, dims, deviation, reach, pieces=(), kind=jnp.bfloat16):
    drawn = deviation * jax.random.normal(key, dims, jnp.float32)
    if pieces:
        drawn = drawn * block_levels(key, dims, pieces, -0.22, 0.18)
    return jnp.clip(drawn, -reach, reach).astype(kind)


def setup_inputs(seed: int = 0) -> dict:
    key_list = jax.random.split(jax.random.key(seed), 19)
    layer_input = gaussian(key_list[0], (TOKENS, D), 1.0, 6.0, ((0, 16), (1, 2)))
    lengths = jax.vmap(lambda own: uneven_parts(own, SEQS, GROUP_TOK, SEQ_MOST, 1))(jax.random.split(key_list[1], GROUPS)).reshape((GROUPS, SEQS)).astype(jnp.int32)
    routes_keys = jax.random.split(jax.random.fold_in(key_list[2], 1), N_COL * (TOKENS // N_COL) // TOK_DEV)
    routes_turns = jax.random.permutation(jax.random.fold_in(key_list[2], 3), N_COL * (TOKENS // N_COL) // TOK_DEV)
    routes = jax.vmap(lambda own, number: routed_block(jax.random.fold_in(key_list[2], 2), own, number, TOK_DEV, EXPERTS, TOPK, CAP, 2))(routes_keys, routes_turns).reshape((N_COL, TOKENS // N_COL, TOPK))
    norm1_gain = jnp.clip(1.0 + 0.1 * jax.random.normal(key_list[3], (D,), jnp.float32), 0.5, 1.5)
    w_query = gaussian(key_list[4], (D, H * (QK_NOPE + ROPE)), D ** -0.5, 0.125, ((0, 2), (1, 4)))
    w_latent = gaussian(key_list[5], (N_COL, D // N_COL, KV_RANK + ROPE), D ** -0.5, 0.125, ((0, 2), (1, 4)))
    latent_gain = jnp.clip(1.0 + 0.1 * jax.random.normal(key_list[6], (KV_RANK,), jnp.float32), 0.5, 1.5)
    w_kv = gaussian(key_list[7], (KV_RANK, H * (QK_NOPE + V_DIM)), KV_RANK ** -0.5, 0.25, ((1, 8),))
    w_out = gaussian(key_list[8], (H * V_DIM, D), (max(2, H * V_DIM // 256)) ** -0.5, 2.0, ((0, 4), (1, 2)))
    norm2_gain = jnp.clip(1.0 + 0.1 * jax.random.normal(key_list[9], (D,), jnp.float32), 0.5, 1.5)
    shared_gate = gaussian(key_list[10], (D, SHARED * FF_E), D ** -0.5, 0.125, ((0, 2), (1, 4)))
    shared_up = gaussian(key_list[11], (D, SHARED * FF_E), D ** -0.5, 0.125, ((0, 2), (1, 4)))
    shared_down = gaussian(key_list[12], (SHARED * FF_E, D), (SHARED * FF_E // 4) ** -0.5, 0.21875, ((0, 4), (1, 2)))
    router = gaussian(key_list[13], (D, EXPERTS), (4 * D) ** -0.5, 0.0625)
    expert_gate = gaussian(key_list[14], (EXPERTS, D, FF_E), D ** -0.5, 0.125, ((0, 16), (2, 2)))
    expert_up = gaussian(key_list[15], (EXPERTS, D, FF_E), D ** -0.5, 0.125, ((0, 16), (2, 2)))
    expert_down = gaussian(key_list[16], (EXPERTS, D, FF_E), (FF_E // 8) ** -0.5, 0.4375, ((0, 16), (2, 2)))
    cotangent = gaussian(key_list[17], (TOKENS, D), 1.0, 6.0, ((0, 16), (1, 2)))
    return dict(layer_input=layer_input, lengths=lengths, routes=routes, norm1_gain=norm1_gain, w_query=w_query, w_latent=w_latent, latent_gain=latent_gain, w_kv=w_kv, w_out=w_out, norm2_gain=norm2_gain, shared_gate=shared_gate, shared_up=shared_up, shared_down=shared_down, router=router, expert_gate=expert_gate, expert_up=expert_up, expert_down=expert_down, cotangent=cotangent)


epsilon = 1e-06
theta_base = 10000.0

@jax.custom_vjp
def low(v):
    return lax.optimization_barrier(v.astype(jnp.bfloat16)).astype(jnp.float32)

@jax.custom_vjp
def low_back(v):
    return v

def low_keep(v):
    return (low(v), None)

def low_pass(kept, grad):
    return (grad,)

def back_keep(v):
    return (v, None)

def back_low(kept, grad):
    return (low(grad),)
low.defvjp(low_keep, low_pass)
low_back.defvjp(back_keep, back_low)

def hdot(left, right):
    return jnp.dot(left, right, precision=lax.Precision.HIGHEST, preferred_element_type=jnp.float32)

def rotate(value, cosine, sine):
    half = value.shape[-1] // 2
    first, second = (value[..., :half], value[..., half:])
    return jnp.concatenate([first * cosine - second * sine, first * sine + second * cosine], axis=-1)

def rms(value, gain):
    return value * lax.rsqrt(lax.optimization_barrier(jnp.mean(value * value, axis=-1, keepdims=True)) + epsilon) * gain

def sequence_layout(lengths_row, group):
    ends = jnp.cumsum(lengths_row).astype(jnp.int32)
    starts = ends - lengths_row
    index = jnp.arange(group, dtype=jnp.int32)
    seq_ids = lax.optimization_barrier(jnp.sum((index[:, None] >= ends[None, :]).astype(jnp.int32), axis=1))
    member = seq_ids[:, None] == jnp.arange(lengths_row.shape[0], dtype=jnp.int32)[None, :]
    begins = lax.optimization_barrier(jnp.sum(jnp.where(member, starts[None, :], 0), axis=1))
    return (seq_ids, index - begins)

def rotary_tables(places):
    half = ROPE // 2
    freqs = jnp.power(theta_base, -jnp.arange(half, dtype=jnp.float32) * (2.0 / ROPE))
    angle = places.astype(jnp.float32)[..., None] * freqs
    return (jnp.cos(angle), jnp.sin(angle))

def attend_group(group_input, seq_ids, cosine, sine, w_query, w_latent, latent_gain, w_kv, w_out):
    group = group_input.shape[0]
    query_pre = low_back(hdot(group_input, w_query)).reshape(group, H, QK_NOPE + ROPE)
    queries = low(jnp.concatenate([query_pre[..., :QK_NOPE], rotate(query_pre[..., QK_NOPE:], cosine[:, None, :], sine[:, None, :])], axis=-1))
    latent = low_back(hdot(group_input, w_latent))
    compressed = low(rms(latent[:, :KV_RANK], latent_gain))
    rotary_key = low(rotate(latent[:, KV_RANK:], cosine, sine))
    key_value = low_back(hdot(compressed, w_kv)).reshape(group, H, QK_NOPE + V_DIM)
    key_plain = low(key_value[..., :QK_NOPE])
    values = low(key_value[..., QK_NOPE:])
    keys = jnp.concatenate([key_plain, jnp.broadcast_to(rotary_key[:, None, :], (group, H, ROPE))], axis=-1)
    scale = 1.0 / math.sqrt(QK_NOPE + ROPE)
    scored = low_back(jnp.einsum('qhd,khd->hqk', queries, keys, precision=lax.Precision.HIGHEST) * scale)
    index = jnp.arange(group, dtype=jnp.int32)
    allowed = (seq_ids[:, None] == seq_ids[None, :]) & (index[None, :] <= index[:, None])
    probs = low(jax.nn.softmax(jnp.where(allowed[None, :, :], scored, -1e+30), axis=-1))
    mixed = jnp.einsum('hqk,khd->qhd', probs, values, precision=lax.Precision.HIGHEST)
    mixed = low(low_back(mixed)).reshape(group, H * V_DIM)
    return hdot(mixed, w_out)

def reference(layer_input, lengths, routes, norm1_gain, w_query, w_latent, latent_gain, w_kv, w_out, norm2_gain, shared_gate, shared_up, shared_down, router, expert_gate, expert_up, expert_down, cotangent):
    col_count = routes.shape[0]
    block_rows = TOK_DEV * col_count
    row_groups = GROUP_TOK // block_rows
    block_count = TOKENS // block_rows
    seq_all, place_all = jax.vmap(lambda row_lengths: sequence_layout(row_lengths, GROUP_TOK))(lengths)
    cos_all, sin_all = rotary_tables(place_all)
    chosen = routes.reshape(col_count, block_count, TOK_DEV, TOPK).transpose(1, 0, 2, 3).reshape(TOKENS, TOPK).astype(jnp.int32)
    pair_count = TOKENS * TOPK
    most_rows = DEVICES * CAP
    flat_ids = chosen.reshape(-1)
    order = jnp.argsort(flat_ids, stable=True).astype(jnp.int32)
    counts = lax.optimization_barrier(jnp.sum((flat_ids[:, None] == jnp.arange(EXPERTS, dtype=jnp.int32)[None, :]).astype(jnp.int32), axis=0))
    offsets = (jnp.cumsum(counts) - counts).astype(jnp.int32)
    order_pad = jnp.concatenate([order, jnp.full((most_rows,), pair_count, dtype=jnp.int32)])
    rows_all = order_pad[offsets[:, None] + jnp.arange(most_rows, dtype=jnp.int32)[None, :]]
    valid_all = jnp.arange(most_rows, dtype=jnp.int32)[None, :] < counts[:, None]

    def to_groups(value):
        return value.reshape(row_groups, GROUPS, block_rows, -1).transpose(1, 0, 2, 3).reshape(GROUPS, GROUP_TOK, -1)

    def from_groups(value):
        return value.reshape(GROUPS, row_groups, block_rows, -1).transpose(1, 0, 2, 3).reshape(TOKENS, -1)

    def forward(layer_in, gain_one, query_w, latent_w, latent_g, kv_w, out_w, gain_two, sh_gate, sh_up, sh_down, router_w, ex_gate, ex_up, ex_down):
        normed = low(rms(layer_in, gain_one))
        latent_full = latent_w.reshape(D, KV_RANK + ROPE)

        def attend(items):
            group_input, seq_ids, cosine, sine = items
            return attend_group(group_input, seq_ids, cosine, sine, query_w, latent_full, latent_g, kv_w, out_w)
        attention = lax.map(jax.checkpoint(attend), (to_groups(normed), seq_all, cos_all, sin_all))
        hidden_state = layer_in + low_back(from_groups(attention))
        second = low(rms(hidden_state, gain_two))
        shared_gate_pre = low_back(hdot(second, sh_gate))
        shared_up_pre = low_back(hdot(second, sh_up))
        shared_hidden = low(jax.nn.silu(shared_gate_pre) * shared_up_pre)
        shared_result = hdot(shared_hidden, sh_down)
        router_probs = jax.nn.softmax(hdot(second, router_w), axis=-1)
        selected = jnp.take_along_axis(router_probs, chosen, axis=1)
        gates = selected / lax.optimization_barrier(jnp.sum(selected, axis=1, keepdims=True))

        def one_expert(items):
            rows_index, valid, gate_w, up_w, down_w = items
            token = jnp.minimum(rows_index // TOPK, TOKENS - 1)
            inputs = low_back(second[token])
            gate_pre = low_back(hdot(inputs, gate_w))
            up_pre = low_back(hdot(inputs, up_w))
            hidden = low(jax.nn.silu(gate_pre) * up_pre)
            result = low(low_back(hdot(hidden, down_w.T)))
            return jnp.where(valid[:, None], result, 0.0)
        results = lax.map(jax.checkpoint(one_expert), (rows_all, valid_all, ex_gate, ex_up, ex_down))
        pair_out = jnp.zeros((pair_count + 1, D), dtype=jnp.float32).at[rows_all.reshape(-1)].add(results.reshape(-1, D))[:pair_count]
        routed = lax.optimization_barrier(jnp.sum(gates[:, :, None] * pair_out.reshape(TOKENS, TOPK, D), axis=1))
        return hidden_state + low_back(shared_result + routed)
    floats = tuple((value.astype(jnp.float32) for value in (layer_input, norm1_gain, w_query, w_latent, latent_gain, w_kv, w_out, norm2_gain, shared_gate, shared_up, shared_down, router, expert_gate, expert_up, expert_down)))
    result, pull = jax.vjp(forward, *floats)
    grads = pull(cotangent.astype(jnp.float32))
    return (result.astype(jnp.bfloat16), grads[0], grads[1], grads[2], grads[3], grads[4], grads[5], grads[6], grads[7], grads[8], grads[9], grads[10], grads[11], grads[12], grads[13], grads[14])
```

```python
import functools
import math

import jax
import jax.numpy as jnp
from jax import lax
from jax.experimental import pallas as pl
from jax.experimental.pallas import tpu as pltpu
from jax.sharding import PartitionSpec as P

QK_NOPE = 128
ROPE = 64
KV_RANK = 512
V_DIM = 128

epsilon = 1e-06
theta_base = 10000.0
SWAP = [(0, 1), (1, 0)]


MESH = pl.DeviceIdType.MESH


class Place:
    def __init__(self, layers):
        self.layers = layers
        self.row, self.col = lax.axis_index("row"), lax.axis_index("col")
        self.layer = lax.axis_index("exp") if layers > 1 else 0
        self.core = lax.rem(self.row, 2)
        self.x_row = lax.rem(self.row + 2, 4)
        self.core_row = self.row + 1 - 2 * self.core
        self.y_col = 1 - self.col
        self.to_x = {"row": self.x_row}
        self.to_y = {"col": self.y_col}
        self.to_core = {"row": self.core_row}
        self.above = {"exp": self.layer + 1}
        self.below = {"exp": self.layer - 1}

    def greet(self):
        barrier = pltpu.get_barrier_semaphore()
        for target in (self.to_x, self.to_y, self.to_core):
            pl.semaphore_signal(barrier, inc=1, device_id=target, device_id_type=MESH)
        if self.layers > 1:

            @pl.when(self.layer > 0)
            def _():
                pl.semaphore_signal(barrier, inc=1, device_id=self.below, device_id_type=MESH)

            @pl.when(self.layer < self.layers - 1)
            def _():
                pl.semaphore_signal(barrier, inc=1, device_id=self.above, device_id_type=MESH)

        peers = 3
        if self.layers > 1:
            peers = peers + jnp.where(self.layer > 0, 1, 0) + jnp.where(self.layer < self.layers - 1, 1, 0)
        pl.semaphore_wait(barrier, peers)


def remote(src, dst, send, recv, target):
    return pltpu.make_async_remote_copy(
        src_ref=src, dst_ref=dst, send_sem=send, recv_sem=recv, device_id=target, device_id_type=MESH
    )


def first_part(rows):
    return (rows // 2 + 15) // 16 * 16


def gather_body(
    layers, src, out, held, store_sem, up_send, down_send, z_recv, send, recv, diag_send, diag_recv
):
    me = Place(layers)
    rows, width = src.shape
    part = first_part(rows)
    spans = ((0, part), (part, rows - part))

    owners = (
        (me.row, me.col),
        (me.x_row, me.col),
        (me.row, me.y_col),
        (me.x_row, me.y_col),
    )
    sides = (me.to_x, me.to_y)

    def area(where, row, col, layer, span=(0, rows)):
        first = pl.multiple_of((row * layers + layer) * rows + span[0], 16)
        return where.at[pl.ds(first, span[1]), pl.ds(pl.multiple_of(col * width, 128), width)]

    def held_piece(kind, layer, span=(0, rows)):
        return area(held, *owners[kind], layer, span)

    def partner_piece(where, kind, layer):
        row, col = owners[kind]
        return area(where, row + 1 - 2 * me.core, col, layer)

    def store(kind, layer, partner):
        if partner:
            pair = (partner_piece(held, kind, layer), partner_piece(out, kind, layer))
        else:
            pair = (held_piece(kind, layer), area(out, *owners[kind], layer))
        return pltpu.make_async_copy(*pair, store_sem.at[1 if partner else 0, kind, layer])

    def to_core(kind, layer):
        piece = held_piece(kind, layer)
        return remote(piece, piece, send.at[4, kind, layer], recv.at[4, kind, layer], me.to_core)

    def from_core(kind, layer):
        piece = partner_piece(held, kind, layer)
        return remote(piece, piece, send.at[4, kind, layer], recv.at[4, kind, layer], me.to_core)

    def beside(axis, half, layer, incoming=False):
        piece = held_piece(axis + 1 if incoming else 0, layer, spans[half])
        sems = (2 * axis + half, 0, layer)
        return remote(piece, piece, send.at[sems], recv.at[sems], sides[axis])

    def corner(axis, layer, incoming=False):
        piece = held_piece(3 if incoming else axis + 1, layer, spans[axis])
        return remote(
            piece, piece, diag_send.at[axis, layer], diag_recv.at[axis, layer], sides[1 - axis]
        )

    def along(up, layer):
        piece = held_piece(0, layer)
        return remote(
            piece,
            piece,
            (up_send if up else down_send).at[layer],
            z_recv.at[layer],
            me.above if up else me.below,
        )

    def spread(layer):
        beside(0, 0, layer).start()
        beside(1, 1, layer).start()
        beside(0, 1, layer).start()
        beside(1, 0, layer).start()
        to_core(0, layer).start()

    def at_distance(distance, act):
        if distance == 0:
            act(me.layer, None)
            return

        @pl.when(me.layer >= distance)
        def _():
            act(me.layer - distance, True)

        @pl.when(me.layer + distance < layers)
        def _():
            act(me.layer + distance, False)

    own = pltpu.make_async_copy(src, held_piece(0, me.layer), store_sem.at[0, 0, me.layer])
    own.start()
    me.greet()
    own.wait()
    if layers > 1:

        @pl.when(me.layer < layers - 1)
        def _():
            along(True, me.layer).start()

        @pl.when(me.layer > 0)
        def _():
            along(False, me.layer).start()

    spread(me.layer)
    store(0, me.layer, False).start()

    def arrived(layer, upward):
        along(upward, layer).wait_recv()
        if upward:

            @pl.when(me.layer < layers - 1)
            def _():
                along(True, layer).start()
        else:

            @pl.when(me.layer > 0)
            def _():
                along(False, layer).start()

        spread(layer)
        store(0, layer, False).start()

    def second(layer, upward):
        for axis in (0, 1):
            beside(axis, axis, layer, True).wait_recv()
            corner(axis, layer).start()
        for axis in (0, 1):
            beside(axis, 1 - axis, layer, True).wait_recv()
            to_core(axis + 1, layer).start()
            store(axis + 1, layer, False).start()

    def third(layer, upward):
        for axis in (0, 1):
            corner(axis, layer, True).wait_recv()
        to_core(3, layer).start()
        store(3, layer, False).start()
        for kind in range(4):
            from_core(kind, layer).wait_recv()
            store(kind, layer, True).start()

    for step in range(1, layers + 2):
        if step < layers:
            at_distance(step, arrived)
        if step - 1 < layers:
            at_distance(step - 1, second)
        if 0 <= step - 2 < layers:
            at_distance(step - 2, third)
    for layer in range(layers):
        for kind in range(4):
            to_core(kind, layer).wait_send()
            store(kind, layer, False).wait()
            store(kind, layer, True).wait()
        for axis in (0, 1):
            for half in (0, 1):
                beside(axis, half, layer).wait_send()
            corner(axis, layer).wait_send()
    if layers > 1:
        for layer in range(layers):

            @pl.when((me.layer < layers - 1) & (layer <= me.layer))
            def _():
                along(True, layer).wait_send()

            @pl.when((me.layer > 0) & (layer >= me.layer))
            def _():
                along(False, layer).wait_send()


def gather(value, layers, collective_id):
    rows, width = value.shape
    dma = pltpu.SemaphoreType.DMA
    whole = (4 * layers * rows, 2 * width)
    return pl.pallas_call(
        functools.partial(gather_body, layers),
        out_shape=jax.ShapeDtypeStruct(whole, value.dtype),
        in_specs=[pl.BlockSpec(memory_space=pl.ANY)],
        out_specs=pl.BlockSpec(memory_space=pl.ANY),
        scratch_shapes=[
            pltpu.VMEM(whole, value.dtype),
            dma((2, 4, layers)),
            dma((layers,)),
            dma((layers,)),
            dma((layers,)),
            dma((5, 4, layers)),
            dma((5, 4, layers)),
            dma((2, layers)),
            dma((2, layers)),
        ],
        compiler_params=pltpu.CompilerParams(
            collective_id=collective_id,
            has_side_effects=True,
            vmem_limit_bytes=56 * 1024 * 1024,
        ),
    )(value)


def scatter_body(
    layers,
    src,
    out,
    acc,
    core_in,
    diag_a,
    diag_b,
    side_in,
    line_in,
    load_sem,
    core_send,
    core_recv,
    diag_send,
    diag_recv,
    side_send,
    side_recv,
    line_send,
    line_recv,
):
    me = Place(layers)
    rows, width = out.shape
    part = first_part(rows)
    owners = (
        (me.row, me.col),
        (me.x_row, me.col),
        (me.row, me.y_col),
        (me.x_row, me.y_col),
    )

    def layer_at(step):
        if layers == 1:
            return 0
        found = 0
        for layer in range(layers):
            order = sorted(range(layers), key=lambda other: (-abs(other - layer), -other))
            found = found + jnp.where(me.layer == layer, order[step], 0)
        return found

    layer_of = [layer_at(step) for step in range(layers)]

    def area(row, col, layer):
        first = pl.multiple_of((row * layers + layer) * rows, 16)
        return src.at[pl.ds(first, rows), pl.ds(pl.multiple_of(col * width, 128), width)]

    def load(step, kind):
        return pltpu.make_async_copy(
            area(*owners[kind], layer_of[step]), acc.at[step, kind], load_sem.at[step, kind]
        )

    def to_core(step, kind):
        row, col = owners[kind]
        return remote(
            area(row + 1 - 2 * me.core, col, layer_of[step]),
            core_in.at[step, kind],
            core_send.at[step, kind],
            core_recv.at[step, kind],
            me.to_core,
        )

    def diag(step, axis):
        start, size = ((0, part), (part, rows - part))[axis]
        return remote(
            acc.at[step, 3, pl.ds(start, size)],
            (diag_a, diag_b)[axis].at[step],
            diag_send.at[axis, step],
            diag_recv.at[axis, step],
            (me.to_y, me.to_x)[axis],
        )

    def side(step, axis):
        return remote(
            acc.at[step, axis + 1],
            side_in.at[axis, step],
            side_send.at[axis, step],
            side_recv.at[axis, step],
            (me.to_x, me.to_y)[axis],
        )

    def line(step, up):
        layer = layer_of[step]
        way = 0 if up else 1
        return remote(
            acc.at[step, 0],
            line_in.at[way, layer],
            line_send.at[step],
            line_recv.at[way, layer],
            me.above if up else me.below,
        )

    lanes = 32 if rows % 32 == 0 else 16

    def add(target, others, start=0, size=rows, into=None):
        def step(i, carry):
            first = pl.multiple_of(i * lanes, 16)
            total = target[pl.ds(start + first, lanes), :].astype(jnp.float32)
            for other in others:
                total = total + other[pl.ds(first, lanes), :].astype(jnp.float32)
            if into is None:
                target[pl.ds(start + first, lanes), :] = total.astype(target.dtype)
            else:
                into[pl.ds(first, lanes), :] = total.astype(into.dtype)
            return carry

        lax.fori_loop(0, size // lanes, step, 0)

    me.greet()
    kinds = (3, 1, 2, 0)
    for step in range(layers):
        for kind in kinds:
            to_core(step, kind).start()
            load(step, kind).start()

    def ready(step, kind):
        load(step, kind).wait()
        to_core(step, kind).wait_recv()

    def stage_a(step):
        ready(step, 3)
        add(acc.at[step, 3], [core_in.at[step, 3]])
        diag(step, 0).start()
        diag(step, 1).start()

    def stage_b(step):
        for axis, buffer, start, size in (
            (0, diag_a, 0, part),
            (1, diag_b, part, rows - part),
        ):
            kind = axis + 1
            ready(step, kind)
            add(acc.at[step, kind], [core_in.at[step, kind]])
            diag(step, axis).wait_recv()
            add(acc.at[step, kind], [buffer.at[step]], start, size)
            side(step, axis).start()

    def stage_c(step):
        ready(step, 0)
        side(step, 0).wait_recv()
        side(step, 1).wait_recv()
        parts = [core_in.at[step, 0], side_in.at[0, step], side_in.at[1, step]]
        if layers == 1:
            add(acc.at[step, 0], parts, into=out)
            return
        add(acc.at[step, 0], parts)
        layer = layer_of[step]
        if step < layers - 1:

            @pl.when((layer > me.layer) & (me.layer > 0))
            def _():
                line(step, True).wait_recv()
                add(acc.at[step, 0], [line_in.at[0, layer]])

            @pl.when((layer < me.layer) & (me.layer < layers - 1))
            def _():
                line(step, False).wait_recv()
                add(acc.at[step, 0], [line_in.at[1, layer]])

            @pl.when(layer > me.layer)
            def _():
                line(step, True).start()

            @pl.when(layer < me.layer)
            def _():
                line(step, False).start()
        else:
            inner = (me.layer > 0) & (me.layer < layers - 1)

            @pl.when(me.layer > 0)
            def _():
                line(step, True).wait_recv()

            @pl.when(me.layer < layers - 1)
            def _():
                line(step, False).wait_recv()

            @pl.when(inner)
            def _():
                add(acc.at[step, 0], [line_in.at[0, layer], line_in.at[1, layer]], into=out)

            @pl.when(me.layer == 0)
            def _():
                add(acc.at[step, 0], [line_in.at[1, layer]], into=out)

            @pl.when(me.layer == layers - 1)
            def _():
                add(acc.at[step, 0], [line_in.at[0, layer]], into=out)

    for step in range(layers + 2):
        if step < layers:
            stage_a(step)
        if 0 <= step - 1 < layers:
            stage_b(step - 1)
        if 0 <= step - 2 < layers:
            stage_c(step - 2)
    for step in range(layers):
        for kind in kinds:
            to_core(step, kind).wait_send()
        for axis in (0, 1):
            diag(step, axis).wait_send()
            side(step, axis).wait_send()
        if step < layers - 1:

            @pl.when(layer_of[step] > me.layer)
            def _():
                line(step, True).wait_send()

            @pl.when(layer_of[step] < me.layer)
            def _():
                line(step, False).wait_send()


def scatter(value, layers, collective_id):
    rows, width = value.shape[0] // (4 * layers), value.shape[1] // 2
    part = first_part(rows)
    dma = pltpu.SemaphoreType.DMA
    buffer = lambda *lead: pltpu.VMEM((*lead, rows, width), value.dtype)
    return pl.pallas_call(
        functools.partial(scatter_body, layers),
        out_shape=jax.ShapeDtypeStruct((rows, width), jnp.float32),
        in_specs=[pl.BlockSpec(memory_space=pl.ANY)],
        out_specs=pl.BlockSpec(memory_space=pltpu.VMEM),
        scratch_shapes=[
            buffer(layers, 4),
            buffer(layers, 4),
            pltpu.VMEM((layers, part, width), value.dtype),
            pltpu.VMEM((layers, rows - part, width), value.dtype),
            buffer(2, layers),
            buffer(2, layers),
            dma((layers, 4)),
            dma((layers, 4)),
            dma((layers, 4)),
            dma((2, layers)),
            dma((2, layers)),
            dma((2, layers)),
            dma((2, layers)),
            dma((layers,)),
            dma((2, layers)),
        ],
        compiler_params=pltpu.CompilerParams(
            collective_id=collective_id,
            has_side_effects=True,
            vmem_limit_bytes=56 * 1024 * 1024,
        ),
    )(value)


def dot_nn(left, right):
    return jnp.dot(left, right, preferred_element_type=jnp.float32)


def dot_nt(left, right):
    return lax.dot_general(
        left, right, (((1,), (1,)), ((), ())), preferred_element_type=jnp.float32
    )


def dot_tn(left, right):
    return lax.dot_general(
        left, right, (((0,), (0,)), ((), ())), preferred_element_type=jnp.float32
    )


def rotate(value, cosine, sine):
    half = value.shape[-1] // 2
    first, second = (value[..., :half], value[..., half:])
    return jnp.concatenate(
        [first * cosine - second * sine, first * sine + second * cosine], axis=-1
    )


def unrotate(value, cosine, sine):
    half = value.shape[-1] // 2
    first, second = (value[..., :half], value[..., half:])
    return jnp.concatenate(
        [first * cosine + second * sine, second * cosine - first * sine], axis=-1
    )


def sequence_layout(lengths_row, group):
    ends = jnp.cumsum(lengths_row)
    starts = ends - lengths_row
    index = jnp.arange(group, dtype=jnp.int32)
    seq_ids = jnp.sum((index[:, None] >= ends[None, :]).astype(jnp.int32), axis=1)
    member = seq_ids[:, None] == jnp.arange(lengths_row.shape[0], dtype=jnp.int32)[None, :]
    begins = jnp.sum(jnp.where(member, starts[None, :], 0), axis=1)
    return (seq_ids, index - begins)


def rotary_tables(places):
    half = ROPE // 2
    freqs = jnp.power(theta_base, -jnp.arange(half, dtype=jnp.float32) * (2.0 / ROPE))
    angle = places.astype(jnp.float32)[..., None] * freqs
    return (jnp.cos(angle), jnp.sin(angle))


def norm_back(value, factor, gain, grad, width):
    weighted = grad * gain
    inner = lax.psum(jnp.sum(weighted * value, axis=1), "col")
    d_value = (
        factor[:, None] * weighted - value * (factor * factor * factor * inner / width)[:, None]
    )
    d_gain = jnp.sum(grad * value * factor[:, None], axis=0)
    return (d_value, d_gain)


def masked_scores(query_block, keys, seq_ids, first, scale):
    size = query_block.shape[0]
    group = keys.shape[0]
    scored = (
        jnp.einsum("qhd,khd->hqk", query_block, keys, preferred_element_type=jnp.float32) * scale
    )
    query_index = first + jnp.arange(size, dtype=jnp.int32)
    key_index = jnp.arange(group, dtype=jnp.int32)
    allowed = (seq_ids[first : first + size][:, None] == seq_ids[None, :group]) & (
        key_index[None, :] <= query_index[:, None]
    )
    return jnp.where(allowed[None, :, :], scored, -1e30)


def own_slice(value, index, axis):
    size = value.shape[axis] // 2
    return lax.dynamic_slice_in_dim(value, index * size, size, axis)


def col_pair(mine, sent, axis):
    received = lax.ppermute(sent, "col", SWAP)
    first = lax.axis_index("col") == 0
    return jnp.where(
        first,
        jnp.concatenate([mine, received], axis=axis),
        jnp.concatenate([received, mine], axis=axis),
    )


def trade(value, split, join):
    col = lax.axis_index("col")
    return col_pair(own_slice(value, col, split), own_slice(value, 1 - col, split), join)


def routed_and_shared(
    tok_dev, capacity, layers, router, expert_weights, shared_own, normed_own, grads_own, chosen
):
    bf16 = jnp.bfloat16
    col_id = lax.axis_index("col")
    own_expert = lax.axis_index("row") * layers + lax.axis_index("exp")
    experts = router.shape[1]
    block, half_width = normed_own.shape
    width = 2 * half_width
    tokens = chosen.shape[0]
    few = min(tok_dev, block)
    slots = -(-min(capacity, few) // 16) * 16
    blocks = tokens // few
    gather_layers = layers
    grads_all = gather(grads_own, gather_layers, 3)
    normed_all = gather(normed_own, gather_layers, 3)

    router_probs = jax.nn.softmax(dot_nn(normed_all, router), axis=1)
    picks = jnp.any(
        chosen[:, :, None] == jnp.arange(experts, dtype=jnp.int32)[None, None, :], axis=1
    )
    selected = jnp.where(picks, router_probs, 0.0)
    selected_total = jnp.sum(selected, axis=1, keepdims=True)
    gates = selected / selected_total
    is_own = jnp.arange(experts, dtype=jnp.int32)[None, :] == own_expert
    own_gate = jnp.sum(jnp.where(is_own, gates, 0.0), axis=1).reshape(blocks, few)
    own_pick = jnp.any(picks & is_own, axis=1).reshape(blocks, few)
    place = jnp.cumsum(own_pick.astype(jnp.int32), axis=1) - 1
    onehot = (place[:, None, :] == jnp.arange(slots, dtype=jnp.int32)[None, :, None]) & own_pick[
        :, None, :
    ]
    slot_gate = jnp.sum(jnp.where(onehot, own_gate[:, None, :], 0.0), axis=2).reshape(-1, 1)
    pick_rows = onehot.astype(bf16)

    def to_slots(value):
        return (
            jnp.einsum(
                "bsi,bid->bsd",
                pick_rows,
                value.reshape(blocks, few, width),
                preferred_element_type=jnp.float32,
            )
            .astype(bf16)
            .reshape(blocks * slots, width)
        )

    def from_slots(value):
        return jnp.einsum(
            "bsi,bsd->bid",
            pick_rows,
            value.reshape(blocks, slots, width),
            preferred_element_type=jnp.float32,
        ).reshape(tokens, width)

    slot_rows = to_slots(normed_all)
    slot_grads = to_slots(grads_all)
    gate_weight, up_weight, down_weight = expert_weights

    def feed_forward(rows, grads, gate_of, gate_w, up_w, down_w):
        gate_pre = dot_nn(rows, gate_w)
        up_pre = dot_nn(rows, up_w)
        sigmoid = jax.nn.sigmoid(gate_pre)
        silu = gate_pre * sigmoid
        hidden = (silu * up_pre).astype(bf16).astype(jnp.float32)
        d_raw = dot_nn(grads, down_w)
        d_gate_of = jnp.sum(d_raw * hidden, axis=1)
        d_hidden = d_raw if gate_of is None else d_raw * gate_of
        hidden = hidden if gate_of is None else hidden * gate_of
        d_up = (d_hidden * silu).astype(bf16)
        d_gate = (d_hidden * up_pre * sigmoid * (1.0 + gate_pre * (1.0 - sigmoid))).astype(bf16)
        return (hidden.astype(bf16), d_gate, d_up, d_gate_of)

    hidden, d_gate, d_up, d_gates_slots = feed_forward(
        slot_rows, slot_grads, slot_gate, gate_weight, up_weight, down_weight
    )
    shared_hidden, d_shared_gate, d_shared_up, _ = feed_forward(
        normed_all, grads_all, None, shared_own[0].T, shared_own[1].T, shared_own[2].T
    )
    d_pair = (dot_nt(d_gate, gate_weight) + dot_nt(d_up, up_weight)).astype(bf16)
    d_normed = scatter(
        (
            from_slots(d_pair)
            + dot_nn(d_shared_gate, shared_own[0])
            + dot_nn(d_shared_up, shared_own[1])
        ).astype(bf16),
        layers,
        4,
    )
    result = dot_nt(hidden, down_weight).astype(bf16)
    branch = scatter(
        (from_slots(result) + dot_nn(shared_hidden, shared_own[2])).astype(bf16), layers, 4
    )
    grad_gate = dot_tn(slot_rows, d_gate)
    grad_up = dot_tn(slot_rows, d_up)
    grad_down = dot_tn(slot_grads, hidden)
    grad_shared = jnp.stack(
        [
            dot_tn(d_shared_gate, normed_all),
            dot_tn(d_shared_up, normed_all),
            dot_tn(shared_hidden, grads_all),
        ]
    )

    d_gates_dense = jnp.sum(
        jnp.where(onehot, d_gates_slots.reshape(blocks, slots, 1), 0.0), axis=1
    ).reshape(experts, block)
    d_gates = lax.psum(
        lax.all_to_all(d_gates_dense, ("row", "exp"), split_axis=0, concat_axis=0, tiled=True), "col"
    ).T

    def own_rows(value):
        return lax.dynamic_slice_in_dim(value, own_expert * block, block, 0)

    own_probs, own_gates, own_total = own_rows(router_probs), own_rows(gates), own_rows(selected_total)
    d_selected = (d_gates - jnp.sum(d_gates * own_gates, axis=1, keepdims=True)) / own_total
    d_router_probs = jnp.where(own_rows(picks), d_selected, 0.0)
    d_logits = own_probs * (
        d_router_probs - jnp.sum(own_probs * d_router_probs, axis=1, keepdims=True)
    )
    router_half = lax.dynamic_slice_in_dim(router, col_id * half_width, half_width, 0)
    grad_router = lax.dot_general(
        normed_own.astype(jnp.float32),
        d_logits,
        (((0,), (0,)), ((), ())),
        precision=lax.Precision.HIGHEST,
        preferred_element_type=jnp.float32,
    )
    d_normed = d_normed + lax.dot_general(
        d_logits,
        router_half.astype(jnp.float32),
        (((1,), (1,)), ((), ())),
        precision=lax.Precision.HIGHEST,
        preferred_element_type=jnp.float32,
    )
    return (d_normed, branch, (grad_gate, grad_up, grad_down, grad_shared, grad_router))


def per_device(
    layer_input,
    lengths,
    routes,
    norm1_gain,
    w_query,
    w_latent,
    latent_gain,
    w_kv,
    w_out,
    norm2_gain,
    shared_gate,
    shared_up,
    shared_down,
    router,
    expert_gate,
    expert_up,
    expert_down,
    cotangent,
):
    row_id = lax.axis_index("row")
    col_id = lax.axis_index("col")
    exp_id = lax.axis_index("exp")
    rows_n, cols_n, exps_n = (lax.axis_size(name) for name in ("row", "col", "exp"))
    experts = rows_n * exps_n
    own_expert = row_id * exps_n + exp_id
    tok_dev = routes.shape[1]
    topk_count = routes.shape[2]
    capacity = max(2, 3 * tok_dev * topk_count // (2 * experts))
    slots = -(-capacity // 16) * 16
    block, half_width = layer_input.shape
    width = half_width * cols_n
    group = block * rows_n
    tokens = group * exps_n
    heads_here = w_kv.shape[1] // (QK_NOPE + V_DIM)
    head_dim = QK_NOPE + ROPE
    scale = 1.0 / math.sqrt(head_dim)
    query_rows = group // 2
    bf16 = jnp.bfloat16

    w_query_own = trade(w_query, 1, 0)
    w_latent_all = lax.all_gather(w_latent[0].T, ("col", "row"), axis=1, tiled=True)
    w_out_own = trade(w_out, 0, 1)
    units = shared_gate.shape[1] // (cols_n * exps_n)
    shared_parts = jnp.stack(
        [
            lax.dynamic_index_in_dim(
                part.reshape(cols_n, exps_n, units, half_width), exp_id, 1, keepdims=False
            )
            for part in (shared_gate.T, shared_up.T, shared_down)
        ]
    )
    shared_own = trade(shared_parts, 1, 3)[:, 0]

    chosen_all = lax.all_gather(routes[0], ("row", "exp", "col"), axis=0, tiled=True)

    seq_ids, places = sequence_layout(lengths[0], group)
    cosine, sine = rotary_tables(places)

    group_input = gather(layer_input, 1, 1).astype(jnp.float32)
    factor_group = lax.rsqrt(jnp.mean(group_input * group_input, axis=1) + epsilon)
    normed_group = (group_input * factor_group[:, None] * norm1_gain).astype(bf16)
    query_pre = dot_nn(normed_group, w_query_own).reshape(group, heads_here, head_dim)
    queries = jnp.concatenate(
        [
            query_pre[..., :QK_NOPE],
            rotate(query_pre[..., QK_NOPE:], cosine[:, None, :], sine[:, None, :]),
        ],
        axis=2,
    ).astype(bf16)
    latent = dot_nt(normed_group, w_latent_all)
    compressed_raw = latent[:, :KV_RANK]
    kv_factor = lax.rsqrt(jnp.mean(compressed_raw * compressed_raw, axis=1) + epsilon)
    compressed = (compressed_raw * kv_factor[:, None] * latent_gain).astype(bf16)
    rotary_key = rotate(latent[:, KV_RANK:], cosine, sine).astype(bf16)
    key_value = (
        dot_nn(compressed, w_kv).astype(bf16).reshape(group, heads_here, QK_NOPE + V_DIM)
    )
    keys = jnp.concatenate(
        [
            key_value[..., :QK_NOPE],
            jnp.broadcast_to(rotary_key[:, None, :], (group, heads_here, ROPE)),
        ],
        axis=2,
    )
    values = key_value[..., QK_NOPE:]
    block_outputs = []
    block_totals = []
    for first in range(0, group, query_rows):
        last = first + query_rows
        scores = masked_scores(queries[first:last], keys[:last], seq_ids, first, scale)
        highest = jnp.max(scores, axis=2, keepdims=True)
        log_total = highest + jnp.log(jnp.sum(jnp.exp(scores - highest), axis=2, keepdims=True))
        probs_low = jnp.exp(scores - log_total).astype(bf16)
        block_outputs.append(
            jnp.einsum(
                "hqk,khd->qhd", probs_low, values[:last], preferred_element_type=jnp.float32
            ).astype(bf16)
        )
        block_totals.append(log_total)
    attended = jnp.concatenate(block_outputs, axis=0).reshape(group, heads_here * V_DIM)

    input_wide = layer_input.astype(jnp.float32)
    hidden_state = input_wide + scatter(dot_nn(attended, w_out_own).astype(bf16), 1, 2)
    gain_two = lax.dynamic_slice_in_dim(norm2_gain, col_id * half_width, half_width)
    square = lax.psum(jnp.sum(hidden_state * hidden_state, axis=1), "col")
    factor_two = lax.rsqrt(square / width + epsilon)
    normed_two = (hidden_state * factor_two[:, None] * gain_two).astype(bf16)
    pieces = max(1, exps_n // 4)
    feed = functools.partial(
        routed_and_shared,
        tok_dev,
        capacity,
        exps_n,
        router,
        (expert_gate[0], expert_up[0], expert_down[0]),
        shared_own,
    )
    if pieces == 1:
        d_normed, branch, weight_grads = feed(normed_two, cotangent, chosen_all)
    else:
        piece_rows = block // pieces

        def one_piece(total, items):
            d_rows, branch_rows, grads = feed(*items)
            return (jax.tree.map(jnp.add, total, grads), (d_rows, branch_rows))

        split = lambda value: value.reshape(pieces, piece_rows, half_width)
        chosen_pieces = chosen_all.reshape(experts, pieces, piece_rows, topk_count)
        items = (
            split(normed_two),
            split(cotangent),
            chosen_pieces.transpose(1, 0, 2, 3).reshape(pieces, -1, topk_count),
        )
        shapes = jax.eval_shape(lambda: feed(*(item[0] for item in items))[2])
        start = jax.tree.map(lambda leaf: jnp.zeros(leaf.shape, leaf.dtype), shapes)
        weight_grads, (d_normed, branch) = lax.scan(one_piece, start, items)
        d_normed, branch = (v.reshape(block, half_width) for v in (d_normed, branch))
    grad_gate, grad_up, grad_down, grad_shared, grad_router = weight_grads
    output = (hidden_state + branch).astype(bf16)
    grad_shared = trade(grad_shared.astype(bf16)[:, None], 3, 1)
    grad_shared = lax.all_gather(grad_shared, "exp", axis=2, tiled=False)
    grad_shared = grad_shared.reshape(3, cols_n * exps_n * units, half_width).astype(jnp.float32)
    d_norm_two, grad_gain_two = norm_back(hidden_state, factor_two, gain_two, d_normed, width)
    d_hidden_state = cotangent.astype(jnp.float32) + d_norm_two

    d_branch = gather(d_hidden_state.astype(bf16), 1, 1)
    grad_w_out = dot_tn(attended, d_branch)
    d_attended = dot_nt(d_branch, w_out_own).astype(bf16).reshape(group, heads_here, V_DIM)
    d_query_blocks = []
    d_keys = jnp.zeros((group, heads_here, head_dim), jnp.float32)
    d_values = jnp.zeros((group, heads_here, V_DIM), jnp.float32)
    for number, first in enumerate(range(0, group, query_rows)):
        last = first + query_rows
        query_block = queries[first:last]
        d_block = d_attended[first:last]
        scores = masked_scores(query_block, keys[:last], seq_ids, first, scale)
        probs = jnp.exp(scores - block_totals[number])
        d_probs = jnp.einsum(
            "qhd,khd->hqk", d_block, values[:last], preferred_element_type=jnp.float32
        )
        delta = jnp.sum(probs * d_probs, axis=2, keepdims=True)
        d_scores = (probs * (d_probs - delta)).astype(bf16)
        d_query_blocks.append(
            jnp.einsum("hqk,khd->qhd", d_scores, keys[:last], preferred_element_type=jnp.float32)
            * scale
        )
        d_keys = d_keys.at[:last].add(
            jnp.einsum("hqk,qhd->khd", d_scores, query_block, preferred_element_type=jnp.float32)
            * scale
        )
        d_values = d_values.at[:last].add(
            jnp.einsum(
                "hqk,qhd->khd", probs.astype(bf16), d_block, preferred_element_type=jnp.float32
            )
        )
    d_query = jnp.concatenate(d_query_blocks, axis=0)
    d_query_pre = (
        jnp.concatenate(
            [
                d_query[..., :QK_NOPE],
                unrotate(d_query[..., QK_NOPE:], cosine[:, None, :], sine[:, None, :]),
            ],
            axis=2,
        )
        .astype(bf16)
        .reshape(group, heads_here * head_dim)
    )
    d_key_value = (
        jnp.concatenate([d_keys[..., :QK_NOPE], d_values], axis=2)
        .astype(bf16)
        .reshape(group, heads_here * (QK_NOPE + V_DIM))
    )
    grad_w_kv = dot_tn(compressed, d_key_value)
    d_latent_sum = lax.psum(
        jnp.concatenate(
            [dot_nt(d_key_value, w_kv), jnp.sum(d_keys[..., QK_NOPE:], axis=1)], axis=1
        ).astype(bf16),
        ("row", "col"),
    ).astype(jnp.float32)
    d_compressed = d_latent_sum[:, :KV_RANK]
    weighted = d_compressed * latent_gain
    grad_latent_gain = jnp.sum(d_compressed * compressed_raw * kv_factor[:, None], axis=0)
    inner = jnp.sum(weighted * compressed_raw, axis=1)
    d_raw = (
        kv_factor[:, None] * weighted
        - compressed_raw * (kv_factor * kv_factor * kv_factor * inner / KV_RANK)[:, None]
    )
    d_latent = jnp.concatenate(
        [d_raw, unrotate(d_latent_sum[:, KV_RANK:], cosine, sine)], axis=1
    ).astype(bf16)
    slab = w_latent.shape[1]
    slab_start = col_id * half_width + row_id * slab
    normed_slab = lax.dynamic_slice_in_dim(normed_group, slab_start, slab, 1)
    grad_w_latent = dot_tn(d_latent, normed_slab)
    grad_w_query = dot_tn(normed_group, d_query_pre)
    d_gathered = dot_nt(d_query_pre, w_query_own)
    piece = lax.dynamic_slice_in_dim(d_gathered, slab_start, slab, 1) + dot_nt(
        d_latent, w_latent[0]
    )
    d_gathered = lax.dynamic_update_slice_in_dim(d_gathered, piece, slab_start, 1)
    d_first = scatter(d_gathered.astype(bf16), 1, 2)
    gain_one = lax.dynamic_slice_in_dim(norm1_gain, col_id * half_width, half_width)
    factor_one = lax.dynamic_slice_in_dim(factor_group, row_id * block, block)
    d_norm_one, grad_gain_one = norm_back(input_wide, factor_one, gain_one, d_first, width)
    input_grad = d_hidden_state + d_norm_one

    latent_share = grad_latent_gain / (rows_n * cols_n)
    small = jnp.concatenate(
        [grad_gain_one[None], grad_gain_two[None], grad_router.T], axis=0
    )
    small = lax.psum(small, ("row", "exp"))
    small = lax.all_gather(small, "col", axis=1, tiled=True)
    summed_latent_gain = lax.psum(latent_share, ("row", "col", "exp"))

    summed = lax.psum(
        tuple(g.astype(bf16) for g in (grad_w_query, grad_w_latent, grad_w_kv, grad_w_out)), "exp"
    )
    out_w_query = trade(summed[0], 0, 1).astype(jnp.float32)
    out_w_out = trade(summed[3], 1, 0).astype(jnp.float32)
    return (
        output,
        input_grad,
        small[0],
        out_w_query,
        summed[1].T.astype(jnp.float32)[None],
        summed_latent_gain,
        summed[2].astype(jnp.float32),
        out_w_out,
        small[1],
        grad_shared[0].T,
        grad_shared[1].T,
        grad_shared[2],
        small[2:].T,
        grad_gate[None],
        grad_up[None],
        grad_down[None],
    )


def solution(mesh):
    placed = (
        P(("row", "exp"), "col"),
        P("exp", None),
        P("col", ("row", "exp"), None),
        P(),
        P("col", "row"),
        P("col", "row", None),
        P(),
        P(None, ("row", "col")),
        P("row", "col"),
        P(),
        P("col", "row"),
        P("col", "row"),
        P("row", "col"),
        P(),
        P(("row", "exp"), None, "col"),
        P(("row", "exp"), None, "col"),
        P(("row", "exp"), None, "col"),
        P(("row", "exp"), "col"),
    )
    return jax.shard_map(
        per_device,
        mesh=mesh,
        in_specs=placed,
        out_specs=(
            P(("row", "exp"), "col"),
            P(("row", "exp"), "col"),
            P(),
            P("col", "row"),
            P("col", "row", None),
            P(),
            P(None, ("row", "col")),
            P("row", "col"),
            P(),
            P("col", "row"),
            P("col", "row"),
            P("row", "col"),
            P(),
            P(("row", "exp"), None, "col"),
            P(("row", "exp"), None, "col"),
            P(("row", "exp"), None, "col"),
        ),
        check_vma=False,
    )
```

```python
import functools
import math

import jax
import jax.numpy as jnp
from jax import lax
from jax.experimental import pallas as pl
from jax.experimental.pallas import tpu as pltpu
from jax.sharding import PartitionSpec as P

QK_NOPE = 128
ROPE = 64
KV_RANK = 512
V_DIM = 128

epsilon = 1e-06
theta_base = 10000.0
SWAP = [(0, 1), (1, 0)]


MESH = pl.DeviceIdType.MESH


class Place:
    def __init__(self, layers):
        self.layers = layers
        self.row, self.col = lax.axis_index("row"), lax.axis_index("col")
        self.layer = lax.axis_index("exp") if layers > 1 else 0
        self.core = lax.rem(self.row, 2)
        self.x_row = lax.rem(self.row + 2, 4)
        self.core_row = self.row + 1 - 2 * self.core
        self.y_col = 1 - self.col
        self.to_x = {"row": self.x_row}
        self.to_y = {"col": self.y_col}
        self.to_core = {"row": self.core_row}
        self.above = {"exp": self.layer + 1}
        self.below = {"exp": self.layer - 1}

    def greet(self):
        barrier = pltpu.get_barrier_semaphore()
        for target in (self.to_x, self.to_y, self.to_core):
            pl.semaphore_signal(barrier, inc=1, device_id=target, device_id_type=MESH)
        if self.layers > 1:

            @pl.when(self.layer > 0)
            def _():
                pl.semaphore_signal(barrier, inc=1, device_id=self.below, device_id_type=MESH)

            @pl.when(self.layer < self.layers - 1)
            def _():
                pl.semaphore_signal(barrier, inc=1, device_id=self.above, device_id_type=MESH)

        peers = 3
        if self.layers > 1:
            peers = peers + jnp.where(self.layer > 0, 1, 0) + jnp.where(self.layer < self.layers - 1, 1, 0)
        pl.semaphore_wait(barrier, peers)


def remote(src, dst, send, recv, target):
    return pltpu.make_async_remote_copy(
        src_ref=src, dst_ref=dst, send_sem=send, recv_sem=recv, device_id=target, device_id_type=MESH
    )


def first_part(rows):
    return (rows // 2 + 15) // 16 * 16


def piece_of(where, layers, shape, by_rows, row, col, layer, span=None):
    rows, width = shape
    start, size = (0, rows) if span is None else span
    if by_rows:
        first = pl.multiple_of((row * 2 + col) * rows + start, 16)
        return where.at[pl.ds(first, size)]
    first = pl.multiple_of((row * layers + layer) * rows + start, 16)
    return where.at[pl.ds(first, size), pl.ds(pl.multiple_of(col * width, 128), width)]


def gather_body(
    layers, by_rows, src, out, held, store_sem, up_send, down_send, z_recv, send, recv, diag_send, diag_recv
):
    me = Place(layers)
    rows, width = src.shape
    part = first_part(rows)
    spans = ((0, part), (part, rows - part))

    owners = (
        (me.row, me.col),
        (me.x_row, me.col),
        (me.row, me.y_col),
        (me.x_row, me.y_col),
    )
    sides = (me.to_x, me.to_y)

    def area(where, row, col, layer, span=None):
        return piece_of(where, layers, (rows, width), by_rows, row, col, layer, span)

    def held_piece(kind, layer, span=None):
        return area(held, *owners[kind], layer, span)

    def partner_piece(where, kind, layer):
        row, col = owners[kind]
        return area(where, row + 1 - 2 * me.core, col, layer)

    def store(kind, layer, partner):
        if partner:
            pair = (partner_piece(held, kind, layer), partner_piece(out, kind, layer))
        else:
            pair = (held_piece(kind, layer), area(out, *owners[kind], layer))
        return pltpu.make_async_copy(*pair, store_sem.at[1 if partner else 0, kind, layer])

    def to_core(kind, layer):
        piece = held_piece(kind, layer)
        return remote(piece, piece, send.at[4, kind, layer], recv.at[4, kind, layer], me.to_core)

    def from_core(kind, layer):
        piece = partner_piece(held, kind, layer)
        return remote(piece, piece, send.at[4, kind, layer], recv.at[4, kind, layer], me.to_core)

    def beside(axis, half, layer, incoming=False):
        piece = held_piece(axis + 1 if incoming else 0, layer, spans[half])
        sems = (2 * axis + half, 0, layer)
        return remote(piece, piece, send.at[sems], recv.at[sems], sides[axis])

    def corner(axis, layer, incoming=False):
        piece = held_piece(3 if incoming else axis + 1, layer, spans[axis])
        return remote(
            piece, piece, diag_send.at[axis, layer], diag_recv.at[axis, layer], sides[1 - axis]
        )

    def along(up, layer):
        piece = held_piece(0, layer)
        return remote(
            piece,
            piece,
            (up_send if up else down_send).at[layer],
            z_recv.at[layer],
            me.above if up else me.below,
        )

    def spread(layer):
        beside(0, 0, layer).start()
        beside(1, 1, layer).start()
        beside(0, 1, layer).start()
        beside(1, 0, layer).start()
        to_core(0, layer).start()

    def at_distance(distance, act):
        if distance == 0:
            act(me.layer, None)
            return

        @pl.when(me.layer >= distance)
        def _():
            act(me.layer - distance, True)

        @pl.when(me.layer + distance < layers)
        def _():
            act(me.layer + distance, False)

    own = pltpu.make_async_copy(src, held_piece(0, me.layer), store_sem.at[0, 0, me.layer])
    own.start()
    me.greet()
    own.wait()
    if layers > 1:

        @pl.when(me.layer < layers - 1)
        def _():
            along(True, me.layer).start()

        @pl.when(me.layer > 0)
        def _():
            along(False, me.layer).start()

    spread(me.layer)
    store(0, me.layer, False).start()

    def arrived(layer, upward):
        along(upward, layer).wait_recv()
        if upward:

            @pl.when(me.layer < layers - 1)
            def _():
                along(True, layer).start()
        else:

            @pl.when(me.layer > 0)
            def _():
                along(False, layer).start()

        spread(layer)
        store(0, layer, False).start()

    def second(layer, upward):
        for axis in (0, 1):
            beside(axis, axis, layer, True).wait_recv()
            corner(axis, layer).start()
        for axis in (0, 1):
            beside(axis, 1 - axis, layer, True).wait_recv()
            to_core(axis + 1, layer).start()
            store(axis + 1, layer, False).start()

    def third(layer, upward):
        for axis in (0, 1):
            corner(axis, layer, True).wait_recv()
        to_core(3, layer).start()
        store(3, layer, False).start()
        for kind in range(4):
            from_core(kind, layer).wait_recv()
            store(kind, layer, True).start()

    for step in range(1, layers + 2):
        if step < layers:
            at_distance(step, arrived)
        if step - 1 < layers:
            at_distance(step - 1, second)
        if 0 <= step - 2 < layers:
            at_distance(step - 2, third)
    for layer in range(layers):
        for kind in range(4):
            to_core(kind, layer).wait_send()
            store(kind, layer, False).wait()
            store(kind, layer, True).wait()
        for axis in (0, 1):
            for half in (0, 1):
                beside(axis, half, layer).wait_send()
            corner(axis, layer).wait_send()
    if layers > 1:
        for layer in range(layers):

            @pl.when((me.layer < layers - 1) & (layer <= me.layer))
            def _():
                along(True, layer).wait_send()

            @pl.when((me.layer > 0) & (layer >= me.layer))
            def _():
                along(False, layer).wait_send()


def gather(value, layers, collective_id, by_rows=False):
    rows, width = value.shape
    dma = pltpu.SemaphoreType.DMA
    whole = (8 * rows, width) if by_rows else (4 * layers * rows, 2 * width)
    return pl.pallas_call(
        functools.partial(gather_body, layers, by_rows),
        out_shape=jax.ShapeDtypeStruct(whole, value.dtype),
        in_specs=[pl.BlockSpec(memory_space=pl.ANY)],
        out_specs=pl.BlockSpec(memory_space=pl.ANY),
        scratch_shapes=[
            pltpu.VMEM(whole, value.dtype),
            dma((2, 4, layers)),
            dma((layers,)),
            dma((layers,)),
            dma((layers,)),
            dma((5, 4, layers)),
            dma((5, 4, layers)),
            dma((2, layers)),
            dma((2, layers)),
        ],
        compiler_params=pltpu.CompilerParams(
            collective_id=collective_id,
            has_side_effects=True,
            vmem_limit_bytes=56 * 1024 * 1024,
        ),
    )(value)


def scatter_body(
    layers,
    by_rows,
    src,
    out,
    acc,
    core_in,
    diag_a,
    diag_b,
    side_in,
    line_in,
    load_sem,
    core_send,
    core_recv,
    diag_send,
    diag_recv,
    side_send,
    side_recv,
    line_send,
    line_recv,
):
    me = Place(layers)
    rows, width = out.shape
    part = first_part(rows)
    owners = (
        (me.row, me.col),
        (me.x_row, me.col),
        (me.row, me.y_col),
        (me.x_row, me.y_col),
    )

    def layer_at(step):
        if layers == 1:
            return 0
        found = 0
        for layer in range(layers):
            order = sorted(range(layers), key=lambda other: (-abs(other - layer), -other))
            found = found + jnp.where(me.layer == layer, order[step], 0)
        return found

    layer_of = [layer_at(step) for step in range(layers)]

    def area(row, col, layer):
        return piece_of(src, layers, (rows, width), by_rows, row, col, layer)

    def load(step, kind):
        return pltpu.make_async_copy(
            area(*owners[kind], layer_of[step]), acc.at[step, kind], load_sem.at[step, kind]
        )

    def to_core(step, kind):
        row, col = owners[kind]
        return remote(
            area(row + 1 - 2 * me.core, col, layer_of[step]),
            core_in.at[step, kind],
            core_send.at[step, kind],
            core_recv.at[step, kind],
            me.to_core,
        )

    def diag(step, axis):
        start, size = ((0, part), (part, rows - part))[axis]
        return remote(
            acc.at[step, 3, pl.ds(start, size)],
            (diag_a, diag_b)[axis].at[step],
            diag_send.at[axis, step],
            diag_recv.at[axis, step],
            (me.to_y, me.to_x)[axis],
        )

    def side(step, axis):
        return remote(
            acc.at[step, axis + 1],
            side_in.at[axis, step],
            side_send.at[axis, step],
            side_recv.at[axis, step],
            (me.to_x, me.to_y)[axis],
        )

    def line(step, up):
        layer = layer_of[step]
        way = 0 if up else 1
        return remote(
            acc.at[step, 0],
            line_in.at[way, layer],
            line_send.at[step],
            line_recv.at[way, layer],
            me.above if up else me.below,
        )

    lanes = 32 if part % 32 == 0 and rows % 32 == 0 else 16

    def add(target, others, start=0, size=rows, into=None):
        def step(i, carry):
            first = pl.multiple_of(i * lanes, 16)
            total = target[pl.ds(start + first, lanes), :].astype(jnp.float32)
            for other in others:
                total = total + other[pl.ds(first, lanes), :].astype(jnp.float32)
            if into is None:
                target[pl.ds(start + first, lanes), :] = total.astype(target.dtype)
            else:
                into[pl.ds(first, lanes), :] = total.astype(into.dtype)
            return carry

        lax.fori_loop(0, size // lanes, step, 0)

    me.greet()
    kinds = (3, 1, 2, 0)
    for step in range(layers):
        for kind in kinds:
            to_core(step, kind).start()
            load(step, kind).start()

    def ready(step, kind):
        load(step, kind).wait()
        to_core(step, kind).wait_recv()

    def stage_a(step):
        ready(step, 3)
        add(acc.at[step, 3], [core_in.at[step, 3]])
        diag(step, 0).start()
        diag(step, 1).start()

    def stage_b(step):
        for axis, buffer, start, size in (
            (0, diag_a, 0, part),
            (1, diag_b, part, rows - part),
        ):
            kind = axis + 1
            ready(step, kind)
            add(acc.at[step, kind], [core_in.at[step, kind]])
            diag(step, axis).wait_recv()
            add(acc.at[step, kind], [buffer.at[step]], start, size)
            side(step, axis).start()

    def stage_c(step):
        ready(step, 0)
        side(step, 0).wait_recv()
        side(step, 1).wait_recv()
        parts = [core_in.at[step, 0], side_in.at[0, step], side_in.at[1, step]]
        if layers == 1:
            add(acc.at[step, 0], parts, into=out)
            return
        add(acc.at[step, 0], parts)
        layer = layer_of[step]
        if step < layers - 1:

            @pl.when((layer > me.layer) & (me.layer > 0))
            def _():
                line(step, True).wait_recv()
                add(acc.at[step, 0], [line_in.at[0, layer]])

            @pl.when((layer < me.layer) & (me.layer < layers - 1))
            def _():
                line(step, False).wait_recv()
                add(acc.at[step, 0], [line_in.at[1, layer]])

            @pl.when(layer > me.layer)
            def _():
                line(step, True).start()

            @pl.when(layer < me.layer)
            def _():
                line(step, False).start()
        else:
            inner = (me.layer > 0) & (me.layer < layers - 1)

            @pl.when(me.layer > 0)
            def _():
                line(step, True).wait_recv()

            @pl.when(me.layer < layers - 1)
            def _():
                line(step, False).wait_recv()

            @pl.when(inner)
            def _():
                add(acc.at[step, 0], [line_in.at[0, layer], line_in.at[1, layer]], into=out)

            @pl.when(me.layer == 0)
            def _():
                add(acc.at[step, 0], [line_in.at[1, layer]], into=out)

            @pl.when(me.layer == layers - 1)
            def _():
                add(acc.at[step, 0], [line_in.at[0, layer]], into=out)

    for step in range(layers + 2):
        if step < layers:
            stage_a(step)
        if 0 <= step - 1 < layers:
            stage_b(step - 1)
        if 0 <= step - 2 < layers:
            stage_c(step - 2)
    for step in range(layers):
        for kind in kinds:
            to_core(step, kind).wait_send()
        for axis in (0, 1):
            diag(step, axis).wait_send()
            side(step, axis).wait_send()
        if step < layers - 1:

            @pl.when(layer_of[step] > me.layer)
            def _():
                line(step, True).wait_send()

            @pl.when(layer_of[step] < me.layer)
            def _():
                line(step, False).wait_send()


def scatter(value, layers, collective_id, by_rows=False):
    if by_rows:
        rows, width = value.shape[0] // 8, value.shape[1]
    else:
        rows, width = value.shape[0] // (4 * layers), value.shape[1] // 2
    part = first_part(rows)
    dma = pltpu.SemaphoreType.DMA
    buffer = lambda *lead: pltpu.VMEM((*lead, rows, width), value.dtype)
    return pl.pallas_call(
        functools.partial(scatter_body, layers, by_rows),
        out_shape=jax.ShapeDtypeStruct((rows, width), jnp.float32),
        in_specs=[pl.BlockSpec(memory_space=pl.ANY)],
        out_specs=pl.BlockSpec(memory_space=pltpu.VMEM),
        scratch_shapes=[
            buffer(layers, 4),
            buffer(layers, 4),
            pltpu.VMEM((layers, part, width), value.dtype),
            pltpu.VMEM((layers, rows - part, width), value.dtype),
            buffer(2, layers),
            buffer(2, layers),
            dma((layers, 4)),
            dma((layers, 4)),
            dma((layers, 4)),
            dma((2, layers)),
            dma((2, layers)),
            dma((2, layers)),
            dma((2, layers)),
            dma((layers,)),
            dma((2, layers)),
        ],
        compiler_params=pltpu.CompilerParams(
            collective_id=collective_id,
            has_side_effects=True,
            vmem_limit_bytes=56 * 1024 * 1024,
        ),
    )(value)


def dot_nn(left, right):
    return jnp.dot(left, right, preferred_element_type=jnp.float32)


def dot_nt(left, right):
    return lax.dot_general(
        left, right, (((1,), (1,)), ((), ())), preferred_element_type=jnp.float32
    )


def dot_tn(left, right):
    return lax.dot_general(
        left, right, (((0,), (0,)), ((), ())), preferred_element_type=jnp.float32
    )


def small_sum_body(layers, src, out, core_in, mid, x_in, near, line_in, total, send, recv, line_send, line_recv):
    me = Place(layers)
    width = src.shape[1]
    barrier = pltpu.get_barrier_semaphore()
    for target in (me.to_x, me.to_y, me.to_core):
        pl.semaphore_signal(barrier, inc=1, device_id=target, device_id_type=MESH)
    for step in range(1, layers):
        other = {"exp": lax.rem(me.layer + step, layers)}
        pl.semaphore_signal(barrier, inc=1, device_id=other, device_id_type=MESH)
    pl.semaphore_wait(barrier, 3 + layers - 1)
    swap = remote(src, core_in, send.at[0], recv.at[0], me.to_core)
    swap.start()
    swap.wait()
    mid[...] = src[...] + core_in[...]
    swap = remote(mid, x_in, send.at[1], recv.at[1], me.to_x)
    swap.start()
    swap.wait()
    near[...] = mid[...] + x_in[...]
    line_in[me.layer] = near[...]

    def along(step, incoming):
        layer = lax.rem(me.layer + (layers - step if incoming else 0), layers)
        return remote(
            near,
            line_in.at[layer],
            line_send.at[step],
            line_recv.at[step],
            {"exp": lax.rem(me.layer + step, layers)},
        )

    for step in range(1, layers):
        along(step, False).start()
    for step in range(1, layers):
        along(step, True).wait_recv()
    summed = line_in[0]
    for layer in range(1, layers):
        summed = summed + line_in[layer]
    total[...] = summed
    mine = pl.ds(pl.multiple_of(me.col * width, 128), width)
    theirs = pl.ds(pl.multiple_of(me.y_col * width, 128), width)
    out[:, mine] = summed
    remote(total, out.at[:, mine], send.at[2], recv.at[2], me.to_y).start()
    remote(total, out.at[:, theirs], send.at[2], recv.at[2], me.to_y).wait()
    for step in range(1, layers):
        along(step, False).wait_send()


def small_sum(value, layers, collective_id):
    rows, width = value.shape
    dma = pltpu.SemaphoreType.DMA
    buffer = lambda *lead: pltpu.VMEM((*lead, rows, width), value.dtype)
    in_vmem = pl.BlockSpec(memory_space=pltpu.VMEM)
    return pl.pallas_call(
        functools.partial(small_sum_body, layers),
        out_shape=jax.ShapeDtypeStruct((rows, 2 * width), value.dtype),
        in_specs=[in_vmem],
        out_specs=in_vmem,
        scratch_shapes=[
            buffer(),
            buffer(),
            buffer(),
            buffer(),
            buffer(layers),
            buffer(),
            dma((3,)),
            dma((3,)),
            dma((layers,)),
            dma((layers,)),
        ],
        compiler_params=pltpu.CompilerParams(
            collective_id=collective_id,
            has_side_effects=True,
            vmem_limit_bytes=32 * 1024 * 1024,
        ),
    )(value)


def expert_body(
    layers,
    few,
    slots,
    units,
    experts,
    rows_ref,
    grads_ref,
    pick_ref,
    spread_ref,
    words_ref,
    gate_w,
    up_w,
    down_w,
    side_w,
    side_down,
    d_rows_ref,
    out_ref,
    slot_rows_ref,
    slot_grads_ref,
    hidden_ref,
    d_gate_ref,
    d_up_ref,
    d_gates_ref,
    grad_side_ref,
    grad_side_down_ref,
    d_slots,
    slot_out,
    side_hidden_ref,
    d_side_ref,
):
    bf16, f32 = jnp.bfloat16, jnp.float32
    own_expert = lax.axis_index("row") * layers + lax.axis_index("exp")
    count = rows_ref.shape[0] // few
    block, half = grads_ref.shape[2:]
    lanes = side_down.shape[0]

    side = dot_nt(rows_ref[...], side_w[...])
    side_gate, side_up = side[:, :lanes], side[:, lanes:]
    lane = lax.broadcasted_iota(jnp.int32, side_gate.shape, 1)
    expert = lane - units
    is_expert = (expert >= 0) & (expert < experts)
    highest = jnp.max(jnp.where(is_expert, side_gate, -jnp.inf), axis=1, keepdims=True)
    words = words_ref[...]
    word = words[:, 0:1]
    for i in range(1, words.shape[1]):
        word = jnp.where(expert >= 16 * i, words[:, i : i + 1], word)
    picked = lax.shift_right_logical(
        jnp.broadcast_to(word, expert.shape), jnp.bitwise_and(expert, 15)
    )
    picked = is_expert & (jnp.bitwise_and(picked, 1) == 1)
    chosen = jnp.where(picked, jnp.exp(jnp.where(is_expert, side_gate - highest, 0.0)), 0.0)
    total = jnp.sum(chosen, axis=1, keepdims=True)
    own = jnp.sum(jnp.where(expert == own_expert, chosen, 0.0), axis=1, keepdims=True) / total

    def two_parts(value):
        high = value.astype(bf16).astype(f32)
        at = lax.broadcasted_iota(jnp.int32, (value.shape[0], lanes), 1)
        return jnp.where(at == 0, high, jnp.where(at == 1, value - high, 0.0)).astype(bf16)

    own_parts = two_parts(own)
    slot_gates = []
    for b in range(count):
        tokens, here = pl.ds(b * few, few), pl.ds(b * slots, slots)
        pick = pick_ref[here, :]
        slot_rows_ref[here, :] = dot_nn(pick, rows_ref[tokens, :]).astype(bf16)
        first = b * few % block
        for c in range(2):
            slot_grads_ref[here, c * half : (c + 1) * half] = dot_nn(
                pick, grads_ref[b * few // block, c, first : first + few, :]
            ).astype(bf16)
        parts = dot_nn(pick, own_parts[b * few : (b + 1) * few])
        slot_gates.append(jnp.sum(parts, axis=1, keepdims=True))
    slot_gate = jnp.concatenate(slot_gates, axis=0)

    gate_pre = dot_nt(slot_rows_ref[...], gate_w[...])
    up_pre = dot_nt(slot_rows_ref[...], up_w[...])
    d_raw = dot_nt(slot_grads_ref[...], down_w[...])
    sigmoid = 1.0 / (1.0 + jnp.exp(-gate_pre))
    silu = gate_pre * sigmoid
    hidden = (silu * up_pre).astype(bf16).astype(f32)
    d_gates = jnp.sum(d_raw * hidden, axis=1, keepdims=True)
    hidden_ref[...] = (hidden * slot_gate).astype(bf16)
    d_hidden = d_raw * slot_gate
    d_up_ref[...] = (d_hidden * silu).astype(bf16)
    d_gate_ref[...] = (
        d_hidden * up_pre * sigmoid * (1.0 + gate_pre * (1.0 - sigmoid))
    ).astype(bf16)
    d_slots[...] = (dot_nn(d_gate_ref[...], gate_w[...]) + dot_nn(d_up_ref[...], up_w[...])).astype(
        bf16
    )
    slot_out[...] = dot_nn(hidden_ref[...], down_w[...]).astype(bf16)

    side_sigmoid = 1.0 / (1.0 + jnp.exp(-side_gate))
    side_silu = side_gate * side_sigmoid
    side_hidden_ref[...] = (side_silu * side_up).astype(bf16)
    d_side_hidden = sum(
        dot_nt(grads_ref[:, c].reshape(-1, half), side_down[:, c * half : (c + 1) * half])
        for c in range(2)
    )
    d_side_ref[:, lanes:] = (d_side_hidden * side_silu).astype(bf16)
    d_side_ref[:, :lanes] = (
        d_side_hidden * side_up * side_sigmoid * (1.0 + side_gate * (1.0 - side_sigmoid))
    ).astype(bf16)

    @pl.when(pl.program_id(0) == 0)
    def _():
        grad_side_ref[...] = jnp.zeros_like(grad_side_ref)
        grad_side_down_ref[...] = jnp.zeros_like(grad_side_down_ref)

    grad_side_ref[...] += dot_tn(d_side_ref[...], rows_ref[...])
    for c in range(2):
        grad_side_down_ref[:, c * half : (c + 1) * half] += dot_tn(
            side_hidden_ref[...], grads_ref[:, c].reshape(-1, half)
        )

    d_gate_parts = two_parts(d_gates)
    for b in range(count):
        tokens, here = pl.ds(b * few, few), pl.ds(b * slots, slots)
        spread = spread_ref[tokens, :]
        d_rows_ref[tokens, :] = (
            dot_nn(spread, d_slots[here, :]) + dot_nn(d_side_ref[tokens, :], side_w[...])
        ).astype(bf16)
        out_ref[tokens, :] = (
            dot_nn(spread, slot_out[here, :]) + dot_nn(side_hidden_ref[tokens, :], side_down[...])
        ).astype(bf16)
        back = dot_nn(spread, d_gate_parts[b * slots : (b + 1) * slots])
        d_gates_ref[tokens, :] = jnp.sum(back, axis=1, keepdims=True)


def expert_pass(layers, few, slots, units, experts, rows, grads, pick, spread, words, weights, side_w, side_down):
    tokens, width = rows.shape
    hidden = weights[0].shape[0]
    block = grads.shape[2]
    blocks = tokens // few
    count = next(n for n in (4, 2, 1) if blocks % n == 0 and n * few <= 640)
    lanes = side_down.shape[0]
    grid = (blocks // count,)
    by_step = lambda n, w: pl.BlockSpec((count * n, w), lambda i: (i, 0))
    whole = lambda value: pl.BlockSpec(
        value.shape, lambda i: (0, 0), pipeline_mode=pl.Buffered(1)
    )
    shape = lambda n, w, kind=jnp.bfloat16: jax.ShapeDtypeStruct((blocks * n, w), kind)
    return pl.pallas_call(
        functools.partial(expert_body, layers, few, slots, units, experts),
        grid=grid,
        in_specs=[
            by_step(few, width),
            pl.BlockSpec((count * few // block, 2, block, width // 2), lambda i: (i, 0, 0, 0)),
            by_step(slots, few),
            by_step(few, slots),
            by_step(few, words.shape[1]),
            *(whole(w) for w in (*weights, side_w, side_down)),
        ],
        out_specs=[
            by_step(few, width),
            by_step(few, width),
            by_step(slots, width),
            by_step(slots, width),
            by_step(slots, hidden),
            by_step(slots, hidden),
            by_step(slots, hidden),
            by_step(few, 1),
            pl.BlockSpec((2 * lanes, width), lambda i: (0, 0)),
            pl.BlockSpec((lanes, width), lambda i: (0, 0)),
        ],
        out_shape=[
            shape(few, width),
            shape(few, width),
            shape(slots, width),
            shape(slots, width),
            shape(slots, hidden),
            shape(slots, hidden),
            shape(slots, hidden),
            shape(few, 1, jnp.float32),
            jax.ShapeDtypeStruct((2 * lanes, width), jnp.float32),
            jax.ShapeDtypeStruct((lanes, width), jnp.float32),
        ],
        scratch_shapes=[
            pltpu.VMEM((count * slots, width), jnp.bfloat16),
            pltpu.VMEM((count * slots, width), jnp.bfloat16),
            pltpu.VMEM((count * few, lanes), jnp.bfloat16),
            pltpu.VMEM((count * few, 2 * lanes), jnp.bfloat16),
        ],
        compiler_params=pltpu.CompilerParams(vmem_limit_bytes=62 * 1024 * 1024),
    )(rows, grads, pick, spread, words, *weights, side_w, side_down)


def rotate(value, cosine, sine):
    half = value.shape[-1] // 2
    first, second = (value[..., :half], value[..., half:])
    return jnp.concatenate(
        [first * cosine - second * sine, first * sine + second * cosine], axis=-1
    )


def unrotate(value, cosine, sine):
    half = value.shape[-1] // 2
    first, second = (value[..., :half], value[..., half:])
    return jnp.concatenate(
        [first * cosine + second * sine, second * cosine - first * sine], axis=-1
    )


def sequence_layout(lengths_row, group):
    ends = jnp.cumsum(lengths_row)
    starts = ends - lengths_row
    index = jnp.arange(group, dtype=jnp.int32)
    seq_ids = jnp.sum((index[:, None] >= ends[None, :]).astype(jnp.int32), axis=1)
    member = seq_ids[:, None] == jnp.arange(lengths_row.shape[0], dtype=jnp.int32)[None, :]
    begins = jnp.sum(jnp.where(member, starts[None, :], 0), axis=1)
    return (seq_ids, index - begins)


def rotary_tables(places):
    half = ROPE // 2
    freqs = jnp.power(theta_base, -jnp.arange(half, dtype=jnp.float32) * (2.0 / ROPE))
    angle = places.astype(jnp.float32)[..., None] * freqs
    return (jnp.cos(angle), jnp.sin(angle))


def norm_back(value, factor, gain, grad, width):
    weighted = grad * gain
    inner = lax.psum(jnp.sum(weighted * value, axis=1), "col")
    d_value = (
        factor[:, None] * weighted - value * (factor * factor * factor * inner / width)[:, None]
    )
    d_gain = jnp.sum(grad * value * factor[:, None], axis=0)
    return (d_value, d_gain)


def masked_scores(query_block, keys, seq_ids, first, scale):
    size = query_block.shape[0]
    group = keys.shape[0]
    scored = (
        jnp.einsum("qhd,khd->hqk", query_block, keys, preferred_element_type=jnp.float32) * scale
    )
    query_index = first + jnp.arange(size, dtype=jnp.int32)
    key_index = jnp.arange(group, dtype=jnp.int32)
    allowed = (seq_ids[first : first + size][:, None] == seq_ids[None, :group]) & (
        key_index[None, :] <= query_index[:, None]
    )
    return jnp.where(allowed[None, :, :], scored, -1e30)


def own_slice(value, index, axis):
    size = value.shape[axis] // 2
    return lax.dynamic_slice_in_dim(value, index * size, size, axis)


def col_pair(mine, sent, axis):
    received = lax.ppermute(sent, "col", SWAP)
    first = lax.axis_index("col") == 0
    return jnp.where(
        first,
        jnp.concatenate([mine, received], axis=axis),
        jnp.concatenate([received, mine], axis=axis),
    )


def trade(value, split, join):
    col = lax.axis_index("col")
    return col_pair(own_slice(value, col, split), own_slice(value, 1 - col, split), join)


def routed_and_shared(
    tok_dev, capacity, layers, router, expert_weights, shared_own, normed_own, grads_own, words
):
    bf16 = jnp.bfloat16
    col_id = lax.axis_index("col")
    own_expert = lax.axis_index("row") * layers + lax.axis_index("exp")
    experts = router.shape[1]
    units = shared_own.shape[1]
    block, half_width = normed_own.shape
    tokens = words.shape[0]
    few = min(tok_dev, block)
    slots = -(-min(capacity, few) // 16) * 16
    blocks = tokens // few

    own_word = lax.dynamic_index_in_dim(words, own_expert // 16, 1, keepdims=False)
    own_pick = (jnp.bitwise_and(lax.shift_right_logical(own_word, own_expert % 16), 1) == 1).reshape(
        blocks, few
    )
    order = jnp.arange(few, dtype=jnp.int32)
    place = dot_nn(own_pick.astype(bf16), (order[:, None] < order[None, :]).astype(bf16)).astype(
        jnp.int32
    )
    places = jnp.arange(slots, dtype=jnp.int32)
    pick = ((place[:, None, :] == places[None, :, None]) & own_pick[:, None, :]).astype(bf16)
    spread = ((place[:, :, None] == places[None, None, :]) & own_pick[:, :, None]).astype(bf16)
    lanes = -(-(units + experts) // 128) * 128
    fill = lambda value, n: jnp.pad(value, ((0, n - value.shape[0]), (0, 0)))
    side_w = jnp.concatenate(
        [fill(jnp.concatenate([shared_own[0], router.T]), lanes), fill(shared_own[1], lanes)]
    )
    side_down = fill(shared_own[2], lanes)

    grads_all = lax.all_gather(grads_own, ("row", "exp", "col"), axis=0)
    grads_all = grads_all.reshape(experts, 2, block, half_width)
    normed_all = gather(normed_own, layers, 3)
    (
        d_rows,
        out_rows,
        slot_rows,
        slot_grads,
        hidden,
        d_gate,
        d_up,
        d_gates_all,
        grad_side,
        grad_side_down,
    ) = expert_pass(
        layers,
        few,
        slots,
        units,
        experts,
        normed_all,
        grads_all,
        pick.reshape(blocks * slots, few),
        spread.reshape(tokens, slots),
        words,
        expert_weights,
        side_w,
        side_down,
    )
    d_normed = scatter(d_rows, layers, 4)
    grad_gate = dot_tn(d_gate, slot_rows)
    grad_up = dot_tn(d_up, slot_rows)
    grad_down = dot_tn(hidden, slot_grads)
    grad_shared = jnp.stack(
        [grad_side[:units], grad_side[lanes : lanes + units], grad_side_down[:units]]
    )

    d_gates = lax.psum(
        lax.all_to_all(
            d_gates_all.reshape(experts, block), ("row", "exp"), split_axis=0, concat_axis=0, tiled=True
        ),
        "col",
    ).T
    own_probs = jax.nn.softmax(
        dot_nn(lax.dynamic_slice_in_dim(normed_all, own_expert * block, block, 0), router), axis=1
    )
    own_words = lax.dynamic_slice_in_dim(words, own_expert * block, block, 0)
    numbers = jnp.arange(experts, dtype=jnp.int32)
    picks = (
        jnp.bitwise_and(
            lax.shift_right_logical(own_words[:, numbers // 16], (numbers % 16)[None, :]), 1
        )
        == 1
    )
    selected = jnp.where(picks, own_probs, 0.0)
    own_total = jnp.sum(selected, axis=1, keepdims=True)
    own_gates = selected / own_total
    d_selected = (d_gates - jnp.sum(d_gates * own_gates, axis=1, keepdims=True)) / own_total
    d_router_probs = jnp.where(picks, d_selected, 0.0)
    d_logits = own_probs * (
        d_router_probs - jnp.sum(own_probs * d_router_probs, axis=1, keepdims=True)
    )
    router_half = lax.dynamic_slice_in_dim(router, col_id * half_width, half_width, 0)
    grad_router = lax.dot_general(
        normed_own.astype(jnp.float32),
        d_logits,
        (((0,), (0,)), ((), ())),
        precision=lax.Precision.HIGHEST,
        preferred_element_type=jnp.float32,
    )
    d_normed = d_normed + lax.dot_general(
        d_logits,
        router_half.astype(jnp.float32),
        (((1,), (1,)), ((), ())),
        precision=lax.Precision.HIGHEST,
        preferred_element_type=jnp.float32,
    )
    return (d_normed, out_rows, (grad_gate, grad_up, grad_down, grad_shared, grad_router))


def per_device(
    layer_input,
    lengths,
    routes,
    norm1_gain,
    w_query,
    w_latent,
    latent_gain,
    w_kv,
    w_out,
    norm2_gain,
    shared_gate,
    shared_up,
    shared_down,
    router,
    expert_gate,
    expert_up,
    expert_down,
    cotangent,
):
    row_id = lax.axis_index("row")
    col_id = lax.axis_index("col")
    exp_id = lax.axis_index("exp")
    rows_n, cols_n, exps_n = (lax.axis_size(name) for name in ("row", "col", "exp"))
    experts = rows_n * exps_n
    own_expert = row_id * exps_n + exp_id
    tok_dev = routes.shape[1]
    topk_count = routes.shape[2]
    capacity = max(2, 3 * tok_dev * topk_count // (2 * experts))
    slots = -(-capacity // 16) * 16
    block, half_width = layer_input.shape
    width = half_width * cols_n
    group = block * rows_n
    tokens = group * exps_n
    heads_here = w_kv.shape[1] // (QK_NOPE + V_DIM)
    head_dim = QK_NOPE + ROPE
    scale = 1.0 / math.sqrt(head_dim)
    query_rows = group // 2
    bf16 = jnp.bfloat16

    w_query_own = trade(w_query, 1, 0)
    w_latent_all = lax.all_gather(w_latent[0].T, ("col", "row"), axis=1, tiled=True)
    seq_ids, places = sequence_layout(lengths[0], group)
    cosine, sine = rotary_tables(places)

    group_input = gather(layer_input, 1, 1)
    group_input, w_out, shared_gate, shared_up, shared_down, cotangent = lax.optimization_barrier(
        (group_input, w_out, shared_gate, shared_up, shared_down, cotangent)
    )
    w_out_own = trade(w_out, 0, 1)
    units = shared_gate.shape[1] // (cols_n * exps_n)
    shared_parts = jnp.stack(
        [
            lax.dynamic_index_in_dim(
                part.reshape(cols_n, exps_n, units, half_width), exp_id, 1, keepdims=False
            )
            for part in (shared_gate.T, shared_up.T, shared_down)
        ]
    )
    shared_own = trade(shared_parts, 1, 3)[:, 0]

    group_input = group_input.astype(jnp.float32)
    factor_group = lax.rsqrt(jnp.mean(group_input * group_input, axis=1) + epsilon)
    normed_group = (group_input * factor_group[:, None] * norm1_gain).astype(bf16)
    query_pre = dot_nn(normed_group, w_query_own).reshape(group, heads_here, head_dim)
    queries = jnp.concatenate(
        [
            query_pre[..., :QK_NOPE],
            rotate(query_pre[..., QK_NOPE:], cosine[:, None, :], sine[:, None, :]),
        ],
        axis=2,
    ).astype(bf16)
    latent = dot_nt(normed_group, w_latent_all)
    compressed_raw = latent[:, :KV_RANK]
    kv_factor = lax.rsqrt(jnp.mean(compressed_raw * compressed_raw, axis=1) + epsilon)
    compressed = (compressed_raw * kv_factor[:, None] * latent_gain).astype(bf16)
    rotary_key = rotate(latent[:, KV_RANK:], cosine, sine).astype(bf16)
    key_value = (
        dot_nn(compressed, w_kv).astype(bf16).reshape(group, heads_here, QK_NOPE + V_DIM)
    )
    keys = jnp.concatenate(
        [
            key_value[..., :QK_NOPE],
            jnp.broadcast_to(rotary_key[:, None, :], (group, heads_here, ROPE)),
        ],
        axis=2,
    )
    values = key_value[..., QK_NOPE:]
    block_outputs = []
    block_totals = []
    for first in range(0, group, query_rows):
        last = first + query_rows
        scores = masked_scores(queries[first:last], keys[:last], seq_ids, first, scale)
        highest = jnp.max(scores, axis=2, keepdims=True)
        log_total = highest + jnp.log(jnp.sum(jnp.exp(scores - highest), axis=2, keepdims=True))
        probs_low = jnp.exp(scores - log_total).astype(bf16)
        block_outputs.append(
            jnp.einsum(
                "hqk,khd->qhd", probs_low, values[:last], preferred_element_type=jnp.float32
            ).astype(bf16)
        )
        block_totals.append(log_total)
    attended = jnp.concatenate(block_outputs, axis=0).reshape(group, heads_here * V_DIM)

    input_wide = layer_input.astype(jnp.float32)
    hidden_state = input_wide + scatter(dot_nn(attended, w_out_own).astype(bf16), 1, 2)
    words_n = -(-experts // 16)
    word_of = jnp.arange(words_n, dtype=jnp.int32)[:, None, None]
    bits = jnp.where(routes // 16 == word_of, jnp.left_shift(1, routes % 16), 0)
    bits = jnp.sum(bits, axis=2).astype(jnp.float32)
    padded = -(-tok_dev // 128) * 128
    bits = jnp.pad(bits, ((0, 0), (0, padded - tok_dev)))
    is_here = jnp.arange(experts, dtype=jnp.int32) == own_expert
    bits = jnp.where(is_here[:, None, None], bits[None], 0.0).reshape(experts * words_n, padded)
    bits, hidden_state = lax.optimization_barrier((bits, hidden_state))
    bits = small_sum(bits, exps_n, 8).reshape(experts, words_n, cols_n, padded)[..., :tok_dev]
    words_all = bits.astype(jnp.int32).transpose(0, 2, 3, 1).reshape(tokens, words_n)

    gain_two = lax.dynamic_slice_in_dim(norm2_gain, col_id * half_width, half_width)
    square = lax.psum(jnp.sum(hidden_state * hidden_state, axis=1), "col")
    factor_two = lax.rsqrt(square / width + epsilon)
    normed_two = (hidden_state * factor_two[:, None] * gain_two).astype(bf16)
    pieces = max(1, exps_n // 4)
    feed = functools.partial(
        routed_and_shared,
        tok_dev,
        capacity,
        exps_n,
        router,
        (expert_gate[0].T, expert_up[0].T, expert_down[0].T),
        shared_own,
    )
    if pieces == 1:
        d_normed, out_rows, weight_grads = feed(normed_two, cotangent, words_all)
    else:
        piece_rows = block // pieces

        def one_piece(total, items):
            d_rows, out_rows, grads = feed(*items)
            return (jax.tree.map(jnp.add, total, grads), (d_rows, scatter(out_rows, exps_n, 4)))

        split = lambda value: value.reshape(pieces, piece_rows, half_width)
        word_pieces = words_all.reshape(experts, pieces, piece_rows, words_n)
        items = (
            split(normed_two),
            split(cotangent),
            word_pieces.transpose(1, 0, 2, 3).reshape(pieces, -1, words_n),
        )
        shapes = jax.eval_shape(lambda: feed(*(item[0] for item in items))[2])
        start = jax.tree.map(lambda leaf: jnp.zeros(leaf.shape, leaf.dtype), shapes)
        weight_grads, (d_normed, branch) = lax.scan(one_piece, start, items)
        d_normed, branch = (v.reshape(block, half_width) for v in (d_normed, branch))
    grad_gate, grad_up, grad_down, grad_shared, grad_router = weight_grads
    grad_shared = trade(grad_shared.astype(bf16)[:, None], 3, 1)
    d_normed, grad_shared = lax.optimization_barrier((d_normed, grad_shared))
    grad_shared = lax.all_gather(grad_shared, "exp", axis=2, tiled=False)
    d_norm_two, grad_gain_two = norm_back(hidden_state, factor_two, gain_two, d_normed, width)
    d_hidden_state = cotangent.astype(jnp.float32) + d_norm_two

    d_branch = gather(d_hidden_state.astype(bf16), 1, 1)
    grad_w_out = trade(dot_tn(attended, d_branch).astype(bf16), 1, 0)
    d_attended = dot_nt(d_branch, w_out_own).astype(bf16).reshape(group, heads_here, V_DIM)
    d_query_blocks = []
    d_keys = jnp.zeros((group, heads_here, head_dim), jnp.float32)
    d_values = jnp.zeros((group, heads_here, V_DIM), jnp.float32)
    for number, first in enumerate(range(0, group, query_rows)):
        last = first + query_rows
        query_block = queries[first:last]
        d_block = d_attended[first:last]
        scores = masked_scores(query_block, keys[:last], seq_ids, first, scale)
        probs = jnp.exp(scores - block_totals[number])
        d_probs = jnp.einsum(
            "qhd,khd->hqk", d_block, values[:last], preferred_element_type=jnp.float32
        )
        delta = jnp.sum(probs * d_probs, axis=2, keepdims=True)
        d_scores = (probs * (d_probs - delta)).astype(bf16)
        d_query_blocks.append(
            jnp.einsum("hqk,khd->qhd", d_scores, keys[:last], preferred_element_type=jnp.float32)
            * scale
        )
        d_keys = d_keys.at[:last].add(
            jnp.einsum("hqk,qhd->khd", d_scores, query_block, preferred_element_type=jnp.float32)
            * scale
        )
        d_values = d_values.at[:last].add(
            jnp.einsum(
                "hqk,qhd->khd", probs.astype(bf16), d_block, preferred_element_type=jnp.float32
            )
        )
    d_query = jnp.concatenate(d_query_blocks, axis=0)
    d_query_pre = (
        jnp.concatenate(
            [
                d_query[..., :QK_NOPE],
                unrotate(d_query[..., QK_NOPE:], cosine[:, None, :], sine[:, None, :]),
            ],
            axis=2,
        )
        .astype(bf16)
        .reshape(group, heads_here * head_dim)
    )
    d_key_value = (
        jnp.concatenate([d_keys[..., :QK_NOPE], d_values], axis=2)
        .astype(bf16)
        .reshape(group, heads_here * (QK_NOPE + V_DIM))
    )
    grad_w_kv = dot_tn(compressed, d_key_value)
    d_latent_sum = scatter(
        jnp.concatenate(
            [dot_nt(d_key_value, w_kv), jnp.sum(d_keys[..., QK_NOPE:], axis=1)], axis=1
        ).astype(bf16),
        1,
        5,
        by_rows=True,
    )
    own_first = (row_id * cols_n + col_id) * (group // (rows_n * cols_n))

    def own_tokens(value):
        return lax.dynamic_slice_in_dim(value, own_first, group // (rows_n * cols_n), 0)

    raw_own, factor_own = own_tokens(compressed_raw), own_tokens(kv_factor)
    d_compressed = d_latent_sum[:, :KV_RANK]
    weighted = d_compressed * latent_gain
    grad_latent_gain = jnp.sum(d_compressed * raw_own * factor_own[:, None], axis=0)
    inner = jnp.sum(weighted * raw_own, axis=1)
    d_raw = (
        factor_own[:, None] * weighted
        - raw_own * (factor_own * factor_own * factor_own * inner / KV_RANK)[:, None]
    )
    d_latent = gather(
        jnp.concatenate(
            [d_raw, unrotate(d_latent_sum[:, KV_RANK:], own_tokens(cosine), own_tokens(sine))],
            axis=1,
        ).astype(bf16),
        1,
        6,
        by_rows=True,
    )
    slab = w_latent.shape[1]
    slab_start = col_id * half_width + row_id * slab
    normed_slab = lax.dynamic_slice_in_dim(normed_group, slab_start, slab, 1)
    grad_w_latent = dot_tn(d_latent, normed_slab)
    grad_w_query = trade(dot_tn(normed_group, d_query_pre).astype(bf16), 0, 1)
    d_gathered = dot_nt(d_query_pre, w_query_own)
    piece = lax.dynamic_slice_in_dim(d_gathered, slab_start, slab, 1) + dot_nt(
        d_latent, w_latent[0]
    )
    d_gathered = lax.dynamic_update_slice_in_dim(d_gathered, piece, slab_start, 1)
    d_first = scatter(d_gathered.astype(bf16), 1, 2)
    gain_one = lax.dynamic_slice_in_dim(norm1_gain, col_id * half_width, half_width)
    factor_one = lax.dynamic_slice_in_dim(factor_group, row_id * block, block)
    d_norm_one, grad_gain_one = norm_back(input_wide, factor_one, gain_one, d_first, width)
    input_grad = d_hidden_state + d_norm_one
    if pieces == 1:
        out_rows, input_grad = lax.optimization_barrier((out_rows, input_grad))
        branch = scatter(out_rows, exps_n, 4)
    output = (hidden_state + branch).astype(bf16)

    small = jnp.concatenate(
        [
            grad_gain_one[None],
            grad_gain_two[None],
            jnp.pad(grad_latent_gain, (0, half_width - KV_RANK))[None],
            grad_router.T,
        ],
        axis=0,
    )
    small = jnp.pad(small, ((0, -small.shape[0] % 8), (0, 0)))
    small = small_sum(small, exps_n, 7)
    summed_latent_gain = small[2, :KV_RANK] + small[2, half_width : half_width + KV_RANK]

    grad_shared, grad_w_query = lax.optimization_barrier((grad_shared, grad_w_query))
    grad_shared = grad_shared.reshape(3, cols_n * exps_n * units, half_width).astype(jnp.float32)
    summed = lax.psum(
        (grad_w_query, grad_w_latent.astype(bf16), grad_w_kv.astype(bf16), grad_w_out), "exp"
    )
    return (
        output,
        input_grad,
        small[0],
        summed[0].astype(jnp.float32),
        summed[1].T.astype(jnp.float32)[None],
        summed_latent_gain,
        summed[2].astype(jnp.float32),
        summed[3].astype(jnp.float32),
        small[1],
        grad_shared[0].T,
        grad_shared[1].T,
        grad_shared[2],
        small[3 : 3 + experts].T,
        grad_gate.T[None],
        grad_up.T[None],
        grad_down.T[None],
    )


def solution(mesh):
    placed = (
        P(("row", "exp"), "col"),
        P("exp", None),
        P("col", ("row", "exp"), None),
        P(),
        P("col", "row"),
        P("col", "row", None),
        P(),
        P(None, ("row", "col")),
        P("row", "col"),
        P(),
        P("col", "row"),
        P("col", "row"),
        P("row", "col"),
        P(),
        P(("row", "exp"), None, "col"),
        P(("row", "exp"), None, "col"),
        P(("row", "exp"), None, "col"),
        P(("row", "exp"), "col"),
    )
    return jax.shard_map(
        per_device,
        mesh=mesh,
        in_specs=placed,
        out_specs=(
            P(("row", "exp"), "col"),
            P(("row", "exp"), "col"),
            P(),
            P("col", "row"),
            P("col", "row", None),
            P(),
            P(None, ("row", "col")),
            P("row", "col"),
            P(),
            P("col", "row"),
            P("col", "row"),
            P("row", "col"),
            P(),
            P(("row", "exp"), None, "col"),
            P(("row", "exp"), None, "col"),
            P(("row", "exp"), None, "col"),
        ),
        check_vma=False,
    )
```

```python
import functools
import math

import jax
import jax.numpy as jnp
from jax import lax
from jax.experimental import pallas as pl
from jax.experimental.pallas import tpu as pltpu
from jax.sharding import PartitionSpec as P

QK_NOPE = 128
ROPE = 64
KV_RANK = 512
V_DIM = 128

epsilon = 1e-06
theta_base = 10000.0
SWAP = [(0, 1), (1, 0)]


MESH = pl.DeviceIdType.MESH


class Place:
    def __init__(self, layers):
        self.layers = layers
        self.row, self.col = lax.axis_index("row"), lax.axis_index("col")
        self.layer = lax.axis_index("exp") if layers > 1 else 0
        self.core = lax.rem(self.row, 2)
        self.x_row = lax.rem(self.row + 2, 4)
        self.core_row = self.row + 1 - 2 * self.core
        self.y_col = 1 - self.col
        self.to_x = {"row": self.x_row}
        self.to_y = {"col": self.y_col}
        self.to_core = {"row": self.core_row}
        self.above = {"exp": self.layer + 1}
        self.below = {"exp": self.layer - 1}

    def greet(self):
        barrier = pltpu.get_barrier_semaphore()
        for target in (self.to_x, self.to_y, self.to_core):
            pl.semaphore_signal(barrier, inc=1, device_id=target, device_id_type=MESH)
        if self.layers > 1:

            @pl.when(self.layer > 0)
            def _():
                pl.semaphore_signal(barrier, inc=1, device_id=self.below, device_id_type=MESH)

            @pl.when(self.layer < self.layers - 1)
            def _():
                pl.semaphore_signal(barrier, inc=1, device_id=self.above, device_id_type=MESH)

        peers = 3
        if self.layers > 1:
            peers = peers + jnp.where(self.layer > 0, 1, 0) + jnp.where(self.layer < self.layers - 1, 1, 0)
        pl.semaphore_wait(barrier, peers)


def remote(src, dst, send, recv, target):
    return pltpu.make_async_remote_copy(
        src_ref=src, dst_ref=dst, send_sem=send, recv_sem=recv, device_id=target, device_id_type=MESH
    )


def first_part(rows):
    return (rows // 2 + 15) // 16 * 16


def piece_of(where, layers, shape, by_rows, row, col, layer, span=None):
    rows, width = shape
    start, size = (0, rows) if span is None else span
    if by_rows:
        first = pl.multiple_of((row * 2 + col) * rows + start, 16)
        return where.at[pl.ds(first, size)]
    first = pl.multiple_of((row * layers + layer) * rows + start, 16)
    return where.at[pl.ds(first, size), pl.ds(pl.multiple_of(col * width, 128), width)]


class Gather:
    def __init__(self, me, layers, by_rows, shape, held, sems):
        self.me, self.layers, self.by_rows, self.shape, self.held = me, layers, by_rows, shape, held
        self.up_send, self.down_send, self.z_recv = sems[:3]
        self.send, self.recv, self.diag_send, self.diag_recv = sems[3:]
        part = first_part(shape[0])
        self.spans = ((0, part), (part, shape[0] - part))
        self.owners = (
            (me.row, me.col),
            (me.x_row, me.col),
            (me.row, me.y_col),
            (me.x_row, me.y_col),
        )
        self.sides = (me.to_x, me.to_y)

    @staticmethod
    def semaphores(layers):
        dma = pltpu.SemaphoreType.DMA
        line = [dma((layers,)) for _ in range(3)]
        return [*line, dma((5, 4, layers)), dma((5, 4, layers)), dma((2, layers)), dma((2, layers))]

    def area(self, where, row, col, layer, span=None):
        return piece_of(where, self.layers, self.shape, self.by_rows, row, col, layer, span)

    def piece(self, kind, layer, span=None):
        return self.area(self.held, *self.owners[kind], layer, span)

    def partner_piece(self, where, kind, layer):
        row, col = self.owners[kind]
        return self.area(where, row + 1 - 2 * self.me.core, col, layer)

    def to_core(self, kind, layer):
        piece = self.piece(kind, layer)
        sems = (4, kind, layer)
        return remote(piece, piece, self.send.at[sems], self.recv.at[sems], self.me.to_core)

    def from_core(self, kind, layer):
        piece = self.partner_piece(self.held, kind, layer)
        sems = (4, kind, layer)
        return remote(piece, piece, self.send.at[sems], self.recv.at[sems], self.me.to_core)

    def beside(self, axis, half, layer, incoming=False):
        piece = self.piece(axis + 1 if incoming else 0, layer, self.spans[half])
        sems = (2 * axis + half, 0, layer)
        return remote(piece, piece, self.send.at[sems], self.recv.at[sems], self.sides[axis])

    def corner(self, axis, layer, incoming=False):
        piece = self.piece(3 if incoming else axis + 1, layer, self.spans[axis])
        sems = (axis, layer)
        return remote(
            piece, piece, self.diag_send.at[sems], self.diag_recv.at[sems], self.sides[1 - axis]
        )

    def along(self, up, layer):
        piece = self.piece(0, layer)
        return remote(
            piece,
            piece,
            (self.up_send if up else self.down_send).at[layer],
            self.z_recv.at[layer],
            self.me.above if up else self.me.below,
        )

    def pass_on(self, up, layer):
        me = self.me

        @pl.when((me.layer < self.layers - 1) if up else (me.layer > 0))
        def _():
            self.along(up, layer).start()

    def spread(self, layer):
        self.beside(0, 0, layer).start()
        self.beside(1, 1, layer).start()
        self.beside(0, 1, layer).start()
        self.beside(1, 0, layer).start()
        self.to_core(0, layer).start()

    def begin(self):
        if self.layers > 1:
            self.pass_on(True, self.me.layer)
            self.pass_on(False, self.me.layer)
        self.spread(self.me.layer)

    def at_distance(self, distance, act):
        me = self.me
        if distance == 0:
            act(me.layer, None)
            return

        @pl.when(me.layer >= distance)
        def _():
            act(me.layer - distance, True)

        @pl.when(me.layer + distance < self.layers)
        def _():
            act(me.layer + distance, False)

    def arrived(self, layer, upward):
        self.along(upward, layer).wait_recv()
        self.pass_on(upward, layer)
        self.spread(layer)

    def second(self, layer):
        for axis in (0, 1):
            self.beside(axis, axis, layer, True).wait_recv()
            self.corner(axis, layer).start()
        for axis in (0, 1):
            self.beside(axis, 1 - axis, layer, True).wait_recv()
            self.to_core(axis + 1, layer).start()

    def third(self, layer):
        for axis in (0, 1):
            self.corner(axis, layer, True).wait_recv()
        self.to_core(3, layer).start()

    def finish(self):
        me, layers = self.me, self.layers
        for layer in range(layers):
            for kind in range(4):
                self.to_core(kind, layer).wait_send()
            for axis in (0, 1):
                for half in (0, 1):
                    self.beside(axis, half, layer).wait_send()
                self.corner(axis, layer).wait_send()
        if layers > 1:
            for layer in range(layers):

                @pl.when((me.layer < layers - 1) & (layer <= me.layer))
                def _():
                    self.along(True, layer).wait_send()

                @pl.when((me.layer > 0) & (layer >= me.layer))
                def _():
                    self.along(False, layer).wait_send()


def gather_body(layers, by_rows, src, out, held, store_sem, *sems):
    me = Place(layers)
    work = Gather(me, layers, by_rows, src.shape, held, sems)

    def store(kind, layer, partner):
        if partner:
            pair = (work.partner_piece(held, kind, layer), work.partner_piece(out, kind, layer))
        else:
            pair = (work.piece(kind, layer), work.area(out, *work.owners[kind], layer))
        return pltpu.make_async_copy(*pair, store_sem.at[1 if partner else 0, kind, layer])

    own = pltpu.make_async_copy(src, work.piece(0, me.layer), store_sem.at[0, 0, me.layer])
    own.start()
    me.greet()
    own.wait()
    work.begin()
    store(0, me.layer, False).start()

    def arrived(layer, upward):
        work.arrived(layer, upward)
        store(0, layer, False).start()

    def second(layer, upward):
        work.second(layer)
        for kind in (1, 2):
            store(kind, layer, False).start()

    def third(layer, upward):
        work.third(layer)
        store(3, layer, False).start()
        for kind in range(4):
            work.from_core(kind, layer).wait_recv()
            store(kind, layer, True).start()

    for step in range(1, layers + 2):
        if step < layers:
            work.at_distance(step, arrived)
        if step - 1 < layers:
            work.at_distance(step - 1, second)
        if 0 <= step - 2 < layers:
            work.at_distance(step - 2, third)
    for layer in range(layers):
        for kind in range(4):
            store(kind, layer, False).wait()
            store(kind, layer, True).wait()
    work.finish()


def gather(value, layers, collective_id, by_rows=False):
    rows, width = value.shape
    dma = pltpu.SemaphoreType.DMA
    whole = (8 * rows, width) if by_rows else (4 * layers * rows, 2 * width)
    return pl.pallas_call(
        functools.partial(gather_body, layers, by_rows),
        out_shape=jax.ShapeDtypeStruct(whole, value.dtype),
        in_specs=[pl.BlockSpec(memory_space=pl.ANY)],
        out_specs=pl.BlockSpec(memory_space=pl.ANY),
        scratch_shapes=[
            pltpu.VMEM(whole, value.dtype),
            dma((2, 4, layers)),
            *Gather.semaphores(layers),
        ],
        compiler_params=pltpu.CompilerParams(
            collective_id=collective_id,
            has_side_effects=True,
            vmem_limit_bytes=56 * 1024 * 1024,
        ),
    )(value)


def scatter_body(
    layers,
    by_rows,
    src,
    out,
    acc,
    core_in,
    diag_a,
    diag_b,
    side_in,
    line_in,
    load_sem,
    core_send,
    core_recv,
    diag_send,
    diag_recv,
    side_send,
    side_recv,
    line_send,
    line_recv,
):
    me = Place(layers)
    rows, width = out.shape
    part = first_part(rows)
    owners = (
        (me.row, me.col),
        (me.x_row, me.col),
        (me.row, me.y_col),
        (me.x_row, me.y_col),
    )

    def layer_at(step):
        if layers == 1:
            return 0
        found = 0
        for layer in range(layers):
            order = sorted(range(layers), key=lambda other: (-abs(other - layer), -other))
            found = found + jnp.where(me.layer == layer, order[step], 0)
        return found

    layer_of = [layer_at(step) for step in range(layers)]

    def area(row, col, layer):
        return piece_of(src, layers, (rows, width), by_rows, row, col, layer)

    def load(step, kind):
        return pltpu.make_async_copy(
            area(*owners[kind], layer_of[step]), acc.at[step, kind], load_sem.at[step, kind]
        )

    def to_core(step, kind):
        row, col = owners[kind]
        return remote(
            area(row + 1 - 2 * me.core, col, layer_of[step]),
            core_in.at[step, kind],
            core_send.at[step, kind],
            core_recv.at[step, kind],
            me.to_core,
        )

    def diag(step, axis):
        start, size = ((0, part), (part, rows - part))[axis]
        return remote(
            acc.at[step, 3, pl.ds(start, size)],
            (diag_a, diag_b)[axis].at[step],
            diag_send.at[axis, step],
            diag_recv.at[axis, step],
            (me.to_y, me.to_x)[axis],
        )

    def side(step, axis):
        return remote(
            acc.at[step, axis + 1],
            side_in.at[axis, step],
            side_send.at[axis, step],
            side_recv.at[axis, step],
            (me.to_x, me.to_y)[axis],
        )

    def line(step, up):
        layer = layer_of[step]
        way = 0 if up else 1
        return remote(
            acc.at[step, 0],
            line_in.at[way, layer],
            line_send.at[step],
            line_recv.at[way, layer],
            me.above if up else me.below,
        )

    lanes = 32 if part % 32 == 0 and rows % 32 == 0 else 16

    def add(target, others, start=0, size=rows, into=None):
        def step(i, carry):
            first = pl.multiple_of(i * lanes, 16)
            total = target[pl.ds(start + first, lanes), :].astype(jnp.float32)
            for other in others:
                total = total + other[pl.ds(first, lanes), :].astype(jnp.float32)
            if into is None:
                target[pl.ds(start + first, lanes), :] = total.astype(target.dtype)
            else:
                into[pl.ds(first, lanes), :] = total.astype(into.dtype)
            return carry

        lax.fori_loop(0, size // lanes, step, 0)

    me.greet()
    kinds = (3, 1, 2, 0)
    for step in range(layers):
        for kind in kinds:
            to_core(step, kind).start()
            load(step, kind).start()

    def ready(step, kind):
        load(step, kind).wait()
        to_core(step, kind).wait_recv()

    def stage_a(step):
        ready(step, 3)
        add(acc.at[step, 3], [core_in.at[step, 3]])
        diag(step, 0).start()
        diag(step, 1).start()

    def stage_b(step):
        for axis, buffer, start, size in (
            (0, diag_a, 0, part),
            (1, diag_b, part, rows - part),
        ):
            kind = axis + 1
            ready(step, kind)
            add(acc.at[step, kind], [core_in.at[step, kind]])
            diag(step, axis).wait_recv()
            add(acc.at[step, kind], [buffer.at[step]], start, size)
            side(step, axis).start()

    def stage_c(step):
        ready(step, 0)
        side(step, 0).wait_recv()
        side(step, 1).wait_recv()
        parts = [core_in.at[step, 0], side_in.at[0, step], side_in.at[1, step]]
        if layers == 1:
            add(acc.at[step, 0], parts, into=out)
            return
        add(acc.at[step, 0], parts)
        layer = layer_of[step]
        if step < layers - 1:

            @pl.when((layer > me.layer) & (me.layer > 0))
            def _():
                line(step, True).wait_recv()
                add(acc.at[step, 0], [line_in.at[0, layer]])

            @pl.when((layer < me.layer) & (me.layer < layers - 1))
            def _():
                line(step, False).wait_recv()
                add(acc.at[step, 0], [line_in.at[1, layer]])

            @pl.when(layer > me.layer)
            def _():
                line(step, True).start()

            @pl.when(layer < me.layer)
            def _():
                line(step, False).start()
        else:
            inner = (me.layer > 0) & (me.layer < layers - 1)

            @pl.when(me.layer > 0)
            def _():
                line(step, True).wait_recv()

            @pl.when(me.layer < layers - 1)
            def _():
                line(step, False).wait_recv()

            @pl.when(inner)
            def _():
                add(acc.at[step, 0], [line_in.at[0, layer], line_in.at[1, layer]], into=out)

            @pl.when(me.layer == 0)
            def _():
                add(acc.at[step, 0], [line_in.at[1, layer]], into=out)

            @pl.when(me.layer == layers - 1)
            def _():
                add(acc.at[step, 0], [line_in.at[0, layer]], into=out)

    for step in range(layers + 2):
        if step < layers:
            stage_a(step)
        if 0 <= step - 1 < layers:
            stage_b(step - 1)
        if 0 <= step - 2 < layers:
            stage_c(step - 2)
    for step in range(layers):
        for kind in kinds:
            to_core(step, kind).wait_send()
        for axis in (0, 1):
            diag(step, axis).wait_send()
            side(step, axis).wait_send()
        if step < layers - 1:

            @pl.when(layer_of[step] > me.layer)
            def _():
                line(step, True).wait_send()

            @pl.when(layer_of[step] < me.layer)
            def _():
                line(step, False).wait_send()


def scatter(value, layers, collective_id, by_rows=False):
    if by_rows:
        rows, width = value.shape[0] // 8, value.shape[1]
    else:
        rows, width = value.shape[0] // (4 * layers), value.shape[1] // 2
    part = first_part(rows)
    dma = pltpu.SemaphoreType.DMA
    buffer = lambda *lead: pltpu.VMEM((*lead, rows, width), value.dtype)
    return pl.pallas_call(
        functools.partial(scatter_body, layers, by_rows),
        out_shape=jax.ShapeDtypeStruct((rows, width), jnp.float32),
        in_specs=[pl.BlockSpec(memory_space=pl.ANY)],
        out_specs=pl.BlockSpec(memory_space=pltpu.VMEM),
        scratch_shapes=[
            buffer(layers, 4),
            buffer(layers, 4),
            pltpu.VMEM((layers, part, width), value.dtype),
            pltpu.VMEM((layers, rows - part, width), value.dtype),
            buffer(2, layers),
            buffer(2, layers),
            dma((layers, 4)),
            dma((layers, 4)),
            dma((layers, 4)),
            dma((2, layers)),
            dma((2, layers)),
            dma((2, layers)),
            dma((2, layers)),
            dma((layers,)),
            dma((2, layers)),
        ],
        compiler_params=pltpu.CompilerParams(
            collective_id=collective_id,
            has_side_effects=True,
            vmem_limit_bytes=56 * 1024 * 1024,
        ),
    )(value)


def dot_nn(left, right):
    return jnp.dot(left, right, preferred_element_type=jnp.float32)


def dot_nt(left, right):
    return lax.dot_general(
        left, right, (((1,), (1,)), ((), ())), preferred_element_type=jnp.float32
    )


def dot_tn(left, right):
    return lax.dot_general(
        left, right, (((0,), (0,)), ((), ())), preferred_element_type=jnp.float32
    )


def made_scatter_body(layers, parts, *refs):
    slots_hbm, refs = refs[:parts], refs[parts:]
    weights_hbm, refs = refs[:parts], refs[parts:]
    spread_hbm, side_hbm, side_w_hbm, out, refs = *refs[:4], refs[4:]
    slots_in, refs = refs[:parts], refs[parts:]
    weights, refs = refs[:parts], refs[parts:]
    spread_in, side_in, side_w, slot_rows, refs = *refs[:4], refs[4:]
    core_out, acc, core_in, diag_a, diag_b, beside_in, line_in, refs = *refs[:7], refs[7:]
    in_sem, weight_sem, core_send, core_recv, diag_send, diag_recv, side_send, side_recv = refs[:8]
    line_send, line_recv = refs[8:]
    me = Place(layers)
    rows, width = out.shape
    part = first_part(rows)
    f32 = jnp.float32
    per_block, few, slots = spread_in.shape[2:]
    x_mine = me.row // 2

    def layer_at(step):
        return nearest_first(layers, layers - 1 - step, me.layer)

    def loads(unit):
        step, own = unit // 2, lax.rem(unit, 2)
        core = me.core * own + (1 - me.core) * (1 - own)
        slot = lax.rem(unit, 2)
        layer = layer_at(step)
        pairs = [*zip(slots_hbm, slots_in), (spread_hbm, spread_in), (side_hbm, side_in)]
        return [
            pltpu.make_async_copy(
                src.at[x_mine if x == 0 else 1 - x_mine, core, layer],
                dst.at[slot, x],
                in_sem.at[slot, i, x],
            )
            for i, (src, dst) in enumerate(pairs)
            for x in range(2)
        ]

    def weight_loads():
        pairs = [*zip(weights_hbm, weights), (side_w_hbm, side_w)]
        copies = []
        for i, (src, dst) in enumerate(pairs):
            for at, col in enumerate((me.col, me.y_col)):
                copies.append(
                    pltpu.make_async_copy(
                        src.at[:, pl.ds(pl.multiple_of(col * width, 128), width)],
                        dst.at[:, pl.ds(at * width, width)],
                        weight_sem.at[i, at],
                    )
                )
        return copies

    def make(unit, put):
        for copy in loads(unit):
            copy.wait()

        @pl.when(unit + 1 < 2 * layers)
        def _():
            for copy in loads(unit + 1):
                copy.start()

        slot = lax.rem(unit, 2)
        total = sum(
            dot_nn(value[slot].reshape(-1, value.shape[-1]), weight[...])
            for value, weight in zip(slots_in, weights)
        )
        slot_rows[...] = total.astype(slot_rows.dtype)
        for x in range(2):
            for j in range(per_block):
                there = pl.ds(j * few, few)
                here = pl.ds((x * per_block + j) * slots, slots)
                made = dot_nn(spread_in[slot, x, j], slot_rows[here, :]) + dot_nn(
                    side_in[slot, x, there, :], side_w[...]
                )
                put(x, there, made[:, :width].astype(acc.dtype))
                put(x + 2, there, made[:, width:].astype(acc.dtype))

    def to_core(step, kind):
        return remote(
            core_out.at[lax.rem(step, 2), kind],
            core_in.at[step, kind],
            core_send.at[step, kind],
            core_recv.at[step, kind],
            me.to_core,
        )

    def diag(step, axis):
        start, size = ((0, part), (part, rows - part))[axis]
        return remote(
            acc.at[step, 3, pl.ds(start, size)],
            (diag_a, diag_b)[axis].at[step],
            diag_send.at[axis, step],
            diag_recv.at[axis, step],
            (me.to_y, me.to_x)[axis],
        )

    def side(step, axis):
        return remote(
            acc.at[step, axis + 1],
            beside_in.at[axis, step],
            side_send.at[axis, step],
            side_recv.at[axis, step],
            (me.to_x, me.to_y)[axis],
        )

    def line(step, up):
        layer = layer_at(step)
        way = 0 if up else 1
        return remote(
            acc.at[step, 0],
            line_in.at[way, layer],
            line_send.at[step],
            line_recv.at[way, layer],
            me.above if up else me.below,
        )

    lanes = 32 if part % 32 == 0 and rows % 32 == 0 else 16

    def add(target, others, start=0, size=rows, into=None):
        def step(i, carry):
            first = pl.multiple_of(i * lanes, 16)
            total = target[pl.ds(start + first, lanes), :].astype(f32)
            for other in others:
                total = total + other[pl.ds(first, lanes), :].astype(f32)
            if into is None:
                target[pl.ds(start + first, lanes), :] = total.astype(target.dtype)
            else:
                into[pl.ds(first, lanes), :] = total.astype(into.dtype)
            return carry

        lax.fori_loop(0, size // lanes, step, 0)

    for copy in (*weight_loads(), *loads(0)):
        copy.start()
    me.greet()
    for copy in weight_loads():
        copy.wait()

    def produce(step):
        @pl.when(step >= 2)
        def _():
            for kind in range(4):
                to_core(step - 2, kind).wait_send()

        half = lax.rem(step, 2)

        def to_other(kind, there, value):
            core_out[half, kind, there, :] = value

        make(2 * step, to_other)
        for kind in (3, 1, 2, 0):
            to_core(step, kind).start()

        def to_own(kind, there, value):
            acc[step, kind, there, :] = value

        make(2 * step + 1, to_own)

    def stage_a(step):
        to_core(step, 3).wait_recv()
        add(acc.at[step, 3], [core_in.at[step, 3]])
        diag(step, 0).start()
        diag(step, 1).start()

    def stage_b(step):
        for axis, buffer, start, size in (
            (0, diag_a, 0, part),
            (1, diag_b, part, rows - part),
        ):
            kind = axis + 1
            to_core(step, kind).wait_recv()
            add(acc.at[step, kind], [core_in.at[step, kind]])
            diag(step, axis).wait_recv()
            add(acc.at[step, kind], [buffer.at[step]], start, size)
            side(step, axis).start()

    def stage_c(step):
        to_core(step, 0).wait_recv()
        side(step, 0).wait_recv()
        side(step, 1).wait_recv()
        add(acc.at[step, 0], [core_in.at[step, 0], beside_in.at[0, step], beside_in.at[1, step]])
        layer = layer_at(step)

        @pl.when((layer > me.layer) & (me.layer > 0))
        def _():
            line(step, True).wait_recv()
            add(acc.at[step, 0], [line_in.at[0, layer]])

        @pl.when((layer < me.layer) & (me.layer < layers - 1))
        def _():
            line(step, False).wait_recv()
            add(acc.at[step, 0], [line_in.at[1, layer]])

        @pl.when(layer > me.layer)
        def _():
            line(step, True).start()

        @pl.when(layer < me.layer)
        def _():
            line(step, False).start()

    def stages(step, carry):
        @pl.when(step < layers)
        def _():
            produce(step)
            stage_a(step)

        @pl.when((step >= 1) & (step <= layers))
        def _():
            stage_b(step - 1)

        @pl.when(step >= 2)
        def _():
            stage_c(step - 2)

        return carry

    lax.fori_loop(0, layers + 2, stages, 0)
    last = layers - 1

    @pl.when(me.layer > 0)
    def _():
        line(last, True).wait_recv()

    @pl.when(me.layer < last)
    def _():
        line(last, False).wait_recv()

    @pl.when((me.layer > 0) & (me.layer < last))
    def _():
        add(acc.at[last, 0], [line_in.at[0, me.layer], line_in.at[1, me.layer]], into=out)

    @pl.when(me.layer == 0)
    def _():
        add(acc.at[last, 0], [line_in.at[1, me.layer]], into=out)

    @pl.when(me.layer == last)
    def _():
        add(acc.at[last, 0], [line_in.at[0, me.layer]], into=out)

    for step in range(layers):
        if step >= layers - 2:
            for kind in range(4):
                to_core(step, kind).wait_send()
        for axis in (0, 1):
            diag(step, axis).wait_send()
            side(step, axis).wait_send()
        if step < last:

            @pl.when(layer_at(step) > me.layer)
            def _():
                line(step, True).wait_send()

            @pl.when(layer_at(step) < me.layer)
            def _():
                line(step, False).wait_send()


def made_scatter(slots_in, weights, spread, side, side_w, layers, collective_id):
    block, width = side.shape[3], side_w.shape[1] // 2
    bf16 = jnp.bfloat16
    parts = len(weights)
    part = first_part(block)
    dma = pltpu.SemaphoreType.DMA
    buffer = lambda *lead: pltpu.VMEM((*lead, block, width), bf16)
    ahead = lambda value: pltpu.VMEM((2, 2, *value.shape[3:]), bf16)
    in_hbm = pl.BlockSpec(memory_space=pl.ANY)
    return pl.pallas_call(
        functools.partial(made_scatter_body, layers, parts),
        out_shape=jax.ShapeDtypeStruct((block, width), jnp.float32),
        in_specs=[in_hbm] * (2 * parts + 3),
        out_specs=pl.BlockSpec(memory_space=pltpu.VMEM),
        scratch_shapes=[
            *(ahead(value) for value in slots_in),
            *(pltpu.VMEM(value.shape, bf16) for value in weights),
            ahead(spread),
            ahead(side),
            pltpu.VMEM(side_w.shape, bf16),
            pltpu.VMEM((2 * slots_in[0].shape[3], 2 * width), bf16),
            buffer(2, 4),
            buffer(layers, 4),
            buffer(layers, 4),
            pltpu.VMEM((layers, part, width), bf16),
            pltpu.VMEM((layers, block - part, width), bf16),
            buffer(2, layers),
            buffer(2, layers),
            dma((2, parts + 2, 2)),
            dma((parts + 1, 2)),
            dma((layers, 4)),
            dma((layers, 4)),
            dma((2, layers)),
            dma((2, layers)),
            dma((2, layers)),
            dma((2, layers)),
            dma((layers,)),
            dma((2, layers)),
        ],
        compiler_params=pltpu.CompilerParams(
            collective_id=collective_id,
            has_side_effects=True,
            vmem_limit_bytes=62 * 1024 * 1024,
        ),
    )(*slots_in, *weights, spread, side, side_w)


def small_sum_body(layers, src, out, core_in, mid, x_in, near, line_in, total, send, recv, line_send, line_recv):
    me = Place(layers)
    width = src.shape[1]
    barrier = pltpu.get_barrier_semaphore()
    for target in (me.to_x, me.to_y, me.to_core):
        pl.semaphore_signal(barrier, inc=1, device_id=target, device_id_type=MESH)
    for step in range(1, layers):
        other = {"exp": lax.rem(me.layer + step, layers)}
        pl.semaphore_signal(barrier, inc=1, device_id=other, device_id_type=MESH)
    pl.semaphore_wait(barrier, 3 + layers - 1)
    swap = remote(src, core_in, send.at[0], recv.at[0], me.to_core)
    swap.start()
    swap.wait()
    mid[...] = src[...] + core_in[...]
    swap = remote(mid, x_in, send.at[1], recv.at[1], me.to_x)
    swap.start()
    swap.wait()
    near[...] = mid[...] + x_in[...]
    line_in[me.layer] = near[...]

    def along(step, incoming):
        layer = lax.rem(me.layer + (layers - step if incoming else 0), layers)
        return remote(
            near,
            line_in.at[layer],
            line_send.at[step],
            line_recv.at[step],
            {"exp": lax.rem(me.layer + step, layers)},
        )

    for step in range(1, layers):
        along(step, False).start()
    for step in range(1, layers):
        along(step, True).wait_recv()
    summed = line_in[0]
    for layer in range(1, layers):
        summed = summed + line_in[layer]
    total[...] = summed
    mine = pl.ds(pl.multiple_of(me.col * width, 128), width)
    theirs = pl.ds(pl.multiple_of(me.y_col * width, 128), width)
    out[:, mine] = summed
    remote(total, out.at[:, mine], send.at[2], recv.at[2], me.to_y).start()
    remote(total, out.at[:, theirs], send.at[2], recv.at[2], me.to_y).wait()
    for step in range(1, layers):
        along(step, False).wait_send()


def small_sum(value, layers, collective_id):
    rows, width = value.shape
    dma = pltpu.SemaphoreType.DMA
    buffer = lambda *lead: pltpu.VMEM((*lead, rows, width), value.dtype)
    in_vmem = pl.BlockSpec(memory_space=pltpu.VMEM)
    return pl.pallas_call(
        functools.partial(small_sum_body, layers),
        out_shape=jax.ShapeDtypeStruct((rows, 2 * width), value.dtype),
        in_specs=[in_vmem],
        out_specs=in_vmem,
        scratch_shapes=[
            buffer(),
            buffer(),
            buffer(),
            buffer(),
            buffer(layers),
            buffer(),
            dma((3,)),
            dma((3,)),
            dma((layers,)),
            dma((layers,)),
        ],
        compiler_params=pltpu.CompilerParams(
            collective_id=collective_id,
            has_side_effects=True,
            vmem_limit_bytes=32 * 1024 * 1024,
        ),
    )(value)


def nearest_first(layers, turn, layer):
    found = 0
    for here in range(layers):
        order = sorted(range(layers), key=lambda other: (abs(other - here), other))
        for at in range(layers):
            found = found + jnp.where((layer == here) & (turn == at), order[at], 0)
    return found


def expert_body(
    layers,
    units,
    experts,
    src,
    grads_ref,
    pick_ref,
    spread_ref,
    words_ref,
    gate_hbm,
    up_hbm,
    down_hbm,
    side_hbm,
    side_down_hbm,
    rows_all,
    slot_rows_ref,
    slot_grads_ref,
    hidden_ref,
    d_gate_ref,
    d_up_ref,
    d_gates_ref,
    side_hidden_ref,
    d_side_ref,
    grad_side_ref,
    grad_side_down_ref,
    gate_w,
    up_w,
    down_w,
    side_w,
    side_down,
    both_rows,
    side_hidden,
    d_side,
    weight_sem,
    rows_sem,
    *sems,
):
    bf16, f32 = jnp.bfloat16, jnp.float32
    me = Place(layers)
    work = Gather(me, layers, False, src.shape, rows_all, sems)
    own_expert = me.row * layers + me.layer
    block, half = src.shape
    width = 2 * half
    few, slots = pick_ref.shape[5], pick_ref.shape[4]
    per_block = block // few
    count = 2 * per_block
    lanes = side_down.shape[0]
    step = pl.program_id(0)
    steps = 2 * layers
    weight_loads = [
        pltpu.make_async_copy(src_ref, dst_ref, weight_sem.at[i])
        for i, (src_ref, dst_ref) in enumerate(
            (
                (down_hbm, down_w),
                (side_down_hbm, side_down),
                (side_hbm, side_w),
                (gate_hbm, gate_w),
                (up_hbm, up_w),
            )
        )
    ]

    def load(which, core):
        layer = nearest_first(layers, which // 2, me.layer)
        far = lax.rem(which, 2)
        x_place = me.row // 2 * (1 - far) + (1 - me.row // 2) * far
        first = pl.multiple_of(((2 * x_place + core) * layers + layer) * block, 16)
        slot = lax.rem(which, 2)
        return pltpu.make_async_copy(
            rows_all.at[pl.ds(first, block)],
            both_rows.at[slot, pl.ds(core * block, block)],
            rows_sem.at[slot, core],
        )

    def prepare(which):
        for distance in range(1, layers):

            @pl.when(which == distance - 1)
            def _():
                work.at_distance(distance, work.arrived)

        for turn in range(layers):
            at = nearest_first(layers, turn, me.layer)
            if turn > 0:

                @pl.when(which == 2 * turn - 1)
                def _():
                    work.second(at)

            @pl.when(which == max(1, 2 * turn))
            def _():
                work.third(at)

        layer = nearest_first(layers, which // 2, me.layer)

        @pl.when(lax.rem(which, 2) == 0)
        def _():
            work.from_core(0, layer).wait_recv()
            work.from_core(2, layer).wait_recv()

        @pl.when(lax.rem(which, 2) == 1)
        def _():
            work.from_core(1, layer).wait_recv()
            work.from_core(3, layer).wait_recv()

        for core in range(2):
            load(which, core).start()

    @pl.when(step == 0)
    def _():
        own = pltpu.make_async_copy(src, work.piece(0, me.layer), rows_sem.at[0, 0])
        own.start()
        for copy in weight_loads:
            copy.start()
        me.greet()
        own.wait()
        work.begin()
        for copy in weight_loads:
            copy.wait()
        work.second(me.layer)
        prepare(step)

    rows = both_rows.at[lax.rem(step, 2)]

    def spot(b):
        core, j = b // per_block, b % per_block
        return core, j, pl.ds(b * few, few), pl.ds(j * slots, slots)

    for b in range(count):
        core, j, _, here = spot(b)
        for c in range(2):
            slot_grads_ref[0, core, 0, here, c * half : (c + 1) * half] = dot_nn(
                pick_ref[0, core, 0, j], grads_ref[0, core, 0, c, j * few : (j + 1) * few, :]
            ).astype(bf16)
    join = lambda ref: jnp.concatenate([ref[0, core, 0] for core in range(2)], axis=0)
    d_raw = dot_nt(join(slot_grads_ref), down_w[...])
    side_grads = [
        jnp.concatenate([grads_ref[0, core, 0, c] for core in range(2)], axis=0) for c in range(2)
    ]
    d_side_hidden = sum(
        dot_nt(side_grads[c], side_down[:, c * half : (c + 1) * half]) for c in range(2)
    )
    for core in range(2):
        load(step, core).wait()

    side = dot_nt(rows[...], side_w[...])
    side_gate, side_up = side[:, :lanes], side[:, lanes:]
    lane = lax.broadcasted_iota(jnp.int32, side_gate.shape, 1)
    expert = lane - units
    is_expert = (expert >= 0) & (expert < experts)
    highest = jnp.max(jnp.where(is_expert, side_gate, -jnp.inf), axis=1, keepdims=True)
    words = join(words_ref)
    word = words[:, 0:1]
    for i in range(1, words.shape[1]):
        word = jnp.where(expert >= 16 * i, words[:, i : i + 1], word)
    picked = lax.shift_right_logical(
        jnp.broadcast_to(word, expert.shape), jnp.bitwise_and(expert, 15)
    )
    picked = is_expert & (jnp.bitwise_and(picked, 1) == 1)
    chosen = jnp.where(picked, jnp.exp(jnp.where(is_expert, side_gate - highest, 0.0)), 0.0)
    total = jnp.sum(chosen, axis=1, keepdims=True)
    own = jnp.sum(jnp.where(expert == own_expert, chosen, 0.0), axis=1, keepdims=True) / total

    def two_parts(value):
        high = value.astype(bf16).astype(f32)
        at = lax.broadcasted_iota(jnp.int32, (value.shape[0], lanes), 1)
        return jnp.where(at == 0, high, jnp.where(at == 1, value - high, 0.0)).astype(bf16)

    own_parts = two_parts(own)
    slot_gates = []
    for b in range(count):
        core, j, tokens, here = spot(b)
        pick = pick_ref[0, core, 0, j]
        slot_rows_ref[0, core, 0, here, :] = dot_nn(pick, rows[tokens, :]).astype(bf16)
        parts = dot_nn(pick, own_parts[b * few : (b + 1) * few])
        slot_gates.append(jnp.sum(parts, axis=1, keepdims=True))
    slot_gate = jnp.concatenate(slot_gates, axis=0)

    slot_rows = join(slot_rows_ref)
    gate_pre = dot_nt(slot_rows, gate_w[...])
    up_pre = dot_nt(slot_rows, up_w[...])
    sigmoid = 1.0 / (1.0 + jnp.exp(-gate_pre))
    silu = gate_pre * sigmoid
    hidden = (silu * up_pre).astype(bf16).astype(f32)
    d_gates = jnp.sum(d_raw * hidden, axis=1, keepdims=True)
    d_hidden = d_raw * slot_gate
    each = per_block * slots

    def keep(ref, value):
        for core in range(2):
            ref[0, core, 0] = value[core * each : (core + 1) * each]

    hidden = (hidden * slot_gate).astype(bf16)
    keep(hidden_ref, hidden)
    d_up = (d_hidden * silu).astype(bf16)
    keep(d_up_ref, d_up)
    d_gate = (d_hidden * up_pre * sigmoid * (1.0 + gate_pre * (1.0 - sigmoid))).astype(bf16)
    keep(d_gate_ref, d_gate)

    @pl.when(step + 1 < steps)
    def _():
        prepare(step + 1)

    side_sigmoid = 1.0 / (1.0 + jnp.exp(-side_gate))
    side_silu = side_gate * side_sigmoid
    side_hidden[...] = (side_silu * side_up).astype(bf16)
    d_side[:, lanes:] = (d_side_hidden * side_silu).astype(bf16)
    d_side[:, :lanes] = (
        d_side_hidden * side_up * side_sigmoid * (1.0 + side_gate * (1.0 - side_sigmoid))
    ).astype(bf16)

    @pl.when(step == 0)
    def _():
        grad_side_ref[...] = jnp.zeros_like(grad_side_ref)
        grad_side_down_ref[...] = jnp.zeros_like(grad_side_down_ref)

    grad_side_ref[...] += dot_tn(d_side[...], rows[...])
    for c in range(2):
        grad_side_down_ref[:, c * half : (c + 1) * half] += dot_tn(side_hidden[...], side_grads[c])

    d_gate_parts = two_parts(d_gates)
    for b in range(count):
        core, j, tokens, _ = spot(b)
        there = pl.ds(j * few, few)
        back = dot_nn(spread_ref[0, core, 0, j], d_gate_parts[b * slots : (b + 1) * slots])
        d_gates_ref[0, core, 0, there, :] = jnp.sum(back, axis=1, keepdims=True)
        side_hidden_ref[0, core, 0, there, :] = side_hidden[tokens, :]
        d_side_ref[0, core, 0, there, :] = d_side[tokens, :]

    @pl.when(step == steps - 1)
    def _():
        work.finish()


def expert_pass(layers, few, slots, units, experts, rows_own, grads, pick, spread, words, weights, side_w, side_down):
    block, half = rows_own.shape
    width = 2 * half
    hidden = weights[0].shape[0]
    per_block = block // few
    tokens = 4 * layers * block
    lanes = side_down.shape[0]

    def by_step(*tail):
        def place(step):
            row = lax.axis_index("row")
            layer = nearest_first(layers, step // 2, lax.axis_index("exp"))
            far = lax.rem(step, 2)
            x_place = row // 2 * (1 - far) + (1 - row // 2) * far
            return (x_place, 0, layer, *(0 for _ in tail))

        return pl.BlockSpec((1, 2, 1, *tail), place)

    shape = lambda *tail, kind=jnp.bfloat16: jax.ShapeDtypeStruct((2, 2, layers, *tail), kind)
    each = per_block * slots
    outs = pl.pallas_call(
        functools.partial(expert_body, layers, units, experts),
        grid=(2 * layers,),
        in_specs=[
            pl.BlockSpec(memory_space=pl.ANY),
            by_step(2, block, half),
            by_step(per_block, slots, few),
            by_step(per_block, few, slots),
            by_step(block, words.shape[1]),
            *[pl.BlockSpec(memory_space=pl.ANY)] * 5,
        ],
        out_specs=[
            pl.BlockSpec(memory_space=pl.ANY),
            by_step(each, width),
            by_step(each, width),
            by_step(each, hidden),
            by_step(each, hidden),
            by_step(each, hidden),
            by_step(block, 1),
            by_step(block, lanes),
            by_step(block, 2 * lanes),
            pl.BlockSpec((2 * lanes, width), lambda i: (0, 0)),
            pl.BlockSpec((lanes, width), lambda i: (0, 0)),
        ],
        out_shape=[
            jax.ShapeDtypeStruct((tokens, width), jnp.bfloat16),
            shape(each, width),
            shape(each, width),
            shape(each, hidden),
            shape(each, hidden),
            shape(each, hidden),
            shape(block, 1, kind=jnp.float32),
            shape(block, lanes),
            shape(block, 2 * lanes),
            jax.ShapeDtypeStruct((2 * lanes, width), jnp.float32),
            jax.ShapeDtypeStruct((lanes, width), jnp.float32),
        ],
        scratch_shapes=[
            *(pltpu.VMEM(w.shape, jnp.bfloat16) for w in (*weights, side_w, side_down)),
            pltpu.VMEM((2, 2 * block, width), jnp.bfloat16),
            pltpu.VMEM((2 * block, lanes), jnp.bfloat16),
            pltpu.VMEM((2 * block, 2 * lanes), jnp.bfloat16),
            pltpu.SemaphoreType.DMA((5,)),
            pltpu.SemaphoreType.DMA((2, 2)),
            *Gather.semaphores(layers),
        ],
        compiler_params=pltpu.CompilerParams(
            collective_id=3, has_side_effects=True, vmem_limit_bytes=62 * 1024 * 1024
        ),
    )(
        rows_own,
        grads.reshape(2, 2, layers, 2, block, half),
        pick.reshape(2, 2, layers, per_block, slots, few),
        spread.reshape(2, 2, layers, per_block, few, slots),
        words.reshape(2, 2, layers, block, -1),
        *weights,
        side_w,
        side_down,
    )
    return outs


def rotate(value, cosine, sine):
    half = value.shape[-1] // 2
    first, second = (value[..., :half], value[..., half:])
    return jnp.concatenate(
        [first * cosine - second * sine, first * sine + second * cosine], axis=-1
    )


def unrotate(value, cosine, sine):
    half = value.shape[-1] // 2
    first, second = (value[..., :half], value[..., half:])
    return jnp.concatenate(
        [first * cosine + second * sine, second * cosine - first * sine], axis=-1
    )


def sequence_layout(lengths_row, group):
    ends = jnp.cumsum(lengths_row)
    starts = ends - lengths_row
    index = jnp.arange(group, dtype=jnp.int32)
    seq_ids = jnp.sum((index[:, None] >= ends[None, :]).astype(jnp.int32), axis=1)
    member = seq_ids[:, None] == jnp.arange(lengths_row.shape[0], dtype=jnp.int32)[None, :]
    begins = jnp.sum(jnp.where(member, starts[None, :], 0), axis=1)
    return (seq_ids, index - begins)


def rotary_tables(places):
    half = ROPE // 2
    freqs = jnp.power(theta_base, -jnp.arange(half, dtype=jnp.float32) * (2.0 / ROPE))
    angle = places.astype(jnp.float32)[..., None] * freqs
    return (jnp.cos(angle), jnp.sin(angle))


def norm_back(value, factor, gain, grad, width):
    weighted = grad * gain
    inner = lax.psum(jnp.sum(weighted * value, axis=1), "col")
    d_value = (
        factor[:, None] * weighted - value * (factor * factor * factor * inner / width)[:, None]
    )
    d_gain = jnp.sum(grad * value * factor[:, None], axis=0)
    return (d_value, d_gain)


def masked_scores(query_block, keys, seq_ids, first, scale):
    size = query_block.shape[0]
    group = keys.shape[0]
    scored = (
        jnp.einsum("qhd,khd->hqk", query_block, keys, preferred_element_type=jnp.float32) * scale
    )
    query_index = first + jnp.arange(size, dtype=jnp.int32)
    key_index = jnp.arange(group, dtype=jnp.int32)
    allowed = (seq_ids[first : first + size][:, None] == seq_ids[None, :group]) & (
        key_index[None, :] <= query_index[:, None]
    )
    return jnp.where(allowed[None, :, :], scored, -1e30)


def own_slice(value, index, axis):
    size = value.shape[axis] // 2
    return lax.dynamic_slice_in_dim(value, index * size, size, axis)


def col_pair(mine, sent, axis):
    received = lax.ppermute(sent, "col", SWAP)
    first = lax.axis_index("col") == 0
    return jnp.where(
        first,
        jnp.concatenate([mine, received], axis=axis),
        jnp.concatenate([received, mine], axis=axis),
    )


def trade(value, split, join):
    col = lax.axis_index("col")
    return col_pair(own_slice(value, col, split), own_slice(value, 1 - col, split), join)


def routed_and_shared(
    tok_dev, capacity, layers, router, expert_weights, shared_own, normed_own, grads_own, words
):
    bf16 = jnp.bfloat16
    col_id = lax.axis_index("col")
    own_expert = lax.axis_index("row") * layers + lax.axis_index("exp")
    experts = router.shape[1]
    units = shared_own.shape[1]
    block, half_width = normed_own.shape
    tokens = words.shape[0]
    few = min(tok_dev, block)
    slots = -(-min(capacity, few) // 16) * 16
    blocks = tokens // few

    own_word = lax.dynamic_index_in_dim(words, own_expert // 16, 1, keepdims=False)
    own_pick = (jnp.bitwise_and(lax.shift_right_logical(own_word, own_expert % 16), 1) == 1).reshape(
        blocks, few
    )
    order = jnp.arange(few, dtype=jnp.int32)
    place = dot_nn(own_pick.astype(bf16), (order[:, None] < order[None, :]).astype(bf16)).astype(
        jnp.int32
    )
    places = jnp.arange(slots, dtype=jnp.int32)
    pick = ((place[:, None, :] == places[None, :, None]) & own_pick[:, None, :]).astype(bf16)
    spread = ((place[:, :, None] == places[None, None, :]) & own_pick[:, :, None]).astype(bf16)
    lanes = -(-(units + experts) // 128) * 128
    fill = lambda value, n: jnp.pad(value, ((0, n - value.shape[0]), (0, 0)))
    side_w = jnp.concatenate(
        [fill(jnp.concatenate([shared_own[0], router.T]), lanes), fill(shared_own[1], lanes)]
    )
    side_down = fill(shared_own[2], lanes)

    grads_all = lax.all_gather(grads_own, ("row", "exp", "col"), axis=0)
    grads_all = grads_all.reshape(experts, 2, block, half_width)
    (
        normed_all,
        slot_rows,
        slot_grads,
        hidden,
        d_gate,
        d_up,
        d_gates_all,
        side_hidden,
        d_side,
        grad_side,
        grad_side_down,
    ) = expert_pass(
        layers,
        few,
        slots,
        units,
        experts,
        normed_own,
        grads_all,
        pick,
        spread,
        words,
        expert_weights,
        side_w,
        side_down,
    )
    spread = spread.reshape(2, 2, layers, -1, few, slots)
    gate_weight, up_weight, down_weight = expert_weights
    d_normed = made_scatter(
        (d_gate, d_up), (gate_weight, up_weight), spread, d_side, side_w, layers, 4
    )
    out_parts = ((hidden,), (down_weight,), spread, side_hidden, side_down)
    flat = lambda value: value.reshape(-1, value.shape[-1])
    grad_gate = dot_tn(flat(d_gate), flat(slot_rows))
    grad_up = dot_tn(flat(d_up), flat(slot_rows))
    grad_down = dot_tn(flat(hidden), flat(slot_grads))
    grad_shared = jnp.stack(
        [grad_side[:units], grad_side[lanes : lanes + units], grad_side_down[:units]]
    )

    d_gates = lax.psum(
        lax.all_to_all(
            d_gates_all.reshape(experts, block), ("row", "exp"), split_axis=0, concat_axis=0, tiled=True
        ),
        "col",
    ).T
    own_probs = jax.nn.softmax(
        dot_nn(lax.dynamic_slice_in_dim(normed_all, own_expert * block, block, 0), router), axis=1
    )
    own_words = lax.dynamic_slice_in_dim(words, own_expert * block, block, 0)
    numbers = jnp.arange(experts, dtype=jnp.int32)
    picks = (
        jnp.bitwise_and(
            lax.shift_right_logical(own_words[:, numbers // 16], (numbers % 16)[None, :]), 1
        )
        == 1
    )
    selected = jnp.where(picks, own_probs, 0.0)
    own_total = jnp.sum(selected, axis=1, keepdims=True)
    own_gates = selected / own_total
    d_selected = (d_gates - jnp.sum(d_gates * own_gates, axis=1, keepdims=True)) / own_total
    d_router_probs = jnp.where(picks, d_selected, 0.0)
    d_logits = own_probs * (
        d_router_probs - jnp.sum(own_probs * d_router_probs, axis=1, keepdims=True)
    )
    router_half = lax.dynamic_slice_in_dim(router, col_id * half_width, half_width, 0)
    grad_router = lax.dot_general(
        normed_own.astype(jnp.float32),
        d_logits,
        (((0,), (0,)), ((), ())),
        precision=lax.Precision.HIGHEST,
        preferred_element_type=jnp.float32,
    )
    d_normed = d_normed + lax.dot_general(
        d_logits,
        router_half.astype(jnp.float32),
        (((1,), (1,)), ((), ())),
        precision=lax.Precision.HIGHEST,
        preferred_element_type=jnp.float32,
    )
    return (d_normed, out_parts, (grad_gate, grad_up, grad_down, grad_shared, grad_router))


def per_device(
    layer_input,
    lengths,
    routes,
    norm1_gain,
    w_query,
    w_latent,
    latent_gain,
    w_kv,
    w_out,
    norm2_gain,
    shared_gate,
    shared_up,
    shared_down,
    router,
    expert_gate,
    expert_up,
    expert_down,
    cotangent,
):
    row_id = lax.axis_index("row")
    col_id = lax.axis_index("col")
    exp_id = lax.axis_index("exp")
    rows_n, cols_n, exps_n = (lax.axis_size(name) for name in ("row", "col", "exp"))
    experts = rows_n * exps_n
    own_expert = row_id * exps_n + exp_id
    tok_dev = routes.shape[1]
    topk_count = routes.shape[2]
    capacity = max(2, 3 * tok_dev * topk_count // (2 * experts))
    slots = -(-capacity // 16) * 16
    block, half_width = layer_input.shape
    width = half_width * cols_n
    group = block * rows_n
    tokens = group * exps_n
    heads_here = w_kv.shape[1] // (QK_NOPE + V_DIM)
    head_dim = QK_NOPE + ROPE
    scale = 1.0 / math.sqrt(head_dim)
    query_rows = group // 2
    bf16 = jnp.bfloat16

    w_query_own = trade(w_query, 1, 0)
    w_latent_all = lax.all_gather(w_latent[0].T, ("col", "row"), axis=1, tiled=True)
    seq_ids, places = sequence_layout(lengths[0], group)
    cosine, sine = rotary_tables(places)

    group_input = gather(layer_input, 1, 1)
    group_input, w_out, shared_gate, shared_up, shared_down, cotangent = lax.optimization_barrier(
        (group_input, w_out, shared_gate, shared_up, shared_down, cotangent)
    )
    w_out_own = trade(w_out, 0, 1)
    units = shared_gate.shape[1] // (cols_n * exps_n)
    shared_parts = jnp.stack(
        [
            lax.dynamic_index_in_dim(
                part.reshape(cols_n, exps_n, units, half_width), exp_id, 1, keepdims=False
            )
            for part in (shared_gate.T, shared_up.T, shared_down)
        ]
    )
    shared_own = trade(shared_parts, 1, 3)[:, 0]

    group_input = group_input.astype(jnp.float32)
    factor_group = lax.rsqrt(jnp.mean(group_input * group_input, axis=1) + epsilon)
    normed_group = (group_input * factor_group[:, None] * norm1_gain).astype(bf16)
    query_pre = dot_nn(normed_group, w_query_own).reshape(group, heads_here, head_dim)
    queries = jnp.concatenate(
        [
            query_pre[..., :QK_NOPE],
            rotate(query_pre[..., QK_NOPE:], cosine[:, None, :], sine[:, None, :]),
        ],
        axis=2,
    ).astype(bf16)
    latent = dot_nt(normed_group, w_latent_all)
    compressed_raw = latent[:, :KV_RANK]
    kv_factor = lax.rsqrt(jnp.mean(compressed_raw * compressed_raw, axis=1) + epsilon)
    compressed = (compressed_raw * kv_factor[:, None] * latent_gain).astype(bf16)
    rotary_key = rotate(latent[:, KV_RANK:], cosine, sine).astype(bf16)
    key_value = (
        dot_nn(compressed, w_kv).astype(bf16).reshape(group, heads_here, QK_NOPE + V_DIM)
    )
    keys = jnp.concatenate(
        [
            key_value[..., :QK_NOPE],
            jnp.broadcast_to(rotary_key[:, None, :], (group, heads_here, ROPE)),
        ],
        axis=2,
    )
    values = key_value[..., QK_NOPE:]
    block_outputs = []
    block_totals = []
    for first in range(0, group, query_rows):
        last = first + query_rows
        scores = masked_scores(queries[first:last], keys[:last], seq_ids, first, scale)
        highest = jnp.max(scores, axis=2, keepdims=True)
        log_total = highest + jnp.log(jnp.sum(jnp.exp(scores - highest), axis=2, keepdims=True))
        probs_low = jnp.exp(scores - log_total).astype(bf16)
        block_outputs.append(
            jnp.einsum(
                "hqk,khd->qhd", probs_low, values[:last], preferred_element_type=jnp.float32
            ).astype(bf16)
        )
        block_totals.append(log_total)
    attended = jnp.concatenate(block_outputs, axis=0).reshape(group, heads_here * V_DIM)

    input_wide = layer_input.astype(jnp.float32)
    hidden_state = input_wide + scatter(dot_nn(attended, w_out_own).astype(bf16), 1, 2)
    words_n = -(-experts // 16)
    word_of = jnp.arange(words_n, dtype=jnp.int32)[:, None, None]
    bits = jnp.where(routes // 16 == word_of, jnp.left_shift(1, routes % 16), 0)
    bits = jnp.sum(bits, axis=2).astype(jnp.float32)
    padded = -(-tok_dev // 128) * 128
    bits = jnp.pad(bits, ((0, 0), (0, padded - tok_dev)))
    is_here = jnp.arange(experts, dtype=jnp.int32) == own_expert
    bits = jnp.where(is_here[:, None, None], bits[None], 0.0).reshape(experts * words_n, padded)
    bits, hidden_state = lax.optimization_barrier((bits, hidden_state))
    bits = small_sum(bits, exps_n, 8).reshape(experts, words_n, cols_n, padded)[..., :tok_dev]
    words_all = bits.astype(jnp.int32).transpose(0, 2, 3, 1).reshape(tokens, words_n)

    gain_two = lax.dynamic_slice_in_dim(norm2_gain, col_id * half_width, half_width)
    square = lax.psum(jnp.sum(hidden_state * hidden_state, axis=1), "col")
    factor_two = lax.rsqrt(square / width + epsilon)
    normed_two = (hidden_state * factor_two[:, None] * gain_two).astype(bf16)
    pieces = max(1, exps_n // 4)
    feed = functools.partial(
        routed_and_shared,
        tok_dev,
        capacity,
        exps_n,
        router,
        (expert_gate[0].T, expert_up[0].T, expert_down[0].T),
        shared_own,
    )
    if pieces == 1:
        d_normed, out_parts, weight_grads = feed(normed_two, cotangent, words_all)
    else:
        piece_rows = block // pieces

        def one_piece(total, items):
            d_rows, out_parts, grads = feed(*items)
            return (jax.tree.map(jnp.add, total, grads), (d_rows, made_scatter(*out_parts, exps_n, 9)))

        split = lambda value: value.reshape(pieces, piece_rows, half_width)
        word_pieces = words_all.reshape(experts, pieces, piece_rows, words_n)
        items = (
            split(normed_two),
            split(cotangent),
            word_pieces.transpose(1, 0, 2, 3).reshape(pieces, -1, words_n),
        )
        shapes = jax.eval_shape(lambda: feed(*(item[0] for item in items))[2])
        start = jax.tree.map(lambda leaf: jnp.zeros(leaf.shape, leaf.dtype), shapes)
        weight_grads, (d_normed, branch) = lax.scan(one_piece, start, items)
        d_normed, branch = (v.reshape(block, half_width) for v in (d_normed, branch))
    grad_gate, grad_up, grad_down, grad_shared, grad_router = weight_grads
    grad_shared = trade(grad_shared.astype(bf16)[:, None], 3, 1)
    d_normed, grad_shared = lax.optimization_barrier((d_normed, grad_shared))
    grad_shared = lax.all_gather(grad_shared, "exp", axis=2, tiled=False)
    d_norm_two, grad_gain_two = norm_back(hidden_state, factor_two, gain_two, d_normed, width)
    d_hidden_state = cotangent.astype(jnp.float32) + d_norm_two

    d_branch = gather(d_hidden_state.astype(bf16), 1, 1)
    grad_w_out = trade(dot_tn(attended, d_branch).astype(bf16), 1, 0)
    d_attended = dot_nt(d_branch, w_out_own).astype(bf16).reshape(group, heads_here, V_DIM)
    d_query_blocks = []
    d_keys = jnp.zeros((group, heads_here, head_dim), jnp.float32)
    d_values = jnp.zeros((group, heads_here, V_DIM), jnp.float32)
    for number, first in enumerate(range(0, group, query_rows)):
        last = first + query_rows
        query_block = queries[first:last]
        d_block = d_attended[first:last]
        scores = masked_scores(query_block, keys[:last], seq_ids, first, scale)
        probs = jnp.exp(scores - block_totals[number])
        d_probs = jnp.einsum(
            "qhd,khd->hqk", d_block, values[:last], preferred_element_type=jnp.float32
        )
        delta = jnp.sum(probs * d_probs, axis=2, keepdims=True)
        d_scores = (probs * (d_probs - delta)).astype(bf16)
        d_query_blocks.append(
            jnp.einsum("hqk,khd->qhd", d_scores, keys[:last], preferred_element_type=jnp.float32)
            * scale
        )
        d_keys = d_keys.at[:last].add(
            jnp.einsum("hqk,qhd->khd", d_scores, query_block, preferred_element_type=jnp.float32)
            * scale
        )
        d_values = d_values.at[:last].add(
            jnp.einsum(
                "hqk,qhd->khd", probs.astype(bf16), d_block, preferred_element_type=jnp.float32
            )
        )
    d_query = jnp.concatenate(d_query_blocks, axis=0)
    d_query_pre = (
        jnp.concatenate(
            [
                d_query[..., :QK_NOPE],
                unrotate(d_query[..., QK_NOPE:], cosine[:, None, :], sine[:, None, :]),
            ],
            axis=2,
        )
        .astype(bf16)
        .reshape(group, heads_here * head_dim)
    )
    d_key_value = (
        jnp.concatenate([d_keys[..., :QK_NOPE], d_values], axis=2)
        .astype(bf16)
        .reshape(group, heads_here * (QK_NOPE + V_DIM))
    )
    grad_w_kv = dot_tn(compressed, d_key_value)
    d_latent_sum = scatter(
        jnp.concatenate(
            [dot_nt(d_key_value, w_kv), jnp.sum(d_keys[..., QK_NOPE:], axis=1)], axis=1
        ).astype(bf16),
        1,
        5,
        by_rows=True,
    )
    own_first = (row_id * cols_n + col_id) * (group // (rows_n * cols_n))

    def own_tokens(value):
        return lax.dynamic_slice_in_dim(value, own_first, group // (rows_n * cols_n), 0)

    raw_own, factor_own = own_tokens(compressed_raw), own_tokens(kv_factor)
    d_compressed = d_latent_sum[:, :KV_RANK]
    weighted = d_compressed * latent_gain
    grad_latent_gain = jnp.sum(d_compressed * raw_own * factor_own[:, None], axis=0)
    inner = jnp.sum(weighted * raw_own, axis=1)
    d_raw = (
        factor_own[:, None] * weighted
        - raw_own * (factor_own * factor_own * factor_own * inner / KV_RANK)[:, None]
    )
    d_latent = gather(
        jnp.concatenate(
            [d_raw, unrotate(d_latent_sum[:, KV_RANK:], own_tokens(cosine), own_tokens(sine))],
            axis=1,
        ).astype(bf16),
        1,
        6,
        by_rows=True,
    )
    slab = w_latent.shape[1]
    slab_start = col_id * half_width + row_id * slab
    normed_slab = lax.dynamic_slice_in_dim(normed_group, slab_start, slab, 1)
    grad_w_latent = dot_tn(d_latent, normed_slab)
    grad_w_query = trade(dot_tn(normed_group, d_query_pre).astype(bf16), 0, 1)
    d_gathered = dot_nt(d_query_pre, w_query_own)
    piece = lax.dynamic_slice_in_dim(d_gathered, slab_start, slab, 1) + dot_nt(
        d_latent, w_latent[0]
    )
    d_gathered = lax.dynamic_update_slice_in_dim(d_gathered, piece, slab_start, 1)
    d_first = scatter(d_gathered.astype(bf16), 1, 2)
    gain_one = lax.dynamic_slice_in_dim(norm1_gain, col_id * half_width, half_width)
    factor_one = lax.dynamic_slice_in_dim(factor_group, row_id * block, block)
    d_norm_one, grad_gain_one = norm_back(input_wide, factor_one, gain_one, d_first, width)
    input_grad = d_hidden_state + d_norm_one
    if pieces == 1:
        out_parts, input_grad = lax.optimization_barrier((out_parts, input_grad))
        branch = made_scatter(*out_parts, exps_n, 9)
    output = (hidden_state + branch).astype(bf16)

    small = jnp.concatenate(
        [
            grad_gain_one[None],
            grad_gain_two[None],
            jnp.pad(grad_latent_gain, (0, half_width - KV_RANK))[None],
            grad_router.T,
        ],
        axis=0,
    )
    small = jnp.pad(small, ((0, -small.shape[0] % 8), (0, 0)))
    small = small_sum(small, exps_n, 7)
    summed_latent_gain = small[2, :KV_RANK] + small[2, half_width : half_width + KV_RANK]

    grad_shared, grad_w_query = lax.optimization_barrier((grad_shared, grad_w_query))
    grad_shared = grad_shared.reshape(3, cols_n * exps_n * units, half_width).astype(jnp.float32)
    summed = lax.psum(
        (grad_w_query, grad_w_latent.astype(bf16), grad_w_kv.astype(bf16), grad_w_out), "exp"
    )
    return (
        output,
        input_grad,
        small[0],
        summed[0].astype(jnp.float32),
        summed[1].T.astype(jnp.float32)[None],
        summed_latent_gain,
        summed[2].astype(jnp.float32),
        summed[3].astype(jnp.float32),
        small[1],
        grad_shared[0].T,
        grad_shared[1].T,
        grad_shared[2],
        small[3 : 3 + experts].T,
        grad_gate.T[None],
        grad_up.T[None],
        grad_down.T[None],
    )


def solution(mesh):
    placed = (
        P(("row", "exp"), "col"),
        P("exp", None),
        P("col", ("row", "exp"), None),
        P(),
        P("col", "row"),
        P("col", "row", None),
        P(),
        P(None, ("row", "col")),
        P("row", "col"),
        P(),
        P("col", "row"),
        P("col", "row"),
        P("row", "col"),
        P(),
        P(("row", "exp"), None, "col"),
        P(("row", "exp"), None, "col"),
        P(("row", "exp"), None, "col"),
        P(("row", "exp"), "col"),
    )
    return jax.shard_map(
        per_device,
        mesh=mesh,
        in_specs=placed,
        out_specs=(
            P(("row", "exp"), "col"),
            P(("row", "exp"), "col"),
            P(),
            P("col", "row"),
            P("col", "row", None),
            P(),
            P(None, ("row", "col")),
            P("row", "col"),
            P(),
            P("col", "row"),
            P("col", "row"),
            P("row", "col"),
            P(),
            P(("row", "exp"), None, "col"),
            P(("row", "exp"), None, "col"),
            P(("row", "exp"), None, "col"),
        ),
        check_vma=False,
    )
```

```python
import functools
import math

import jax
import jax.numpy as jnp
from jax import lax
from jax.experimental import pallas as pl
from jax.experimental.pallas import tpu as pltpu
from jax.sharding import PartitionSpec as P

QK_NOPE = 128
ROPE = 64
KV_RANK = 512
V_DIM = 128

epsilon = 1e-06
theta_base = 10000.0
SWAP = [(0, 1), (1, 0)]


MESH = pl.DeviceIdType.MESH


class Place:
    def __init__(self, layers):
        self.layers = layers
        self.row, self.col = lax.axis_index("row"), lax.axis_index("col")
        self.layer = lax.axis_index("exp") if layers > 1 else 0
        self.core = lax.rem(self.row, 2)
        self.x_row = lax.rem(self.row + 2, 4)
        self.core_row = self.row + 1 - 2 * self.core
        self.y_col = 1 - self.col
        self.to_x = {"row": self.x_row}
        self.to_y = {"col": self.y_col}
        self.to_core = {"row": self.core_row}
        self.above = {"exp": self.layer + 1}
        self.below = {"exp": self.layer - 1}

    def greet(self):
        barrier = pltpu.get_barrier_semaphore()
        for target in (self.to_x, self.to_y, self.to_core):
            pl.semaphore_signal(barrier, inc=1, device_id=target, device_id_type=MESH)
        if self.layers > 1:

            @pl.when(self.layer > 0)
            def _():
                pl.semaphore_signal(barrier, inc=1, device_id=self.below, device_id_type=MESH)

            @pl.when(self.layer < self.layers - 1)
            def _():
                pl.semaphore_signal(barrier, inc=1, device_id=self.above, device_id_type=MESH)

        peers = 3
        if self.layers > 1:
            peers = peers + jnp.where(self.layer > 0, 1, 0) + jnp.where(self.layer < self.layers - 1, 1, 0)
        pl.semaphore_wait(barrier, peers)


def remote(src, dst, send, recv, target):
    return pltpu.make_async_remote_copy(
        src_ref=src, dst_ref=dst, send_sem=send, recv_sem=recv, device_id=target, device_id_type=MESH
    )


def first_part(rows):
    return (rows // 2 + 15) // 16 * 16


def piece_of(where, layers, shape, by_rows, row, col, layer, span=None):
    rows, width = shape
    start, size = (0, rows) if span is None else span
    if by_rows:
        first = pl.multiple_of((row * 2 + col) * rows + start, 16)
        return where.at[pl.ds(first, size)]
    first = pl.multiple_of((row * layers + layer) * rows + start, 16)
    return where.at[pl.ds(first, size), pl.ds(pl.multiple_of(col * width, 128), width)]


class Gather:
    def __init__(self, me, layers, by_rows, shape, held, sems):
        self.me, self.layers, self.by_rows, self.shape, self.held = me, layers, by_rows, shape, held
        self.up_send, self.down_send, self.z_recv = sems[:3]
        self.send, self.recv, self.diag_send, self.diag_recv = sems[3:]
        part = first_part(shape[0])
        self.spans = ((0, part), (part, shape[0] - part))
        self.owners = (
            (me.row, me.col),
            (me.x_row, me.col),
            (me.row, me.y_col),
            (me.x_row, me.y_col),
        )
        self.sides = (me.to_x, me.to_y)

    @staticmethod
    def semaphores(layers):
        dma = pltpu.SemaphoreType.DMA
        line = [dma((layers,)) for _ in range(3)]
        return [*line, dma((5, 4, layers)), dma((5, 4, layers)), dma((2, layers)), dma((2, layers))]

    def area(self, where, row, col, layer, span=None):
        return piece_of(where, self.layers, self.shape, self.by_rows, row, col, layer, span)

    def piece(self, kind, layer, span=None):
        return self.area(self.held, *self.owners[kind], layer, span)

    def partner_piece(self, where, kind, layer):
        row, col = self.owners[kind]
        return self.area(where, row + 1 - 2 * self.me.core, col, layer)

    def to_core(self, kind, layer):
        piece = self.piece(kind, layer)
        sems = (4, kind, layer)
        return remote(piece, piece, self.send.at[sems], self.recv.at[sems], self.me.to_core)

    def from_core(self, kind, layer):
        piece = self.partner_piece(self.held, kind, layer)
        sems = (4, kind, layer)
        return remote(piece, piece, self.send.at[sems], self.recv.at[sems], self.me.to_core)

    def beside(self, axis, half, layer, incoming=False):
        piece = self.piece(axis + 1 if incoming else 0, layer, self.spans[half])
        sems = (2 * axis + half, 0, layer)
        return remote(piece, piece, self.send.at[sems], self.recv.at[sems], self.sides[axis])

    def corner(self, axis, layer, incoming=False):
        piece = self.piece(3 if incoming else axis + 1, layer, self.spans[axis])
        sems = (axis, layer)
        return remote(
            piece, piece, self.diag_send.at[sems], self.diag_recv.at[sems], self.sides[1 - axis]
        )

    def along(self, up, layer):
        piece = self.piece(0, layer)
        return remote(
            piece,
            piece,
            (self.up_send if up else self.down_send).at[layer],
            self.z_recv.at[layer],
            self.me.above if up else self.me.below,
        )

    def pass_on(self, up, layer):
        me = self.me

        @pl.when((me.layer < self.layers - 1) if up else (me.layer > 0))
        def _():
            self.along(up, layer).start()

    def spread(self, layer):
        self.beside(0, 0, layer).start()
        self.beside(1, 1, layer).start()
        self.beside(0, 1, layer).start()
        self.beside(1, 0, layer).start()
        self.to_core(0, layer).start()

    def begin(self):
        if self.layers > 1:
            self.pass_on(True, self.me.layer)
            self.pass_on(False, self.me.layer)
        self.spread(self.me.layer)

    def at_distance(self, distance, act):
        me = self.me
        if distance == 0:
            act(me.layer, None)
            return

        @pl.when(me.layer >= distance)
        def _():
            act(me.layer - distance, True)

        @pl.when(me.layer + distance < self.layers)
        def _():
            act(me.layer + distance, False)

    def arrived(self, layer, upward):
        self.along(upward, layer).wait_recv()
        self.pass_on(upward, layer)
        self.spread(layer)

    def second(self, layer):
        for axis in (0, 1):
            self.beside(axis, axis, layer, True).wait_recv()
            self.corner(axis, layer).start()
        for axis in (0, 1):
            self.beside(axis, 1 - axis, layer, True).wait_recv()
            self.to_core(axis + 1, layer).start()

    def third(self, layer):
        for axis in (0, 1):
            self.corner(axis, layer, True).wait_recv()
        self.to_core(3, layer).start()

    def finish(self):
        me, layers = self.me, self.layers
        for layer in range(layers):
            for kind in range(4):
                self.to_core(kind, layer).wait_send()
            for axis in (0, 1):
                for half in (0, 1):
                    self.beside(axis, half, layer).wait_send()
                self.corner(axis, layer).wait_send()
        if layers > 1:
            for layer in range(layers):

                @pl.when((me.layer < layers - 1) & (layer <= me.layer))
                def _():
                    self.along(True, layer).wait_send()

                @pl.when((me.layer > 0) & (layer >= me.layer))
                def _():
                    self.along(False, layer).wait_send()


def gather_body(layers, by_rows, *refs):
    count = len(by_rows)
    me = Place(layers)
    srcs, outs, refs = refs[:count], refs[count : 2 * count], refs[2 * count :]
    works, stores = [], []
    for i in range(count):
        held, store_sem, *sems = refs[9 * i : 9 * i + 9]
        works.append(Gather(me, layers, by_rows[i], srcs[i].shape, held, sems))

        def store(kind, layer, partner, work=works[i], out=outs[i], store_sem=store_sem):
            if partner:
                pair = (
                    work.partner_piece(work.held, kind, layer),
                    work.partner_piece(out, kind, layer),
                )
            else:
                pair = (work.piece(kind, layer), work.area(out, *work.owners[kind], layer))
            return pltpu.make_async_copy(*pair, store_sem.at[1 if partner else 0, kind, layer])

        stores.append(store)
    own = [
        pltpu.make_async_copy(src, work.piece(0, me.layer), refs[9 * i + 1].at[0, 0, me.layer])
        for i, (src, work) in enumerate(zip(srcs, works))
    ]
    for copy in own:
        copy.start()
    me.greet()
    for copy, work, store in zip(own, works, stores):
        copy.wait()
        work.begin()
        store(0, me.layer, False).start()

    def arrived(layer, upward):
        for work, store in zip(works, stores):
            work.arrived(layer, upward)
            store(0, layer, False).start()

    def second(layer, upward):
        for work, store in zip(works, stores):
            work.second(layer)
            for kind in (1, 2):
                store(kind, layer, False).start()

    def third(layer, upward):
        for work, store in zip(works, stores):
            work.third(layer)
            store(3, layer, False).start()
            for kind in range(4):
                work.from_core(kind, layer).wait_recv()
                store(kind, layer, True).start()

    for step in range(1, layers + 2):
        if step < layers:
            works[0].at_distance(step, arrived)
        if step - 1 < layers:
            works[0].at_distance(step - 1, second)
        if 0 <= step - 2 < layers:
            works[0].at_distance(step - 2, third)
    for work, store in zip(works, stores):
        for layer in range(layers):
            for kind in range(4):
                store(kind, layer, False).wait()
                store(kind, layer, True).wait()
        work.finish()


def gather(value, layers, collective_id, by_rows=False):
    return gather_several((value,), layers, collective_id, (by_rows,))[0]


def gather_several(values, layers, collective_id, by_rows):
    dma = pltpu.SemaphoreType.DMA
    shapes, scratch = [], []
    for value, rows_only in zip(values, by_rows):
        rows, width = value.shape
        shapes.append((8 * rows, width) if rows_only else (4 * layers * rows, 2 * width))
        scratch += [
            pltpu.VMEM(shapes[-1], value.dtype),
            dma((2, 4, layers)),
            *Gather.semaphores(layers),
        ]
    in_hbm = pl.BlockSpec(memory_space=pl.ANY)
    return pl.pallas_call(
        functools.partial(gather_body, layers, by_rows),
        out_shape=[
            jax.ShapeDtypeStruct(shape, value.dtype) for shape, value in zip(shapes, values)
        ],
        in_specs=[in_hbm] * len(values),
        out_specs=[in_hbm] * len(values),
        scratch_shapes=scratch,
        compiler_params=pltpu.CompilerParams(
            collective_id=collective_id,
            has_side_effects=True,
            vmem_limit_bytes=56 * 1024 * 1024,
        ),
    )(*values)


def scatter_body(
    layers,
    by_rows,
    src,
    out,
    acc,
    core_in,
    diag_a,
    diag_b,
    side_in,
    line_in,
    load_sem,
    core_send,
    core_recv,
    diag_send,
    diag_recv,
    side_send,
    side_recv,
    line_send,
    line_recv,
):
    me = Place(layers)
    rows, width = out.shape
    part = first_part(rows)
    owners = (
        (me.row, me.col),
        (me.x_row, me.col),
        (me.row, me.y_col),
        (me.x_row, me.y_col),
    )

    def layer_at(step):
        if layers == 1:
            return 0
        found = 0
        for layer in range(layers):
            order = sorted(range(layers), key=lambda other: (-abs(other - layer), -other))
            found = found + jnp.where(me.layer == layer, order[step], 0)
        return found

    layer_of = [layer_at(step) for step in range(layers)]

    def area(row, col, layer):
        return piece_of(src, layers, (rows, width), by_rows, row, col, layer)

    def load(step, kind):
        return pltpu.make_async_copy(
            area(*owners[kind], layer_of[step]), acc.at[step, kind], load_sem.at[step, kind]
        )

    def to_core(step, kind):
        row, col = owners[kind]
        return remote(
            area(row + 1 - 2 * me.core, col, layer_of[step]),
            core_in.at[step, kind],
            core_send.at[step, kind],
            core_recv.at[step, kind],
            me.to_core,
        )

    def diag(step, axis):
        start, size = ((0, part), (part, rows - part))[axis]
        return remote(
            acc.at[step, 3, pl.ds(start, size)],
            (diag_a, diag_b)[axis].at[step],
            diag_send.at[axis, step],
            diag_recv.at[axis, step],
            (me.to_y, me.to_x)[axis],
        )

    def side(step, axis):
        return remote(
            acc.at[step, axis + 1],
            side_in.at[axis, step],
            side_send.at[axis, step],
            side_recv.at[axis, step],
            (me.to_x, me.to_y)[axis],
        )

    def line(step, up):
        layer = layer_of[step]
        way = 0 if up else 1
        return remote(
            acc.at[step, 0],
            line_in.at[way, layer],
            line_send.at[step],
            line_recv.at[way, layer],
            me.above if up else me.below,
        )

    lanes = 32 if part % 32 == 0 and rows % 32 == 0 else 16

    def add(target, others, start=0, size=rows, into=None):
        def step(i, carry):
            first = pl.multiple_of(i * lanes, 16)
            total = target[pl.ds(start + first, lanes), :].astype(jnp.float32)
            for other in others:
                total = total + other[pl.ds(first, lanes), :].astype(jnp.float32)
            if into is None:
                target[pl.ds(start + first, lanes), :] = total.astype(target.dtype)
            else:
                into[pl.ds(first, lanes), :] = total.astype(into.dtype)
            return carry

        lax.fori_loop(0, size // lanes, step, 0)

    me.greet()
    kinds = (3, 1, 2, 0)
    for step in range(layers):
        for kind in kinds:
            to_core(step, kind).start()
            load(step, kind).start()

    def ready(step, kind):
        load(step, kind).wait()
        to_core(step, kind).wait_recv()

    def stage_a(step):
        ready(step, 3)
        add(acc.at[step, 3], [core_in.at[step, 3]])
        diag(step, 0).start()
        diag(step, 1).start()

    def stage_b(step):
        for axis, buffer, start, size in (
            (0, diag_a, 0, part),
            (1, diag_b, part, rows - part),
        ):
            kind = axis + 1
            ready(step, kind)
            add(acc.at[step, kind], [core_in.at[step, kind]])
            diag(step, axis).wait_recv()
            add(acc.at[step, kind], [buffer.at[step]], start, size)
            side(step, axis).start()

    def stage_c(step):
        ready(step, 0)
        side(step, 0).wait_recv()
        side(step, 1).wait_recv()
        parts = [core_in.at[step, 0], side_in.at[0, step], side_in.at[1, step]]
        if layers == 1:
            add(acc.at[step, 0], parts, into=out)
            return
        add(acc.at[step, 0], parts)
        layer = layer_of[step]
        if step < layers - 1:

            @pl.when((layer > me.layer) & (me.layer > 0))
            def _():
                line(step, True).wait_recv()
                add(acc.at[step, 0], [line_in.at[0, layer]])

            @pl.when((layer < me.layer) & (me.layer < layers - 1))
            def _():
                line(step, False).wait_recv()
                add(acc.at[step, 0], [line_in.at[1, layer]])

            @pl.when(layer > me.layer)
            def _():
                line(step, True).start()

            @pl.when(layer < me.layer)
            def _():
                line(step, False).start()
        else:
            inner = (me.layer > 0) & (me.layer < layers - 1)

            @pl.when(me.layer > 0)
            def _():
                line(step, True).wait_recv()

            @pl.when(me.layer < layers - 1)
            def _():
                line(step, False).wait_recv()

            @pl.when(inner)
            def _():
                add(acc.at[step, 0], [line_in.at[0, layer], line_in.at[1, layer]], into=out)

            @pl.when(me.layer == 0)
            def _():
                add(acc.at[step, 0], [line_in.at[1, layer]], into=out)

            @pl.when(me.layer == layers - 1)
            def _():
                add(acc.at[step, 0], [line_in.at[0, layer]], into=out)

    for step in range(layers + 2):
        if step < layers:
            stage_a(step)
        if 0 <= step - 1 < layers:
            stage_b(step - 1)
        if 0 <= step - 2 < layers:
            stage_c(step - 2)
    for step in range(layers):
        for kind in kinds:
            to_core(step, kind).wait_send()
        for axis in (0, 1):
            diag(step, axis).wait_send()
            side(step, axis).wait_send()
        if step < layers - 1:

            @pl.when(layer_of[step] > me.layer)
            def _():
                line(step, True).wait_send()

            @pl.when(layer_of[step] < me.layer)
            def _():
                line(step, False).wait_send()


def scatter(value, layers, collective_id, by_rows=False):
    if by_rows:
        rows, width = value.shape[0] // 8, value.shape[1]
    else:
        rows, width = value.shape[0] // (4 * layers), value.shape[1] // 2
    part = first_part(rows)
    dma = pltpu.SemaphoreType.DMA
    buffer = lambda *lead: pltpu.VMEM((*lead, rows, width), value.dtype)
    return pl.pallas_call(
        functools.partial(scatter_body, layers, by_rows),
        out_shape=jax.ShapeDtypeStruct((rows, width), jnp.float32),
        in_specs=[pl.BlockSpec(memory_space=pl.ANY)],
        out_specs=pl.BlockSpec(memory_space=pltpu.VMEM),
        scratch_shapes=[
            buffer(layers, 4),
            buffer(layers, 4),
            pltpu.VMEM((layers, part, width), value.dtype),
            pltpu.VMEM((layers, rows - part, width), value.dtype),
            buffer(2, layers),
            buffer(2, layers),
            dma((layers, 4)),
            dma((layers, 4)),
            dma((layers, 4)),
            dma((2, layers)),
            dma((2, layers)),
            dma((2, layers)),
            dma((2, layers)),
            dma((layers,)),
            dma((2, layers)),
        ],
        compiler_params=pltpu.CompilerParams(
            collective_id=collective_id,
            has_side_effects=True,
            vmem_limit_bytes=56 * 1024 * 1024,
        ),
    )(value)


def dot_nn(left, right):
    return jnp.dot(left, right, preferred_element_type=jnp.float32)


def dot_nt(left, right):
    return lax.dot_general(
        left, right, (((1,), (1,)), ((), ())), preferred_element_type=jnp.float32
    )


def dot_tn(left, right):
    return lax.dot_general(
        left, right, (((0,), (0,)), ((), ())), preferred_element_type=jnp.float32
    )


def made_scatter_body(layers, parts, jobs, *refs):
    slots_hbm, refs = refs[:parts], refs[parts:]
    weights_hbm, refs = refs[:parts], refs[parts:]
    spread_hbm, side_hbm, side_w_hbm, refs = *refs[:3], refs[3:]
    job_a, job_b, refs = refs[:jobs], refs[jobs : 2 * jobs], refs[2 * jobs :]
    out, job_out, refs = refs[0], refs[1 : 1 + jobs], refs[1 + jobs :]
    if jobs:
        job_acc, a_in, b_in, job_sem, flush_sem, refs = *refs[:5], refs[5:]
    slots_in, refs = refs[:parts], refs[parts:]
    weights, refs = refs[:parts], refs[parts:]
    spread_in, side_in, side_w, slot_rows, refs = *refs[:4], refs[4:]
    core_out, acc, core_in, diag_a, diag_b, beside_in, line_in, refs = *refs[:7], refs[7:]
    in_sem, weight_sem, core_send, core_recv, diag_send, diag_recv, side_send, side_recv = refs[:8]
    line_send, line_recv = refs[8:]
    me = Place(layers)
    rows, width = out.shape
    part = first_part(rows)
    f32 = jnp.float32
    per_block, few, slots = spread_in.shape[2:]
    x_mine = me.row // 2

    def layer_at(step):
        return nearest_first(layers, layers - 1 - step, me.layer)

    def loads(unit):
        step, own = unit // 2, lax.rem(unit, 2)
        core = me.core * own + (1 - me.core) * (1 - own)
        slot = lax.rem(unit, 2)
        layer = layer_at(step)
        pairs = [*zip(slots_hbm, slots_in), (spread_hbm, spread_in), (side_hbm, side_in)]
        return [
            pltpu.make_async_copy(
                src.at[x_mine if x == 0 else 1 - x_mine, core, layer],
                dst.at[slot, x],
                in_sem.at[slot, i, x],
            )
            for i, (src, dst) in enumerate(pairs)
            for x in range(2)
        ]

    def weight_loads():
        pairs = [*zip(weights_hbm, weights), (side_w_hbm, side_w)]
        copies = []
        for i, (src, dst) in enumerate(pairs):
            for at, col in enumerate((me.col, me.y_col)):
                copies.append(
                    pltpu.make_async_copy(
                        src.at[:, pl.ds(pl.multiple_of(col * width, 128), width)],
                        dst.at[:, pl.ds(at * width, width)],
                        weight_sem.at[i, at],
                    )
                )
        return copies

    def make(unit, put):
        for copy in loads(unit):
            copy.wait()

        @pl.when(unit + 1 < 2 * layers)
        def _():
            for copy in loads(unit + 1):
                copy.start()

        slot = lax.rem(unit, 2)
        total = sum(
            dot_nn(value[slot].reshape(-1, value.shape[-1]), weight[...])
            for value, weight in zip(slots_in, weights)
        )
        slot_rows[...] = total.astype(slot_rows.dtype)
        for x in range(2):
            for j in range(per_block):
                there = pl.ds(j * few, few)
                here = pl.ds((x * per_block + j) * slots, slots)
                made = dot_nn(spread_in[slot, x, j], slot_rows[here, :]) + dot_nn(
                    side_in[slot, x, there, :], side_w[...]
                )
                put(x, there, made[:, :width].astype(acc.dtype))
                put(x + 2, there, made[:, width:].astype(acc.dtype))

    def to_core(step, kind):
        return remote(
            core_out.at[lax.rem(step, 2), kind],
            core_in.at[step, kind],
            core_send.at[step, kind],
            core_recv.at[step, kind],
            me.to_core,
        )

    def diag(step, axis):
        start, size = ((0, part), (part, rows - part))[axis]
        return remote(
            acc.at[step, 3, pl.ds(start, size)],
            (diag_a, diag_b)[axis].at[step],
            diag_send.at[axis, step],
            diag_recv.at[axis, step],
            (me.to_y, me.to_x)[axis],
        )

    def side(step, axis):
        return remote(
            acc.at[step, axis + 1],
            beside_in.at[axis, step],
            side_send.at[axis, step],
            side_recv.at[axis, step],
            (me.to_x, me.to_y)[axis],
        )

    def line(step, up):
        layer = layer_at(step)
        way = 0 if up else 1
        return remote(
            acc.at[step, 0],
            line_in.at[way, layer],
            line_send.at[step],
            line_recv.at[way, layer],
            me.above if up else me.below,
        )

    lanes = 32 if part % 32 == 0 and rows % 32 == 0 else 16

    def add(target, others, start=0, size=rows, into=None):
        def step(i, carry):
            first = pl.multiple_of(i * lanes, 16)
            total = target[pl.ds(start + first, lanes), :].astype(f32)
            for other in others:
                total = total + other[pl.ds(first, lanes), :].astype(f32)
            if into is None:
                target[pl.ds(start + first, lanes), :] = total.astype(target.dtype)
            else:
                into[pl.ds(first, lanes), :] = total.astype(into.dtype)
            return carry

        lax.fori_loop(0, size // lanes, step, 0)

    turns = layers + 2
    chunk = a_in.shape[1] if jobs else 0
    chunks = job_a[0].shape[0] // chunk if jobs else 0

    def job_loads(unit, job):
        slot = lax.rem(unit, 2)
        here = pl.ds(pl.multiple_of(lax.rem(unit, turns) * chunk, 16), chunk)
        return [
            pltpu.make_async_copy(src.at[here], dst.at[slot], job_sem.at[slot, i])
            for i, (src, dst) in enumerate(((job_a[job], a_in), (job_b[job], b_in)))
        ]

    def start_job_loads(unit):
        for job in range(jobs):

            @pl.when((unit // turns == job) & (lax.rem(unit, turns) < chunks))
            def _():
                for copy in job_loads(unit, job):
                    copy.start()

    def flush(job):
        return pltpu.make_async_copy(job_acc, job_out[job], flush_sem)

    def job_turn(unit):
        if not jobs:
            return
        at = lax.rem(unit, turns)
        slot = lax.rem(unit, 2)

        @pl.when(unit + 1 < jobs * turns)
        def _():
            start_job_loads(unit + 1)

        @pl.when((at == 0) & (unit > 0))
        def _():
            flush(0).wait()

        @pl.when(at == 0)
        def _():
            job_acc[...] = jnp.zeros_like(job_acc)

        @pl.when(at < chunks)
        def _():
            for copy in job_loads(unit, 0):
                copy.wait()
            left = a_in[slot].T
            for first in range(0, 2 * width, width // 2):
                here = pl.ds(first, width // 2)
                job_acc[:, here] += dot_nn(left, b_in[slot, :, here])

        for job in range(jobs):

            @pl.when((at == chunks - 1) & (unit // turns == job))
            def _():
                flush(job).start()

    for copy in (*weight_loads(), *loads(0)):
        copy.start()
    if jobs:
        start_job_loads(0)
    me.greet()
    for copy in weight_loads():
        copy.wait()

    def produce(step):
        @pl.when(step >= 2)
        def _():
            for kind in range(4):
                to_core(step - 2, kind).wait_send()

        half = lax.rem(step, 2)

        def to_other(kind, there, value):
            core_out[half, kind, there, :] = value

        make(2 * step, to_other)
        for kind in (3, 1, 2, 0):
            to_core(step, kind).start()

        def to_own(kind, there, value):
            acc[step, kind, there, :] = value

        make(2 * step + 1, to_own)

    def stage_a(step):
        to_core(step, 3).wait_recv()
        add(acc.at[step, 3], [core_in.at[step, 3]])
        diag(step, 0).start()
        diag(step, 1).start()

    def stage_b(step):
        for axis, buffer, start, size in (
            (0, diag_a, 0, part),
            (1, diag_b, part, rows - part),
        ):
            kind = axis + 1
            to_core(step, kind).wait_recv()
            add(acc.at[step, kind], [core_in.at[step, kind]])
            diag(step, axis).wait_recv()
            add(acc.at[step, kind], [buffer.at[step]], start, size)
            side(step, axis).start()

    def stage_c(step):
        to_core(step, 0).wait_recv()
        side(step, 0).wait_recv()
        side(step, 1).wait_recv()
        add(acc.at[step, 0], [core_in.at[step, 0], beside_in.at[0, step], beside_in.at[1, step]])
        layer = layer_at(step)

        @pl.when((layer > me.layer) & (me.layer > 0))
        def _():
            line(step, True).wait_recv()
            add(acc.at[step, 0], [line_in.at[0, layer]])

        @pl.when((layer < me.layer) & (me.layer < layers - 1))
        def _():
            line(step, False).wait_recv()
            add(acc.at[step, 0], [line_in.at[1, layer]])

        @pl.when(layer > me.layer)
        def _():
            line(step, True).start()

        @pl.when(layer < me.layer)
        def _():
            line(step, False).start()

    def stages(step, carry):
        @pl.when(step < layers)
        def _():
            produce(step)
            stage_a(step)

        job_turn(3 * step)

        @pl.when((step >= 1) & (step <= layers))
        def _():
            stage_b(step - 1)

        job_turn(3 * step + 1)

        @pl.when(step >= 2)
        def _():
            stage_c(step - 2)

        job_turn(3 * step + 2)
        return carry

    lax.fori_loop(0, layers + 2, stages, 0)
    last = layers - 1

    @pl.when(me.layer > 0)
    def _():
        line(last, True).wait_recv()

    @pl.when(me.layer < last)
    def _():
        line(last, False).wait_recv()

    @pl.when((me.layer > 0) & (me.layer < last))
    def _():
        add(acc.at[last, 0], [line_in.at[0, me.layer], line_in.at[1, me.layer]], into=out)

    @pl.when(me.layer == 0)
    def _():
        add(acc.at[last, 0], [line_in.at[1, me.layer]], into=out)

    @pl.when(me.layer == last)
    def _():
        add(acc.at[last, 0], [line_in.at[0, me.layer]], into=out)

    if jobs:
        flush(0).wait()
    for step in range(layers):
        if step >= layers - 2:
            for kind in range(4):
                to_core(step, kind).wait_send()
        for axis in (0, 1):
            diag(step, axis).wait_send()
            side(step, axis).wait_send()
        if step < last:

            @pl.when(layer_at(step) > me.layer)
            def _():
                line(step, True).wait_send()

            @pl.when(layer_at(step) < me.layer)
            def _():
                line(step, False).wait_send()


def made_scatter(slots_in, weights, spread, side, side_w, job_a, job_b, layers, collective_id):
    block, width = side.shape[3], side_w.shape[1] // 2
    bf16, f32 = jnp.bfloat16, jnp.float32
    parts, jobs = len(weights), len(job_a)
    part = first_part(block)
    dma = pltpu.SemaphoreType.DMA
    buffer = lambda *lead: pltpu.VMEM((*lead, block, width), bf16)
    ahead = lambda value: pltpu.VMEM((2, 2, *value.shape[3:]), bf16)
    in_hbm = pl.BlockSpec(memory_space=pl.ANY)
    job_shapes, job_scratch = [], []
    if jobs:
        rows, tall, wide = *job_a[0].shape, job_b[0].shape[1]
        chunks = max(n for n in range(1, layers + 3) if rows % (16 * n) == 0)
        job_shapes = [jax.ShapeDtypeStruct((tall, wide), f32)] * jobs
        job_scratch = [
            pltpu.VMEM((tall, wide), f32),
            pltpu.VMEM((2, rows // chunks, tall), bf16),
            pltpu.VMEM((2, rows // chunks, wide), bf16),
            dma((2, 2)),
            dma,
        ]
    return pl.pallas_call(
        functools.partial(made_scatter_body, layers, parts, jobs),
        out_shape=[jax.ShapeDtypeStruct((block, width), f32), *job_shapes],
        in_specs=[in_hbm] * (2 * parts + 3 + 2 * jobs),
        out_specs=[pl.BlockSpec(memory_space=pltpu.VMEM), *[in_hbm] * jobs],
        scratch_shapes=[
            *job_scratch,
            *(ahead(value) for value in slots_in),
            *(pltpu.VMEM(value.shape, bf16) for value in weights),
            ahead(spread),
            ahead(side),
            pltpu.VMEM(side_w.shape, bf16),
            pltpu.VMEM((2 * slots_in[0].shape[3], 2 * width), bf16),
            buffer(2, 4),
            buffer(layers, 4),
            buffer(layers, 4),
            pltpu.VMEM((layers, part, width), bf16),
            pltpu.VMEM((layers, block - part, width), bf16),
            buffer(2, layers),
            buffer(2, layers),
            dma((2, parts + 2, 2)),
            dma((parts + 1, 2)),
            dma((layers, 4)),
            dma((layers, 4)),
            dma((2, layers)),
            dma((2, layers)),
            dma((2, layers)),
            dma((2, layers)),
            dma((layers,)),
            dma((2, layers)),
        ],
        compiler_params=pltpu.CompilerParams(
            collective_id=collective_id,
            has_side_effects=True,
            vmem_limit_bytes=62 * 1024 * 1024,
        ),
    )(*slots_in, *weights, spread, side, side_w, *job_a, *job_b)


def small_sum_body(layers, src, out, core_in, mid, x_in, near, line_in, total, send, recv, line_send, line_recv):
    me = Place(layers)
    width = src.shape[1]
    barrier = pltpu.get_barrier_semaphore()
    for target in (me.to_x, me.to_y, me.to_core):
        pl.semaphore_signal(barrier, inc=1, device_id=target, device_id_type=MESH)
    for step in range(1, layers):
        other = {"exp": lax.rem(me.layer + step, layers)}
        pl.semaphore_signal(barrier, inc=1, device_id=other, device_id_type=MESH)
    pl.semaphore_wait(barrier, 3 + layers - 1)
    swap = remote(src, core_in, send.at[0], recv.at[0], me.to_core)
    swap.start()
    swap.wait()
    mid[...] = src[...] + core_in[...]
    swap = remote(mid, x_in, send.at[1], recv.at[1], me.to_x)
    swap.start()
    swap.wait()
    near[...] = mid[...] + x_in[...]
    line_in[me.layer] = near[...]

    def along(step, incoming):
        layer = lax.rem(me.layer + (layers - step if incoming else 0), layers)
        return remote(
            near,
            line_in.at[layer],
            line_send.at[step],
            line_recv.at[step],
            {"exp": lax.rem(me.layer + step, layers)},
        )

    for step in range(1, layers):
        along(step, False).start()
    for step in range(1, layers):
        along(step, True).wait_recv()
    summed = line_in[0]
    for layer in range(1, layers):
        summed = summed + line_in[layer]
    total[...] = summed
    mine = pl.ds(pl.multiple_of(me.col * width, 128), width)
    theirs = pl.ds(pl.multiple_of(me.y_col * width, 128), width)
    out[:, mine] = summed
    remote(total, out.at[:, mine], send.at[2], recv.at[2], me.to_y).start()
    remote(total, out.at[:, theirs], send.at[2], recv.at[2], me.to_y).wait()
    for step in range(1, layers):
        along(step, False).wait_send()


def small_sum(value, layers, collective_id):
    rows, width = value.shape
    dma = pltpu.SemaphoreType.DMA
    buffer = lambda *lead: pltpu.VMEM((*lead, rows, width), value.dtype)
    in_vmem = pl.BlockSpec(memory_space=pltpu.VMEM)
    return pl.pallas_call(
        functools.partial(small_sum_body, layers),
        out_shape=jax.ShapeDtypeStruct((rows, 2 * width), value.dtype),
        in_specs=[in_vmem],
        out_specs=in_vmem,
        scratch_shapes=[
            buffer(),
            buffer(),
            buffer(),
            buffer(),
            buffer(layers),
            buffer(),
            dma((3,)),
            dma((3,)),
            dma((layers,)),
            dma((layers,)),
        ],
        compiler_params=pltpu.CompilerParams(
            collective_id=collective_id,
            has_side_effects=True,
            vmem_limit_bytes=32 * 1024 * 1024,
        ),
    )(value)


def nearest_first(layers, turn, layer):
    found = 0
    for here in range(layers):
        order = sorted(range(layers), key=lambda other: (abs(other - here), other))
        for at in range(layers):
            found = found + jnp.where((layer == here) & (turn == at), order[at], 0)
    return found


def expert_body(
    layers,
    units,
    experts,
    src,
    grads_ref,
    pick_ref,
    spread_ref,
    words_ref,
    gate_hbm,
    up_hbm,
    down_hbm,
    side_hbm,
    side_down_hbm,
    rows_all,
    slot_rows_ref,
    slot_grads_ref,
    hidden_ref,
    d_gate_ref,
    d_up_ref,
    d_gates_ref,
    side_hidden_ref,
    d_side_ref,
    grad_side_ref,
    grad_side_down_ref,
    gate_w,
    up_w,
    down_w,
    side_w,
    side_down,
    both_rows,
    side_hidden,
    d_side,
    weight_sem,
    rows_sem,
    *sems,
):
    bf16, f32 = jnp.bfloat16, jnp.float32
    me = Place(layers)
    work = Gather(me, layers, False, src.shape, rows_all, sems)
    own_expert = me.row * layers + me.layer
    block, half = src.shape
    width = 2 * half
    few, slots = pick_ref.shape[5], pick_ref.shape[4]
    per_block = block // few
    count = 2 * per_block
    lanes = side_down.shape[0]
    step = pl.program_id(0)
    steps = 2 * layers
    weight_loads = [
        pltpu.make_async_copy(src_ref, dst_ref, weight_sem.at[i])
        for i, (src_ref, dst_ref) in enumerate(
            (
                (down_hbm, down_w),
                (side_down_hbm, side_down),
                (side_hbm, side_w),
                (gate_hbm, gate_w),
                (up_hbm, up_w),
            )
        )
    ]

    def load(which, core):
        layer = nearest_first(layers, which // 2, me.layer)
        far = lax.rem(which, 2)
        x_place = me.row // 2 * (1 - far) + (1 - me.row // 2) * far
        first = pl.multiple_of(((2 * x_place + core) * layers + layer) * block, 16)
        slot = lax.rem(which, 2)
        return pltpu.make_async_copy(
            rows_all.at[pl.ds(first, block)],
            both_rows.at[slot, pl.ds(core * block, block)],
            rows_sem.at[slot, core],
        )

    def prepare(which):
        for distance in range(1, layers):

            @pl.when(which == distance - 1)
            def _():
                work.at_distance(distance, work.arrived)

        for turn in range(layers):
            at = nearest_first(layers, turn, me.layer)

            @pl.when(which == (max(1, 2 * turn) if turn != 1 else 3))
            def _():
                work.third(at)

            if turn > 0:

                @pl.when(which == (2 * turn - 1 if turn != 1 else 2))
                def _():
                    work.second(at)

        layer = nearest_first(layers, which // 2, me.layer)

        @pl.when(lax.rem(which, 2) == 0)
        def _():
            work.from_core(0, layer).wait_recv()
            work.from_core(2, layer).wait_recv()

        @pl.when(lax.rem(which, 2) == 1)
        def _():
            work.from_core(1, layer).wait_recv()
            work.from_core(3, layer).wait_recv()

        for core in range(2):
            load(which, core).start()

    @pl.when(step == 0)
    def _():
        own = pltpu.make_async_copy(src, work.piece(0, me.layer), rows_sem.at[0, 0])
        own.start()
        for copy in weight_loads:
            copy.start()
        me.greet()
        own.wait()
        work.begin()
        for copy in weight_loads:
            copy.wait()

    rows = both_rows.at[lax.rem(step, 2)]

    def spot(b):
        core, j = b // per_block, b % per_block
        return core, j, pl.ds(b * few, few), pl.ds(j * slots, slots)

    for b in range(count):
        core, j, _, here = spot(b)
        for c in range(2):
            slot_grads_ref[0, core, 0, here, c * half : (c + 1) * half] = dot_nn(
                pick_ref[0, core, 0, j], grads_ref[0, core, 0, c, j * few : (j + 1) * few, :]
            ).astype(bf16)
    join = lambda ref: jnp.concatenate([ref[0, core, 0] for core in range(2)], axis=0)
    d_raw = dot_nt(join(slot_grads_ref), down_w[...])
    side_grads = [
        jnp.concatenate([grads_ref[0, core, 0, c] for core in range(2)], axis=0) for c in range(2)
    ]
    d_side_hidden = sum(
        dot_nt(side_grads[c], side_down[:, c * half : (c + 1) * half]) for c in range(2)
    )

    @pl.when(step == 0)
    def _():
        work.second(me.layer)
        prepare(step)

    for core in range(2):
        load(step, core).wait()

    side = dot_nt(rows[...], side_w[...])
    side_gate, side_up = side[:, :lanes], side[:, lanes:]
    lane = lax.broadcasted_iota(jnp.int32, side_gate.shape, 1)
    expert = lane - units
    is_expert = (expert >= 0) & (expert < experts)
    highest = jnp.max(jnp.where(is_expert, side_gate, -jnp.inf), axis=1, keepdims=True)
    words = join(words_ref)
    word = words[:, 0:1]
    for i in range(1, words.shape[1]):
        word = jnp.where(expert >= 16 * i, words[:, i : i + 1], word)
    picked = lax.shift_right_logical(
        jnp.broadcast_to(word, expert.shape), jnp.bitwise_and(expert, 15)
    )
    picked = is_expert & (jnp.bitwise_and(picked, 1) == 1)
    chosen = jnp.where(picked, jnp.exp(jnp.where(is_expert, side_gate - highest, 0.0)), 0.0)
    total = jnp.sum(chosen, axis=1, keepdims=True)
    own = jnp.sum(jnp.where(expert == own_expert, chosen, 0.0), axis=1, keepdims=True) / total

    def two_parts(value):
        high = value.astype(bf16).astype(f32)
        at = lax.broadcasted_iota(jnp.int32, (value.shape[0], lanes), 1)
        return jnp.where(at == 0, high, jnp.where(at == 1, value - high, 0.0)).astype(bf16)

    own_parts = two_parts(own)
    slot_gates = []
    for b in range(count):
        core, j, tokens, here = spot(b)
        pick = pick_ref[0, core, 0, j]
        slot_rows_ref[0, core, 0, here, :] = dot_nn(pick, rows[tokens, :]).astype(bf16)
        parts = dot_nn(pick, own_parts[b * few : (b + 1) * few])
        slot_gates.append(jnp.sum(parts, axis=1, keepdims=True))
    slot_gate = jnp.concatenate(slot_gates, axis=0)

    slot_rows = join(slot_rows_ref)
    gate_pre = dot_nt(slot_rows, gate_w[...])
    up_pre = dot_nt(slot_rows, up_w[...])
    sigmoid = 1.0 / (1.0 + jnp.exp(-gate_pre))
    silu = gate_pre * sigmoid
    hidden = (silu * up_pre).astype(bf16).astype(f32)
    d_gates = jnp.sum(d_raw * hidden, axis=1, keepdims=True)
    d_hidden = d_raw * slot_gate
    each = per_block * slots

    def keep(ref, value):
        for core in range(2):
            ref[0, core, 0] = value[core * each : (core + 1) * each]

    hidden = (hidden * slot_gate).astype(bf16)
    keep(hidden_ref, hidden)
    d_up = (d_hidden * silu).astype(bf16)
    keep(d_up_ref, d_up)
    d_gate = (d_hidden * up_pre * sigmoid * (1.0 + gate_pre * (1.0 - sigmoid))).astype(bf16)
    keep(d_gate_ref, d_gate)

    @pl.when(step + 1 < steps)
    def _():
        prepare(step + 1)

    side_sigmoid = 1.0 / (1.0 + jnp.exp(-side_gate))
    side_silu = side_gate * side_sigmoid
    side_hidden[...] = (side_silu * side_up).astype(bf16)
    d_side[:, lanes:] = (d_side_hidden * side_silu).astype(bf16)
    d_side[:, :lanes] = (
        d_side_hidden * side_up * side_sigmoid * (1.0 + side_gate * (1.0 - side_sigmoid))
    ).astype(bf16)

    @pl.when(step == 0)
    def _():
        grad_side_ref[...] = jnp.zeros_like(grad_side_ref)
        grad_side_down_ref[...] = jnp.zeros_like(grad_side_down_ref)

    grad_side_ref[...] += dot_tn(d_side[...], rows[...])
    for c in range(2):
        grad_side_down_ref[:, c * half : (c + 1) * half] += dot_tn(side_hidden[...], side_grads[c])

    d_gate_parts = two_parts(d_gates)
    for b in range(count):
        core, j, tokens, _ = spot(b)
        there = pl.ds(j * few, few)
        back = dot_nn(spread_ref[0, core, 0, j], d_gate_parts[b * slots : (b + 1) * slots])
        d_gates_ref[0, core, 0, there, :] = jnp.sum(back, axis=1, keepdims=True)
        side_hidden_ref[0, core, 0, there, :] = side_hidden[tokens, :]
        d_side_ref[0, core, 0, there, :] = d_side[tokens, :]

    @pl.when(step == steps - 1)
    def _():
        work.finish()


def expert_pass(layers, few, slots, units, experts, rows_own, grads, pick, spread, words, weights, side_w, side_down):
    block, half = rows_own.shape
    width = 2 * half
    hidden = weights[0].shape[0]
    per_block = block // few
    tokens = 4 * layers * block
    lanes = side_down.shape[0]

    def by_step(*tail):
        def place(step):
            row = lax.axis_index("row")
            layer = nearest_first(layers, step // 2, lax.axis_index("exp"))
            far = lax.rem(step, 2)
            x_place = row // 2 * (1 - far) + (1 - row // 2) * far
            return (x_place, 0, layer, *(0 for _ in tail))

        return pl.BlockSpec((1, 2, 1, *tail), place)

    shape = lambda *tail, kind=jnp.bfloat16: jax.ShapeDtypeStruct((2, 2, layers, *tail), kind)
    each = per_block * slots
    outs = pl.pallas_call(
        functools.partial(expert_body, layers, units, experts),
        grid=(2 * layers,),
        in_specs=[
            pl.BlockSpec(memory_space=pl.ANY),
            by_step(2, block, half),
            by_step(per_block, slots, few),
            by_step(per_block, few, slots),
            by_step(block, words.shape[1]),
            *[pl.BlockSpec(memory_space=pl.ANY)] * 5,
        ],
        out_specs=[
            pl.BlockSpec(memory_space=pl.ANY),
            by_step(each, width),
            by_step(each, width),
            by_step(each, hidden),
            by_step(each, hidden),
            by_step(each, hidden),
            by_step(block, 1),
            by_step(block, lanes),
            by_step(block, 2 * lanes),
            pl.BlockSpec((2 * lanes, width), lambda i: (0, 0)),
            pl.BlockSpec((lanes, width), lambda i: (0, 0)),
        ],
        out_shape=[
            jax.ShapeDtypeStruct((tokens, width), jnp.bfloat16),
            shape(each, width),
            shape(each, width),
            shape(each, hidden),
            shape(each, hidden),
            shape(each, hidden),
            shape(block, 1, kind=jnp.float32),
            shape(block, lanes),
            shape(block, 2 * lanes),
            jax.ShapeDtypeStruct((2 * lanes, width), jnp.float32),
            jax.ShapeDtypeStruct((lanes, width), jnp.float32),
        ],
        scratch_shapes=[
            *(pltpu.VMEM(w.shape, jnp.bfloat16) for w in (*weights, side_w, side_down)),
            pltpu.VMEM((2, 2 * block, width), jnp.bfloat16),
            pltpu.VMEM((2 * block, lanes), jnp.bfloat16),
            pltpu.VMEM((2 * block, 2 * lanes), jnp.bfloat16),
            pltpu.SemaphoreType.DMA((5,)),
            pltpu.SemaphoreType.DMA((2, 2)),
            *Gather.semaphores(layers),
        ],
        compiler_params=pltpu.CompilerParams(
            collective_id=3, has_side_effects=True, vmem_limit_bytes=62 * 1024 * 1024
        ),
    )(
        rows_own,
        grads.reshape(2, 2, layers, 2, block, half),
        pick.reshape(2, 2, layers, per_block, slots, few),
        spread.reshape(2, 2, layers, per_block, few, slots),
        words.reshape(2, 2, layers, block, -1),
        *weights,
        side_w,
        side_down,
    )
    return outs


def rotate(value, cosine, sine):
    half = value.shape[-1] // 2
    first, second = (value[..., :half], value[..., half:])
    return jnp.concatenate(
        [first * cosine - second * sine, first * sine + second * cosine], axis=-1
    )


def unrotate(value, cosine, sine):
    half = value.shape[-1] // 2
    first, second = (value[..., :half], value[..., half:])
    return jnp.concatenate(
        [first * cosine + second * sine, second * cosine - first * sine], axis=-1
    )


def sequence_layout(lengths_row, group):
    ends = jnp.cumsum(lengths_row)
    starts = ends - lengths_row
    index = jnp.arange(group, dtype=jnp.int32)
    seq_ids = jnp.sum((index[:, None] >= ends[None, :]).astype(jnp.int32), axis=1)
    member = seq_ids[:, None] == jnp.arange(lengths_row.shape[0], dtype=jnp.int32)[None, :]
    begins = jnp.sum(jnp.where(member, starts[None, :], 0), axis=1)
    return (seq_ids, index - begins)


def rotary_tables(places):
    half = ROPE // 2
    freqs = jnp.power(theta_base, -jnp.arange(half, dtype=jnp.float32) * (2.0 / ROPE))
    angle = places.astype(jnp.float32)[..., None] * freqs
    return (jnp.cos(angle), jnp.sin(angle))


def norm_back(value, factor, gain, grad, width):
    weighted = grad * gain
    inner = lax.psum(jnp.sum(weighted * value, axis=1), "col")
    d_value = (
        factor[:, None] * weighted - value * (factor * factor * factor * inner / width)[:, None]
    )
    d_gain = jnp.sum(grad * value * factor[:, None], axis=0)
    return (d_value, d_gain)


def masked_scores(query_block, keys, seq_ids, first, scale):
    size = query_block.shape[0]
    group = keys.shape[0]
    scored = (
        jnp.einsum("qhd,khd->hqk", query_block, keys, preferred_element_type=jnp.float32) * scale
    )
    query_index = first + jnp.arange(size, dtype=jnp.int32)
    key_index = jnp.arange(group, dtype=jnp.int32)
    allowed = (seq_ids[first : first + size][:, None] == seq_ids[None, :group]) & (
        key_index[None, :] <= query_index[:, None]
    )
    return jnp.where(allowed[None, :, :], scored, -1e30)


def own_slice(value, index, axis):
    size = value.shape[axis] // 2
    return lax.dynamic_slice_in_dim(value, index * size, size, axis)


def col_pair(mine, sent, axis):
    received = lax.ppermute(sent, "col", SWAP)
    first = lax.axis_index("col") == 0
    return jnp.where(
        first,
        jnp.concatenate([mine, received], axis=axis),
        jnp.concatenate([received, mine], axis=axis),
    )


def halves(value, split):
    col = lax.axis_index("col")
    return own_slice(value, col, split), own_slice(value, 1 - col, split)


def trade(value, split, join):
    return col_pair(*halves(value, split), join)


def routed_and_shared(
    tok_dev, capacity, layers, router, expert_weights, shared_own, normed_own, grads_own, words
):
    bf16 = jnp.bfloat16
    col_id = lax.axis_index("col")
    own_expert = lax.axis_index("row") * layers + lax.axis_index("exp")
    experts = router.shape[1]
    units = shared_own.shape[1]
    block, half_width = normed_own.shape
    tokens = words.shape[0]
    few = min(tok_dev, block)
    slots = -(-min(capacity, few) // 16) * 16
    blocks = tokens // few

    own_word = lax.dynamic_index_in_dim(words, own_expert // 16, 1, keepdims=False)
    own_pick = (jnp.bitwise_and(lax.shift_right_logical(own_word, own_expert % 16), 1) == 1).reshape(
        blocks, few
    )
    order = jnp.arange(few, dtype=jnp.int32)
    place = dot_nn(own_pick.astype(bf16), (order[:, None] < order[None, :]).astype(bf16)).astype(
        jnp.int32
    )
    places = jnp.arange(slots, dtype=jnp.int32)
    pick = ((place[:, None, :] == places[None, :, None]) & own_pick[:, None, :]).astype(bf16)
    spread = ((place[:, :, None] == places[None, None, :]) & own_pick[:, :, None]).astype(bf16)
    lanes = -(-(units + experts) // 128) * 128
    fill = lambda value, n: jnp.pad(value, ((0, n - value.shape[0]), (0, 0)))
    side_w = jnp.concatenate(
        [fill(jnp.concatenate([shared_own[0], router.T]), lanes), fill(shared_own[1], lanes)]
    )
    side_down = fill(shared_own[2], lanes)

    grads_all = lax.all_gather(grads_own, ("row", "exp", "col"), axis=0)
    grads_all = grads_all.reshape(experts, 2, block, half_width)
    (
        normed_all,
        slot_rows,
        slot_grads,
        hidden,
        d_gate,
        d_up,
        d_gates_all,
        side_hidden,
        d_side,
        grad_side,
        grad_side_down,
    ) = expert_pass(
        layers,
        few,
        slots,
        units,
        experts,
        normed_own,
        grads_all,
        pick,
        spread,
        words,
        expert_weights,
        side_w,
        side_down,
    )
    spread = spread.reshape(2, 2, layers, -1, few, slots)
    gate_weight, up_weight, down_weight = expert_weights
    (d_normed,) = made_scatter(
        (d_gate, d_up), (gate_weight, up_weight), spread, d_side, side_w, (), (), layers, 4
    )
    flat = lambda *values: tuple(value.reshape(-1, value.shape[-1]) for value in values)
    out_parts = (
        (hidden,),
        (down_weight,),
        spread,
        side_hidden,
        side_down,
        flat(d_gate, d_up, hidden),
        flat(slot_rows, slot_rows, slot_grads),
    )
    grad_shared = jnp.stack(
        [grad_side[:units], grad_side[lanes : lanes + units], grad_side_down[:units]]
    )

    d_gates = lax.psum(
        lax.all_to_all(
            d_gates_all.reshape(experts, block), ("row", "exp"), split_axis=0, concat_axis=0, tiled=True
        ),
        "col",
    ).T
    own_probs = jax.nn.softmax(
        dot_nn(lax.dynamic_slice_in_dim(normed_all, own_expert * block, block, 0), router), axis=1
    )
    own_words = lax.dynamic_slice_in_dim(words, own_expert * block, block, 0)
    numbers = jnp.arange(experts, dtype=jnp.int32)
    picks = (
        jnp.bitwise_and(
            lax.shift_right_logical(own_words[:, numbers // 16], (numbers % 16)[None, :]), 1
        )
        == 1
    )
    selected = jnp.where(picks, own_probs, 0.0)
    own_total = jnp.sum(selected, axis=1, keepdims=True)
    own_gates = selected / own_total
    d_selected = (d_gates - jnp.sum(d_gates * own_gates, axis=1, keepdims=True)) / own_total
    d_router_probs = jnp.where(picks, d_selected, 0.0)
    d_logits = own_probs * (
        d_router_probs - jnp.sum(own_probs * d_router_probs, axis=1, keepdims=True)
    )
    router_half = lax.dynamic_slice_in_dim(router, col_id * half_width, half_width, 0)
    grad_router = lax.dot_general(
        normed_own.astype(jnp.float32),
        d_logits,
        (((0,), (0,)), ((), ())),
        precision=lax.Precision.HIGHEST,
        preferred_element_type=jnp.float32,
    )
    d_normed = d_normed + lax.dot_general(
        d_logits,
        router_half.astype(jnp.float32),
        (((1,), (1,)), ((), ())),
        precision=lax.Precision.HIGHEST,
        preferred_element_type=jnp.float32,
    )
    return (d_normed, out_parts, (grad_shared, grad_router))


def per_device(
    layer_input,
    lengths,
    routes,
    norm1_gain,
    w_query,
    w_latent,
    latent_gain,
    w_kv,
    w_out,
    norm2_gain,
    shared_gate,
    shared_up,
    shared_down,
    router,
    expert_gate,
    expert_up,
    expert_down,
    cotangent,
):
    row_id = lax.axis_index("row")
    col_id = lax.axis_index("col")
    exp_id = lax.axis_index("exp")
    rows_n, cols_n, exps_n = (lax.axis_size(name) for name in ("row", "col", "exp"))
    experts = rows_n * exps_n
    own_expert = row_id * exps_n + exp_id
    tok_dev = routes.shape[1]
    topk_count = routes.shape[2]
    capacity = max(2, 3 * tok_dev * topk_count // (2 * experts))
    slots = -(-capacity // 16) * 16
    block, half_width = layer_input.shape
    width = half_width * cols_n
    group = block * rows_n
    tokens = group * exps_n
    heads_here = w_kv.shape[1] // (QK_NOPE + V_DIM)
    head_dim = QK_NOPE + ROPE
    scale = 1.0 / math.sqrt(head_dim)
    query_rows = group // 2
    bf16 = jnp.bfloat16

    query_halves, layer_input = lax.optimization_barrier((halves(w_query, 1), layer_input))
    w_query_own = col_pair(*query_halves, 0)
    seq_ids, places = sequence_layout(lengths[0], group)
    cosine, sine = rotary_tables(places)

    group_input, w_latent_all = gather_several((layer_input, w_latent[0].T), 1, 10, (False, True))
    latent_width, slab = w_latent.shape[2], w_latent.shape[1]
    w_latent_all = w_latent_all.reshape(rows_n, cols_n, latent_width, slab)
    w_latent_all = w_latent_all.transpose(2, 1, 0, 3).reshape(latent_width, width)
    group_input, w_out, cotangent = lax.optimization_barrier((group_input, w_out, cotangent))
    w_out_own = trade(w_out, 0, 1)
    group_input = group_input.astype(jnp.float32)
    factor_group = lax.rsqrt(jnp.mean(group_input * group_input, axis=1) + epsilon)
    normed_group = (group_input * factor_group[:, None] * norm1_gain).astype(bf16)
    query_pre = dot_nn(normed_group, w_query_own).reshape(group, heads_here, head_dim)
    queries = jnp.concatenate(
        [
            query_pre[..., :QK_NOPE],
            rotate(query_pre[..., QK_NOPE:], cosine[:, None, :], sine[:, None, :]),
        ],
        axis=2,
    ).astype(bf16)
    queries, shared_gate, shared_up, shared_down = lax.optimization_barrier(
        (queries, shared_gate, shared_up, shared_down)
    )
    units = shared_gate.shape[1] // (cols_n * exps_n)
    shared_parts = jnp.stack(
        [
            lax.dynamic_index_in_dim(
                part.reshape(cols_n, exps_n, units, half_width), exp_id, 1, keepdims=False
            )
            for part in (shared_gate.T, shared_up.T, shared_down)
        ]
    )
    shared_own = trade(shared_parts, 1, 3)[:, 0]

    latent = dot_nt(normed_group, w_latent_all)
    compressed_raw = latent[:, :KV_RANK]
    kv_factor = lax.rsqrt(jnp.mean(compressed_raw * compressed_raw, axis=1) + epsilon)
    compressed = (compressed_raw * kv_factor[:, None] * latent_gain).astype(bf16)
    rotary_key = rotate(latent[:, KV_RANK:], cosine, sine).astype(bf16)
    key_value = (
        dot_nn(compressed, w_kv).astype(bf16).reshape(group, heads_here, QK_NOPE + V_DIM)
    )
    keys = jnp.concatenate(
        [
            key_value[..., :QK_NOPE],
            jnp.broadcast_to(rotary_key[:, None, :], (group, heads_here, ROPE)),
        ],
        axis=2,
    )
    values = key_value[..., QK_NOPE:]
    block_outputs = []
    block_totals = []
    for first in range(0, group, query_rows):
        last = first + query_rows
        scores = masked_scores(queries[first:last], keys[:last], seq_ids, first, scale)
        highest = jnp.max(scores, axis=2, keepdims=True)
        log_total = highest + jnp.log(jnp.sum(jnp.exp(scores - highest), axis=2, keepdims=True))
        probs_low = jnp.exp(scores - log_total).astype(bf16)
        block_outputs.append(
            jnp.einsum(
                "hqk,khd->qhd", probs_low, values[:last], preferred_element_type=jnp.float32
            ).astype(bf16)
        )
        block_totals.append(log_total)
    attended = jnp.concatenate(block_outputs, axis=0).reshape(group, heads_here * V_DIM)

    input_wide = layer_input.astype(jnp.float32)
    hidden_state = input_wide + scatter(dot_nn(attended, w_out_own).astype(bf16), 1, 2)
    words_n = -(-experts // 16)
    word_of = jnp.arange(words_n, dtype=jnp.int32)[:, None, None]
    bits = jnp.where(routes // 16 == word_of, jnp.left_shift(1, routes % 16), 0)
    bits = jnp.sum(bits, axis=2).astype(jnp.float32)
    padded = -(-tok_dev // 128) * 128
    bits = jnp.pad(bits, ((0, 0), (0, padded - tok_dev)))
    is_here = jnp.arange(experts, dtype=jnp.int32) == own_expert
    bits = jnp.where(is_here[:, None, None], bits[None], 0.0).reshape(experts * words_n, padded)
    bits, hidden_state = lax.optimization_barrier((bits, hidden_state))
    bits = small_sum(bits, exps_n, 8).reshape(experts, words_n, cols_n, padded)[..., :tok_dev]
    words_all = bits.astype(jnp.int32).transpose(0, 2, 3, 1).reshape(tokens, words_n)

    gain_two = lax.dynamic_slice_in_dim(norm2_gain, col_id * half_width, half_width)
    square = lax.psum(jnp.sum(hidden_state * hidden_state, axis=1), "col")
    factor_two = lax.rsqrt(square / width + epsilon)
    normed_two = (hidden_state * factor_two[:, None] * gain_two).astype(bf16)
    pieces = max(1, exps_n // 4)
    feed = functools.partial(
        routed_and_shared,
        tok_dev,
        capacity,
        exps_n,
        router,
        (expert_gate[0].T, expert_up[0].T, expert_down[0].T),
        shared_own,
    )
    if pieces == 1:
        d_normed, out_parts, weight_grads = feed(normed_two, cotangent, words_all)
    else:
        piece_rows = block // pieces

        def one_piece(total, items):
            d_rows, out_parts, grads = feed(*items)
            *out_parts, job_a, job_b = out_parts
            (branch_rows,) = made_scatter(*out_parts, (), (), exps_n, 9)
            grads = (*grads, tuple(dot_tn(a, b) for a, b in zip(job_a, job_b)))
            return (jax.tree.map(jnp.add, total, grads), (d_rows, branch_rows))

        split = lambda value: value.reshape(pieces, piece_rows, half_width)
        word_pieces = words_all.reshape(experts, pieces, piece_rows, words_n)
        items = (
            split(normed_two),
            split(cotangent),
            word_pieces.transpose(1, 0, 2, 3).reshape(pieces, -1, words_n),
        )
        start = (
            jnp.zeros((3, units, width), jnp.float32),
            jnp.zeros((half_width, experts), jnp.float32),
            (jnp.zeros(expert_gate.shape[:0:-1], jnp.float32),) * 3,
        )
        weight_grads, (d_normed, branch) = lax.scan(one_piece, start, items)
        d_normed, branch = (v.reshape(block, half_width) for v in (d_normed, branch))
    grad_shared, grad_router = weight_grads[:2]
    expert_grads = weight_grads[2] if pieces > 1 else None
    grad_shared = trade(grad_shared.astype(bf16)[:, None], 3, 1)
    d_normed, grad_shared = lax.optimization_barrier((d_normed, grad_shared))
    grad_shared = lax.all_gather(grad_shared, "exp", axis=2, tiled=False)
    d_norm_two, grad_gain_two = norm_back(hidden_state, factor_two, gain_two, d_normed, width)
    d_hidden_state = cotangent.astype(jnp.float32) + d_norm_two

    d_branch = gather(d_hidden_state.astype(bf16), 1, 1)
    grad_w_out = trade(dot_tn(attended, d_branch).astype(bf16), 1, 0)
    d_attended = dot_nt(d_branch, w_out_own).astype(bf16).reshape(group, heads_here, V_DIM)
    d_query_blocks = []
    d_keys = jnp.zeros((group, heads_here, head_dim), jnp.float32)
    d_values = jnp.zeros((group, heads_here, V_DIM), jnp.float32)
    for number, first in enumerate(range(0, group, query_rows)):
        last = first + query_rows
        query_block = queries[first:last]
        d_block = d_attended[first:last]
        scores = masked_scores(query_block, keys[:last], seq_ids, first, scale)
        probs = jnp.exp(scores - block_totals[number])
        d_probs = jnp.einsum(
            "qhd,khd->hqk", d_block, values[:last], preferred_element_type=jnp.float32
        )
        delta = jnp.sum(probs * d_probs, axis=2, keepdims=True)
        d_scores = (probs * (d_probs - delta)).astype(bf16)
        d_query_blocks.append(
            jnp.einsum("hqk,khd->qhd", d_scores, keys[:last], preferred_element_type=jnp.float32)
            * scale
        )
        d_keys = d_keys.at[:last].add(
            jnp.einsum("hqk,qhd->khd", d_scores, query_block, preferred_element_type=jnp.float32)
            * scale
        )
        d_values = d_values.at[:last].add(
            jnp.einsum(
                "hqk,qhd->khd", probs.astype(bf16), d_block, preferred_element_type=jnp.float32
            )
        )
    d_query = jnp.concatenate(d_query_blocks, axis=0)
    d_query_pre = (
        jnp.concatenate(
            [
                d_query[..., :QK_NOPE],
                unrotate(d_query[..., QK_NOPE:], cosine[:, None, :], sine[:, None, :]),
            ],
            axis=2,
        )
        .astype(bf16)
        .reshape(group, heads_here * head_dim)
    )
    d_key_value = (
        jnp.concatenate([d_keys[..., :QK_NOPE], d_values], axis=2)
        .astype(bf16)
        .reshape(group, heads_here * (QK_NOPE + V_DIM))
    )
    grad_w_kv = dot_tn(compressed, d_key_value)
    d_latent_sum = scatter(
        jnp.concatenate(
            [dot_nt(d_key_value, w_kv), jnp.sum(d_keys[..., QK_NOPE:], axis=1)], axis=1
        ).astype(bf16),
        1,
        5,
        by_rows=True,
    )
    own_first = (row_id * cols_n + col_id) * (group // (rows_n * cols_n))

    def own_tokens(value):
        return lax.dynamic_slice_in_dim(value, own_first, group // (rows_n * cols_n), 0)

    raw_own, factor_own = own_tokens(compressed_raw), own_tokens(kv_factor)
    d_compressed = d_latent_sum[:, :KV_RANK]
    weighted = d_compressed * latent_gain
    grad_latent_gain = jnp.sum(d_compressed * raw_own * factor_own[:, None], axis=0)
    inner = jnp.sum(weighted * raw_own, axis=1)
    d_raw = (
        factor_own[:, None] * weighted
        - raw_own * (factor_own * factor_own * factor_own * inner / KV_RANK)[:, None]
    )
    d_latent = gather(
        jnp.concatenate(
            [d_raw, unrotate(d_latent_sum[:, KV_RANK:], own_tokens(cosine), own_tokens(sine))],
            axis=1,
        ).astype(bf16),
        1,
        6,
        by_rows=True,
    )
    slab = w_latent.shape[1]
    slab_start = col_id * half_width + row_id * slab
    normed_slab = lax.dynamic_slice_in_dim(normed_group, slab_start, slab, 1)
    grad_w_latent = dot_tn(d_latent, normed_slab)
    grad_w_query = trade(dot_tn(normed_group, d_query_pre).astype(bf16), 0, 1)
    d_gathered = dot_nt(d_query_pre, w_query_own)
    piece = lax.dynamic_slice_in_dim(d_gathered, slab_start, slab, 1) + dot_nt(
        d_latent, w_latent[0]
    )
    d_gathered = lax.dynamic_update_slice_in_dim(d_gathered, piece, slab_start, 1)
    d_first = scatter(d_gathered.astype(bf16), 1, 2)
    gain_one = lax.dynamic_slice_in_dim(norm1_gain, col_id * half_width, half_width)
    factor_one = lax.dynamic_slice_in_dim(factor_group, row_id * block, block)
    d_norm_one, grad_gain_one = norm_back(input_wide, factor_one, gain_one, d_first, width)
    input_grad = d_hidden_state + d_norm_one
    if pieces == 1:
        out_parts, input_grad = lax.optimization_barrier((out_parts, input_grad))
        branch, *expert_grads = made_scatter(*out_parts, exps_n, 9)
    output = (hidden_state + branch).astype(bf16)

    small = jnp.concatenate(
        [
            grad_gain_one[None],
            grad_gain_two[None],
            jnp.pad(grad_latent_gain, (0, half_width - KV_RANK))[None],
            grad_router.T,
        ],
        axis=0,
    )
    small = jnp.pad(small, ((0, -small.shape[0] % 8), (0, 0)))
    small = small_sum(small, exps_n, 7)
    summed_latent_gain = small[2, :KV_RANK] + small[2, half_width : half_width + KV_RANK]

    grad_shared, grad_w_query = lax.optimization_barrier((grad_shared, grad_w_query))
    grad_shared = grad_shared.reshape(3, cols_n * exps_n * units, half_width).astype(jnp.float32)
    summed = lax.psum(
        (grad_w_query, grad_w_latent.astype(bf16), grad_w_kv.astype(bf16), grad_w_out), "exp"
    )
    return (
        output,
        input_grad,
        small[0],
        summed[0].astype(jnp.float32),
        summed[1].T.astype(jnp.float32)[None],
        summed_latent_gain,
        summed[2].astype(jnp.float32),
        summed[3].astype(jnp.float32),
        small[1],
        grad_shared[0].T,
        grad_shared[1].T,
        grad_shared[2],
        small[3 : 3 + experts].T,
        *(grad.T[None] for grad in expert_grads),
    )


def solution(mesh):
    placed = (
        P(("row", "exp"), "col"),
        P("exp", None),
        P("col", ("row", "exp"), None),
        P(),
        P("col", "row"),
        P("col", "row", None),
        P(),
        P(None, ("row", "col")),
        P("row", "col"),
        P(),
        P("col", "row"),
        P("col", "row"),
        P("row", "col"),
        P(),
        P(("row", "exp"), None, "col"),
        P(("row", "exp"), None, "col"),
        P(("row", "exp"), None, "col"),
        P(("row", "exp"), "col"),
    )
    return jax.shard_map(
        per_device,
        mesh=mesh,
        in_specs=placed,
        out_specs=(
            P(("row", "exp"), "col"),
            P(("row", "exp"), "col"),
            P(),
            P("col", "row"),
            P("col", "row", None),
            P(),
            P(None, ("row", "col")),
            P("row", "col"),
            P(),
            P("col", "row"),
            P("col", "row"),
            P("row", "col"),
            P(),
            P(("row", "exp"), None, "col"),
            P(("row", "exp"), None, "col"),
            P(("row", "exp"), None, "col"),
        ),
        check_vma=False,
    )
```

```python
import functools
import math

import jax
import jax.numpy as jnp
from jax import lax
from jax.experimental import pallas as pl
from jax.experimental.pallas import tpu as pltpu
from jax.sharding import PartitionSpec as P

QK_NOPE = 128
ROPE = 64
KV_RANK = 512
V_DIM = 128

epsilon = 1e-06
theta_base = 10000.0
SWAP = [(0, 1), (1, 0)]


MESH = pl.DeviceIdType.MESH


class Place:
    def __init__(self, layers):
        self.layers = layers
        self.row, self.col = lax.axis_index("row"), lax.axis_index("col")
        self.layer = lax.axis_index("exp") if layers > 1 else 0
        self.core = lax.rem(self.row, 2)
        self.x_row = lax.rem(self.row + 2, 4)
        self.core_row = self.row + 1 - 2 * self.core
        self.y_col = 1 - self.col
        self.to_x = {"row": self.x_row}
        self.to_y = {"col": self.y_col}
        self.to_core = {"row": self.core_row}
        self.above = {"exp": self.layer + 1}
        self.below = {"exp": self.layer - 1}

    def greet(self):
        barrier = pltpu.get_barrier_semaphore()
        for target in (self.to_x, self.to_y, self.to_core):
            pl.semaphore_signal(barrier, inc=1, device_id=target, device_id_type=MESH)
        if self.layers > 1:

            @pl.when(self.layer > 0)
            def _():
                pl.semaphore_signal(barrier, inc=1, device_id=self.below, device_id_type=MESH)

            @pl.when(self.layer < self.layers - 1)
            def _():
                pl.semaphore_signal(barrier, inc=1, device_id=self.above, device_id_type=MESH)

        peers = 3
        if self.layers > 1:
            peers = peers + jnp.where(self.layer > 0, 1, 0) + jnp.where(self.layer < self.layers - 1, 1, 0)
        pl.semaphore_wait(barrier, peers)


def remote(src, dst, send, recv, target):
    return pltpu.make_async_remote_copy(
        src_ref=src, dst_ref=dst, send_sem=send, recv_sem=recv, device_id=target, device_id_type=MESH
    )


def first_part(rows):
    return (rows // 2 + 15) // 16 * 16


def piece_of(where, layers, shape, by_rows, row, col, layer, span=None):
    rows, width = shape
    start, size = (0, rows) if span is None else span
    if by_rows:
        first = pl.multiple_of((row * 2 + col) * rows + start, 16)
        return where.at[pl.ds(first, size)]
    first = pl.multiple_of((row * layers + layer) * rows + start, 16)
    return where.at[pl.ds(first, size), pl.ds(pl.multiple_of(col * width, 128), width)]


class Gather:
    def __init__(self, me, layers, by_rows, shape, held, sems):
        self.me, self.layers, self.by_rows, self.shape, self.held = me, layers, by_rows, shape, held
        self.up_send, self.down_send, self.z_recv = sems[:3]
        self.send, self.recv, self.diag_send, self.diag_recv = sems[3:]
        part = first_part(shape[0])
        self.spans = ((0, part), (part, shape[0] - part))
        self.owners = (
            (me.row, me.col),
            (me.x_row, me.col),
            (me.row, me.y_col),
            (me.x_row, me.y_col),
        )
        self.sides = (me.to_x, me.to_y)

    @staticmethod
    def semaphores(layers):
        dma = pltpu.SemaphoreType.DMA
        line = [dma((layers,)) for _ in range(3)]
        return [*line, dma((5, 4, layers)), dma((5, 4, layers)), dma((2, layers)), dma((2, layers))]

    def area(self, where, row, col, layer, span=None):
        return piece_of(where, self.layers, self.shape, self.by_rows, row, col, layer, span)

    def piece(self, kind, layer, span=None):
        return self.area(self.held, *self.owners[kind], layer, span)

    def partner_piece(self, where, kind, layer):
        row, col = self.owners[kind]
        return self.area(where, row + 1 - 2 * self.me.core, col, layer)

    def to_core(self, kind, layer):
        piece = self.piece(kind, layer)
        sems = (4, kind, layer)
        return remote(piece, piece, self.send.at[sems], self.recv.at[sems], self.me.to_core)

    def from_core(self, kind, layer):
        piece = self.partner_piece(self.held, kind, layer)
        sems = (4, kind, layer)
        return remote(piece, piece, self.send.at[sems], self.recv.at[sems], self.me.to_core)

    def beside(self, axis, half, layer, incoming=False):
        piece = self.piece(axis + 1 if incoming else 0, layer, self.spans[half])
        sems = (2 * axis + half, 0, layer)
        return remote(piece, piece, self.send.at[sems], self.recv.at[sems], self.sides[axis])

    def corner(self, axis, layer, incoming=False):
        piece = self.piece(3 if incoming else axis + 1, layer, self.spans[axis])
        sems = (axis, layer)
        return remote(
            piece, piece, self.diag_send.at[sems], self.diag_recv.at[sems], self.sides[1 - axis]
        )

    def along(self, up, layer):
        piece = self.piece(0, layer)
        return remote(
            piece,
            piece,
            (self.up_send if up else self.down_send).at[layer],
            self.z_recv.at[layer],
            self.me.above if up else self.me.below,
        )

    def pass_on(self, up, layer):
        me = self.me

        @pl.when((me.layer < self.layers - 1) if up else (me.layer > 0))
        def _():
            self.along(up, layer).start()

    def spread(self, layer):
        self.beside(0, 0, layer).start()
        self.beside(1, 1, layer).start()
        self.beside(0, 1, layer).start()
        self.beside(1, 0, layer).start()
        self.to_core(0, layer).start()

    def begin(self):
        if self.layers > 1:
            self.pass_on(True, self.me.layer)
            self.pass_on(False, self.me.layer)
        self.spread(self.me.layer)

    def at_distance(self, distance, act):
        me = self.me
        if distance == 0:
            act(me.layer, None)
            return

        @pl.when(me.layer >= distance)
        def _():
            act(me.layer - distance, True)

        @pl.when(me.layer + distance < self.layers)
        def _():
            act(me.layer + distance, False)

    def arrived(self, layer, upward):
        self.along(upward, layer).wait_recv()
        self.pass_on(upward, layer)
        self.spread(layer)

    def second(self, layer):
        for axis in (0, 1):
            self.beside(axis, axis, layer, True).wait_recv()
            self.corner(axis, layer).start()
        for axis in (0, 1):
            self.beside(axis, 1 - axis, layer, True).wait_recv()
            self.to_core(axis + 1, layer).start()

    def third(self, layer):
        for axis in (0, 1):
            self.corner(axis, layer, True).wait_recv()
        self.to_core(3, layer).start()

    def finish(self):
        me, layers = self.me, self.layers
        for layer in range(layers):
            for kind in range(4):
                self.to_core(kind, layer).wait_send()
            for axis in (0, 1):
                for half in (0, 1):
                    self.beside(axis, half, layer).wait_send()
                self.corner(axis, layer).wait_send()
        if layers > 1:
            for layer in range(layers):

                @pl.when((me.layer < layers - 1) & (layer <= me.layer))
                def _():
                    self.along(True, layer).wait_send()

                @pl.when((me.layer > 0) & (layer >= me.layer))
                def _():
                    self.along(False, layer).wait_send()


def gather_body(layers, by_rows, *refs):
    count = len(by_rows)
    me = Place(layers)
    srcs, outs, refs = refs[:count], refs[count : 2 * count], refs[2 * count :]
    works, stores = [], []
    for i in range(count):
        held, store_sem, *sems = refs[9 * i : 9 * i + 9]
        works.append(Gather(me, layers, by_rows[i], srcs[i].shape, held, sems))

        def store(kind, layer, partner, work=works[i], out=outs[i], store_sem=store_sem):
            if partner:
                pair = (
                    work.partner_piece(work.held, kind, layer),
                    work.partner_piece(out, kind, layer),
                )
            else:
                pair = (work.piece(kind, layer), work.area(out, *work.owners[kind], layer))
            return pltpu.make_async_copy(*pair, store_sem.at[1 if partner else 0, kind, layer])

        stores.append(store)
    own = [
        pltpu.make_async_copy(src, work.piece(0, me.layer), refs[9 * i + 1].at[0, 0, me.layer])
        for i, (src, work) in enumerate(zip(srcs, works))
    ]
    for copy in own:
        copy.start()
    me.greet()
    for copy, work, store in zip(own, works, stores):
        copy.wait()
        work.begin()
        store(0, me.layer, False).start()

    def arrived(layer, upward):
        for work, store in zip(works, stores):
            work.arrived(layer, upward)
            store(0, layer, False).start()

    def second(layer, upward):
        for work, store in zip(works, stores):
            work.second(layer)
            for kind in (1, 2):
                store(kind, layer, False).start()

    def third(layer, upward):
        for work, store in zip(works, stores):
            work.third(layer)
            store(3, layer, False).start()
            for kind in range(4):
                work.from_core(kind, layer).wait_recv()
                store(kind, layer, True).start()

    for step in range(1, layers + 2):
        if step < layers:
            works[0].at_distance(step, arrived)
        if step - 1 < layers:
            works[0].at_distance(step - 1, second)
        if 0 <= step - 2 < layers:
            works[0].at_distance(step - 2, third)
    for work, store in zip(works, stores):
        for layer in range(layers):
            for kind in range(4):
                store(kind, layer, False).wait()
                store(kind, layer, True).wait()
        work.finish()


def gather(value, layers, collective_id, by_rows=False):
    return gather_several((value,), layers, collective_id, (by_rows,))[0]


def gather_several(values, layers, collective_id, by_rows):
    dma = pltpu.SemaphoreType.DMA
    shapes, scratch = [], []
    for value, rows_only in zip(values, by_rows):
        rows, width = value.shape
        shapes.append((8 * rows, width) if rows_only else (4 * layers * rows, 2 * width))
        scratch += [
            pltpu.VMEM(shapes[-1], value.dtype),
            dma((2, 4, layers)),
            *Gather.semaphores(layers),
        ]
    in_hbm = pl.BlockSpec(memory_space=pl.ANY)
    return pl.pallas_call(
        functools.partial(gather_body, layers, by_rows),
        out_shape=[
            jax.ShapeDtypeStruct(shape, value.dtype) for shape, value in zip(shapes, values)
        ],
        in_specs=[in_hbm] * len(values),
        out_specs=[in_hbm] * len(values),
        scratch_shapes=scratch,
        compiler_params=pltpu.CompilerParams(
            collective_id=collective_id,
            has_side_effects=True,
            vmem_limit_bytes=56 * 1024 * 1024,
        ),
    )(*values)


def scatter_body(
    layers,
    by_rows,
    src,
    out,
    acc,
    core_in,
    diag_a,
    diag_b,
    side_in,
    line_in,
    load_sem,
    core_send,
    core_recv,
    diag_send,
    diag_recv,
    side_send,
    side_recv,
    line_send,
    line_recv,
):
    me = Place(layers)
    rows, width = out.shape
    part = first_part(rows)
    owners = (
        (me.row, me.col),
        (me.x_row, me.col),
        (me.row, me.y_col),
        (me.x_row, me.y_col),
    )

    def layer_at(step):
        if layers == 1:
            return 0
        found = 0
        for layer in range(layers):
            order = sorted(range(layers), key=lambda other: (-abs(other - layer), -other))
            found = found + jnp.where(me.layer == layer, order[step], 0)
        return found

    layer_of = [layer_at(step) for step in range(layers)]

    def area(row, col, layer):
        return piece_of(src, layers, (rows, width), by_rows, row, col, layer)

    def load(step, kind):
        return pltpu.make_async_copy(
            area(*owners[kind], layer_of[step]), acc.at[step, kind], load_sem.at[step, kind]
        )

    def to_core(step, kind):
        row, col = owners[kind]
        return remote(
            area(row + 1 - 2 * me.core, col, layer_of[step]),
            core_in.at[step, kind],
            core_send.at[step, kind],
            core_recv.at[step, kind],
            me.to_core,
        )

    def diag(step, axis):
        start, size = ((0, part), (part, rows - part))[axis]
        return remote(
            acc.at[step, 3, pl.ds(start, size)],
            (diag_a, diag_b)[axis].at[step],
            diag_send.at[axis, step],
            diag_recv.at[axis, step],
            (me.to_y, me.to_x)[axis],
        )

    def side(step, axis):
        return remote(
            acc.at[step, axis + 1],
            side_in.at[axis, step],
            side_send.at[axis, step],
            side_recv.at[axis, step],
            (me.to_x, me.to_y)[axis],
        )

    def line(step, up):
        layer = layer_of[step]
        way = 0 if up else 1
        return remote(
            acc.at[step, 0],
            line_in.at[way, layer],
            line_send.at[step],
            line_recv.at[way, layer],
            me.above if up else me.below,
        )

    lanes = 32 if part % 32 == 0 and rows % 32 == 0 else 16

    def add(target, others, start=0, size=rows, into=None):
        def step(i, carry):
            first = pl.multiple_of(i * lanes, 16)
            total = target[pl.ds(start + first, lanes), :].astype(jnp.float32)
            for other in others:
                total = total + other[pl.ds(first, lanes), :].astype(jnp.float32)
            if into is None:
                target[pl.ds(start + first, lanes), :] = total.astype(target.dtype)
            else:
                into[pl.ds(first, lanes), :] = total.astype(into.dtype)
            return carry

        lax.fori_loop(0, size // lanes, step, 0)

    me.greet()
    kinds = (3, 1, 2, 0)
    for step in range(layers):
        for kind in kinds:
            to_core(step, kind).start()
            load(step, kind).start()

    def ready(step, kind):
        load(step, kind).wait()
        to_core(step, kind).wait_recv()

    def stage_a(step):
        ready(step, 3)
        add(acc.at[step, 3], [core_in.at[step, 3]])
        diag(step, 0).start()
        diag(step, 1).start()

    def stage_b(step):
        for axis, buffer, start, size in (
            (0, diag_a, 0, part),
            (1, diag_b, part, rows - part),
        ):
            kind = axis + 1
            ready(step, kind)
            add(acc.at[step, kind], [core_in.at[step, kind]])
            diag(step, axis).wait_recv()
            add(acc.at[step, kind], [buffer.at[step]], start, size)
            side(step, axis).start()

    def stage_c(step):
        ready(step, 0)
        side(step, 0).wait_recv()
        side(step, 1).wait_recv()
        parts = [core_in.at[step, 0], side_in.at[0, step], side_in.at[1, step]]
        if layers == 1:
            add(acc.at[step, 0], parts, into=out)
            return
        add(acc.at[step, 0], parts)
        layer = layer_of[step]
        if step < layers - 1:

            @pl.when((layer > me.layer) & (me.layer > 0))
            def _():
                line(step, True).wait_recv()
                add(acc.at[step, 0], [line_in.at[0, layer]])

            @pl.when((layer < me.layer) & (me.layer < layers - 1))
            def _():
                line(step, False).wait_recv()
                add(acc.at[step, 0], [line_in.at[1, layer]])

            @pl.when(layer > me.layer)
            def _():
                line(step, True).start()

            @pl.when(layer < me.layer)
            def _():
                line(step, False).start()
        else:
            inner = (me.layer > 0) & (me.layer < layers - 1)

            @pl.when(me.layer > 0)
            def _():
                line(step, True).wait_recv()

            @pl.when(me.layer < layers - 1)
            def _():
                line(step, False).wait_recv()

            @pl.when(inner)
            def _():
                add(acc.at[step, 0], [line_in.at[0, layer], line_in.at[1, layer]], into=out)

            @pl.when(me.layer == 0)
            def _():
                add(acc.at[step, 0], [line_in.at[1, layer]], into=out)

            @pl.when(me.layer == layers - 1)
            def _():
                add(acc.at[step, 0], [line_in.at[0, layer]], into=out)

    for step in range(layers + 2):
        if step < layers:
            stage_a(step)
        if 0 <= step - 1 < layers:
            stage_b(step - 1)
        if 0 <= step - 2 < layers:
            stage_c(step - 2)
    for step in range(layers):
        for kind in kinds:
            to_core(step, kind).wait_send()
        for axis in (0, 1):
            diag(step, axis).wait_send()
            side(step, axis).wait_send()
        if step < layers - 1:

            @pl.when(layer_of[step] > me.layer)
            def _():
                line(step, True).wait_send()

            @pl.when(layer_of[step] < me.layer)
            def _():
                line(step, False).wait_send()


def scatter(value, layers, collective_id, by_rows=False):
    if by_rows:
        rows, width = value.shape[0] // 8, value.shape[1]
    else:
        rows, width = value.shape[0] // (4 * layers), value.shape[1] // 2
    part = first_part(rows)
    dma = pltpu.SemaphoreType.DMA
    buffer = lambda *lead: pltpu.VMEM((*lead, rows, width), value.dtype)
    return pl.pallas_call(
        functools.partial(scatter_body, layers, by_rows),
        out_shape=jax.ShapeDtypeStruct((rows, width), jnp.float32),
        in_specs=[pl.BlockSpec(memory_space=pl.ANY)],
        out_specs=pl.BlockSpec(memory_space=pltpu.VMEM),
        scratch_shapes=[
            buffer(layers, 4),
            buffer(layers, 4),
            pltpu.VMEM((layers, part, width), value.dtype),
            pltpu.VMEM((layers, rows - part, width), value.dtype),
            buffer(2, layers),
            buffer(2, layers),
            dma((layers, 4)),
            dma((layers, 4)),
            dma((layers, 4)),
            dma((2, layers)),
            dma((2, layers)),
            dma((2, layers)),
            dma((2, layers)),
            dma((layers,)),
            dma((2, layers)),
        ],
        compiler_params=pltpu.CompilerParams(
            collective_id=collective_id,
            has_side_effects=True,
            vmem_limit_bytes=56 * 1024 * 1024,
        ),
    )(value)


def dot_nn(left, right):
    return jnp.dot(left, right, preferred_element_type=jnp.float32)


def dot_nt(left, right):
    return lax.dot_general(
        left, right, (((1,), (1,)), ((), ())), preferred_element_type=jnp.float32
    )


def dot_tn(left, right):
    return lax.dot_general(
        left, right, (((0,), (0,)), ((), ())), preferred_element_type=jnp.float32
    )


def made_scatter_body(layers, parts, jobs, *refs):
    slots_hbm, refs = refs[:parts], refs[parts:]
    weights_hbm, refs = refs[:parts], refs[parts:]
    spread_hbm, side_hbm, side_w_hbm, refs = *refs[:3], refs[3:]
    job_a, job_b, refs = refs[:jobs], refs[jobs : 2 * jobs], refs[2 * jobs :]
    out, job_out, refs = refs[0], refs[1 : 1 + jobs], refs[1 + jobs :]
    if jobs:
        job_acc, a_in, b_in, job_sem, flush_sem, refs = *refs[:5], refs[5:]
    slots_in, refs = refs[:parts], refs[parts:]
    weights, refs = refs[:parts], refs[parts:]
    spread_in, side_in, side_w, slot_rows, refs = *refs[:4], refs[4:]
    core_out, acc, core_in, diag_a, diag_b, beside_in, line_in, refs = *refs[:7], refs[7:]
    in_sem, weight_sem, core_send, core_recv, diag_send, diag_recv, side_send, side_recv = refs[:8]
    line_send, line_recv = refs[8:]
    me = Place(layers)
    rows, width = out.shape
    part = first_part(rows)
    f32 = jnp.float32
    per_block, few, slots = spread_in.shape[2:]
    x_mine = me.row // 2

    def layer_at(step):
        return nearest_first(layers, layers - 1 - step, me.layer)

    def loads(unit):
        step, own = unit // 2, lax.rem(unit, 2)
        core = me.core * own + (1 - me.core) * (1 - own)
        slot = lax.rem(unit, 2)
        layer = layer_at(step)
        pairs = [*zip(slots_hbm, slots_in), (spread_hbm, spread_in), (side_hbm, side_in)]
        return [
            pltpu.make_async_copy(
                src.at[x_mine if x == 0 else 1 - x_mine, core, layer],
                dst.at[slot, x],
                in_sem.at[slot, i, x],
            )
            for i, (src, dst) in enumerate(pairs)
            for x in range(2)
        ]

    def weight_loads():
        pairs = [*zip(weights_hbm, weights), (side_w_hbm, side_w)]
        copies = []
        for i, (src, dst) in enumerate(pairs):
            for at, col in enumerate((me.col, me.y_col)):
                copies.append(
                    pltpu.make_async_copy(
                        src.at[:, pl.ds(pl.multiple_of(col * width, 128), width)],
                        dst.at[:, pl.ds(at * width, width)],
                        weight_sem.at[i, at],
                    )
                )
        return copies

    def make(unit, put):
        for copy in loads(unit):
            copy.wait()

        @pl.when(unit + 1 < 2 * layers)
        def _():
            for copy in loads(unit + 1):
                copy.start()

        slot = lax.rem(unit, 2)
        total = sum(
            dot_nn(value[slot].reshape(-1, value.shape[-1]), weight[...])
            for value, weight in zip(slots_in, weights)
        )
        slot_rows[...] = total.astype(slot_rows.dtype)
        for x in range(2):
            for j in range(per_block):
                there = pl.ds(j * few, few)
                here = pl.ds((x * per_block + j) * slots, slots)
                made = dot_nn(spread_in[slot, x, j], slot_rows[here, :]) + dot_nn(
                    side_in[slot, x, there, :], side_w[...]
                )
                put(x, there, made[:, :width].astype(acc.dtype))
                put(x + 2, there, made[:, width:].astype(acc.dtype))

    def to_core(step, kind):
        return remote(
            core_out.at[lax.rem(step, 2), kind],
            core_in.at[step, kind],
            core_send.at[step, kind],
            core_recv.at[step, kind],
            me.to_core,
        )

    def diag(step, axis):
        start, size = ((0, part), (part, rows - part))[axis]
        return remote(
            acc.at[step, 3, pl.ds(start, size)],
            (diag_a, diag_b)[axis].at[step],
            diag_send.at[axis, step],
            diag_recv.at[axis, step],
            (me.to_y, me.to_x)[axis],
        )

    def side(step, axis):
        return remote(
            acc.at[step, axis + 1],
            beside_in.at[axis, step],
            side_send.at[axis, step],
            side_recv.at[axis, step],
            (me.to_x, me.to_y)[axis],
        )

    def line(step, up):
        layer = layer_at(step)
        way = 0 if up else 1
        return remote(
            acc.at[step, 0],
            line_in.at[way, layer],
            line_send.at[step],
            line_recv.at[way, layer],
            me.above if up else me.below,
        )

    lanes = 32 if part % 32 == 0 and rows % 32 == 0 else 16

    def add(target, others, start=0, size=rows, into=None):
        def step(i, carry):
            first = pl.multiple_of(i * lanes, 16)
            total = target[pl.ds(start + first, lanes), :].astype(f32)
            for other in others:
                total = total + other[pl.ds(first, lanes), :].astype(f32)
            if into is None:
                target[pl.ds(start + first, lanes), :] = total.astype(target.dtype)
            else:
                into[pl.ds(first, lanes), :] = total.astype(into.dtype)
            return carry

        lax.fori_loop(0, size // lanes, step, 0)

    turns = layers + 2
    chunk = a_in.shape[1] if jobs else 0
    chunks = job_a[0].shape[0] // chunk if jobs else 0

    def job_loads(unit, job):
        slot = lax.rem(unit, 2)
        here = pl.ds(pl.multiple_of(lax.rem(unit, turns) * chunk, 16), chunk)
        return [
            pltpu.make_async_copy(src.at[here], dst.at[slot], job_sem.at[slot, i])
            for i, (src, dst) in enumerate(((job_a[job], a_in), (job_b[job], b_in)))
        ]

    def start_job_loads(unit):
        for job in range(jobs):

            @pl.when((unit // turns == job) & (lax.rem(unit, turns) < chunks))
            def _():
                for copy in job_loads(unit, job):
                    copy.start()

    def flush(job):
        return pltpu.make_async_copy(job_acc, job_out[job], flush_sem)

    def job_turn(unit):
        if not jobs:
            return
        at = lax.rem(unit, turns)
        slot = lax.rem(unit, 2)

        @pl.when(unit + 1 < jobs * turns)
        def _():
            start_job_loads(unit + 1)

        @pl.when((at == 0) & (unit > 0))
        def _():
            flush(0).wait()

        @pl.when(at == 0)
        def _():
            job_acc[...] = jnp.zeros_like(job_acc)

        @pl.when(at < chunks)
        def _():
            for copy in job_loads(unit, 0):
                copy.wait()
            left = a_in[slot].T
            for first in range(0, 2 * width, width // 2):
                here = pl.ds(first, width // 2)
                job_acc[:, here] += dot_nn(left, b_in[slot, :, here])

        for job in range(jobs):

            @pl.when((at == chunks - 1) & (unit // turns == job))
            def _():
                flush(job).start()

    for copy in (*weight_loads(), *loads(0)):
        copy.start()
    if jobs:
        start_job_loads(0)
    me.greet()
    for copy in weight_loads():
        copy.wait()

    def produce(step):
        @pl.when(step >= 2)
        def _():
            for kind in range(4):
                to_core(step - 2, kind).wait_send()

        half = lax.rem(step, 2)

        def to_other(kind, there, value):
            core_out[half, kind, there, :] = value

        make(2 * step, to_other)
        for kind in (3, 1, 2, 0):
            to_core(step, kind).start()

        def to_own(kind, there, value):
            acc[step, kind, there, :] = value

        make(2 * step + 1, to_own)

    def stage_a(step):
        to_core(step, 3).wait_recv()
        add(acc.at[step, 3], [core_in.at[step, 3]])
        diag(step, 0).start()
        diag(step, 1).start()

    def stage_b(step):
        for axis, buffer, start, size in (
            (0, diag_a, 0, part),
            (1, diag_b, part, rows - part),
        ):
            kind = axis + 1
            to_core(step, kind).wait_recv()
            add(acc.at[step, kind], [core_in.at[step, kind]])
            diag(step, axis).wait_recv()
            add(acc.at[step, kind], [buffer.at[step]], start, size)
            side(step, axis).start()

    def stage_c(step):
        to_core(step, 0).wait_recv()
        side(step, 0).wait_recv()
        side(step, 1).wait_recv()
        add(acc.at[step, 0], [core_in.at[step, 0], beside_in.at[0, step], beside_in.at[1, step]])
        layer = layer_at(step)

        @pl.when((layer > me.layer) & (me.layer > 0))
        def _():
            line(step, True).wait_recv()
            add(acc.at[step, 0], [line_in.at[0, layer]])

        @pl.when((layer < me.layer) & (me.layer < layers - 1))
        def _():
            line(step, False).wait_recv()
            add(acc.at[step, 0], [line_in.at[1, layer]])

        @pl.when(layer > me.layer)
        def _():
            line(step, True).start()

        @pl.when(layer < me.layer)
        def _():
            line(step, False).start()

    def stages(step, carry):
        @pl.when(step < layers)
        def _():
            produce(step)
            stage_a(step)

        job_turn(3 * step)

        @pl.when((step >= 1) & (step <= layers))
        def _():
            stage_b(step - 1)

        job_turn(3 * step + 1)

        @pl.when(step >= 2)
        def _():
            stage_c(step - 2)

        job_turn(3 * step + 2)
        return carry

    lax.fori_loop(0, layers + 2, stages, 0)
    last = layers - 1

    @pl.when(me.layer > 0)
    def _():
        line(last, True).wait_recv()

    @pl.when(me.layer < last)
    def _():
        line(last, False).wait_recv()

    @pl.when((me.layer > 0) & (me.layer < last))
    def _():
        add(acc.at[last, 0], [line_in.at[0, me.layer], line_in.at[1, me.layer]], into=out)

    @pl.when(me.layer == 0)
    def _():
        add(acc.at[last, 0], [line_in.at[1, me.layer]], into=out)

    @pl.when(me.layer == last)
    def _():
        add(acc.at[last, 0], [line_in.at[0, me.layer]], into=out)

    if jobs:
        flush(0).wait()
    for step in range(layers):
        if step >= layers - 2:
            for kind in range(4):
                to_core(step, kind).wait_send()
        for axis in (0, 1):
            diag(step, axis).wait_send()
            side(step, axis).wait_send()
        if step < last:

            @pl.when(layer_at(step) > me.layer)
            def _():
                line(step, True).wait_send()

            @pl.when(layer_at(step) < me.layer)
            def _():
                line(step, False).wait_send()


def made_scatter(slots_in, weights, spread, side, side_w, job_a, job_b, layers, collective_id):
    block, width = side.shape[3], side_w.shape[1] // 2
    bf16, f32 = jnp.bfloat16, jnp.float32
    parts, jobs = len(weights), len(job_a)
    part = first_part(block)
    dma = pltpu.SemaphoreType.DMA
    buffer = lambda *lead: pltpu.VMEM((*lead, block, width), bf16)
    ahead = lambda value: pltpu.VMEM((2, 2, *value.shape[3:]), bf16)
    in_hbm = pl.BlockSpec(memory_space=pl.ANY)
    job_shapes, job_scratch = [], []
    if jobs:
        rows, tall, wide = *job_a[0].shape, job_b[0].shape[1]
        chunks = max(n for n in range(1, layers + 3) if rows % (16 * n) == 0)
        job_shapes = [jax.ShapeDtypeStruct((tall, wide), f32)] * jobs
        job_scratch = [
            pltpu.VMEM((tall, wide), f32),
            pltpu.VMEM((2, rows // chunks, tall), bf16),
            pltpu.VMEM((2, rows // chunks, wide), bf16),
            dma((2, 2)),
            dma,
        ]
    return pl.pallas_call(
        functools.partial(made_scatter_body, layers, parts, jobs),
        out_shape=[jax.ShapeDtypeStruct((block, width), f32), *job_shapes],
        in_specs=[in_hbm] * (2 * parts + 3 + 2 * jobs),
        out_specs=[pl.BlockSpec(memory_space=pltpu.VMEM), *[in_hbm] * jobs],
        scratch_shapes=[
            *job_scratch,
            *(ahead(value) for value in slots_in),
            *(pltpu.VMEM(value.shape, bf16) for value in weights),
            ahead(spread),
            ahead(side),
            pltpu.VMEM(side_w.shape, bf16),
            pltpu.VMEM((2 * slots_in[0].shape[3], 2 * width), bf16),
            buffer(2, 4),
            buffer(layers, 4),
            buffer(layers, 4),
            pltpu.VMEM((layers, part, width), bf16),
            pltpu.VMEM((layers, block - part, width), bf16),
            buffer(2, layers),
            buffer(2, layers),
            dma((2, parts + 2, 2)),
            dma((parts + 1, 2)),
            dma((layers, 4)),
            dma((layers, 4)),
            dma((2, layers)),
            dma((2, layers)),
            dma((2, layers)),
            dma((2, layers)),
            dma((layers,)),
            dma((2, layers)),
        ],
        compiler_params=pltpu.CompilerParams(
            collective_id=collective_id,
            has_side_effects=True,
            vmem_limit_bytes=62 * 1024 * 1024,
        ),
    )(*slots_in, *weights, spread, side, side_w, *job_a, *job_b)


def small_sum_body(layers, src, out, core_in, mid, x_in, near, line_in, total, send, recv, line_send, line_recv):
    me = Place(layers)
    width = src.shape[1]
    barrier = pltpu.get_barrier_semaphore()
    for target in (me.to_x, me.to_y, me.to_core):
        pl.semaphore_signal(barrier, inc=1, device_id=target, device_id_type=MESH)
    for step in range(1, layers):
        other = {"exp": lax.rem(me.layer + step, layers)}
        pl.semaphore_signal(barrier, inc=1, device_id=other, device_id_type=MESH)
    pl.semaphore_wait(barrier, 3 + layers - 1)
    swap = remote(src, core_in, send.at[0], recv.at[0], me.to_core)
    swap.start()
    swap.wait()
    mid[...] = src[...] + core_in[...]
    swap = remote(mid, x_in, send.at[1], recv.at[1], me.to_x)
    swap.start()
    swap.wait()
    near[...] = mid[...] + x_in[...]
    line_in[me.layer] = near[...]

    def along(step, incoming):
        layer = lax.rem(me.layer + (layers - step if incoming else 0), layers)
        return remote(
            near,
            line_in.at[layer],
            line_send.at[step],
            line_recv.at[step],
            {"exp": lax.rem(me.layer + step, layers)},
        )

    for step in range(1, layers):
        along(step, False).start()
    for step in range(1, layers):
        along(step, True).wait_recv()
    summed = line_in[0]
    for layer in range(1, layers):
        summed = summed + line_in[layer]
    total[...] = summed
    mine = pl.ds(pl.multiple_of(me.col * width, 128), width)
    theirs = pl.ds(pl.multiple_of(me.y_col * width, 128), width)
    out[:, mine] = summed
    remote(total, out.at[:, mine], send.at[2], recv.at[2], me.to_y).start()
    remote(total, out.at[:, theirs], send.at[2], recv.at[2], me.to_y).wait()
    for step in range(1, layers):
        along(step, False).wait_send()


def small_sum(value, layers, collective_id):
    rows, width = value.shape
    dma = pltpu.SemaphoreType.DMA
    buffer = lambda *lead: pltpu.VMEM((*lead, rows, width), value.dtype)
    in_vmem = pl.BlockSpec(memory_space=pltpu.VMEM)
    return pl.pallas_call(
        functools.partial(small_sum_body, layers),
        out_shape=jax.ShapeDtypeStruct((rows, 2 * width), value.dtype),
        in_specs=[in_vmem],
        out_specs=in_vmem,
        scratch_shapes=[
            buffer(),
            buffer(),
            buffer(),
            buffer(),
            buffer(layers),
            buffer(),
            dma((3,)),
            dma((3,)),
            dma((layers,)),
            dma((layers,)),
        ],
        compiler_params=pltpu.CompilerParams(
            collective_id=collective_id,
            has_side_effects=True,
            vmem_limit_bytes=32 * 1024 * 1024,
        ),
    )(value)


class PairGather(Gather):
    def area(self, where, row, col, layer, span=None):
        rows, width = self.shape
        start, size = (0, rows) if span is None else span
        at = (row // 2 * self.layers + layer) * 2 + lax.rem(row, 2)
        first = pl.multiple_of(at * rows + start, 16)
        return where.at[pl.ds(first, size), pl.ds(pl.multiple_of(col * width, 128), width)]


def nearest_first(layers, turn, layer):
    found = 0
    for here in range(layers):
        order = sorted(range(layers), key=lambda other: (abs(other - here), other))
        for at in range(layers):
            found = found + jnp.where((layer == here) & (turn == at), order[at], 0)
    return found


def expert_body(
    layers,
    units,
    experts,
    src,
    grads_ref,
    pick_ref,
    spread_ref,
    words_ref,
    gate_hbm,
    up_hbm,
    down_hbm,
    side_hbm,
    side_down_hbm,
    own_rows_ref,
    slot_rows_ref,
    slot_grads_ref,
    hidden_ref,
    d_gate_ref,
    d_up_ref,
    d_gates_ref,
    side_hidden_ref,
    d_side_ref,
    grad_side_ref,
    grad_side_down_ref,
    gate_w,
    up_w,
    down_w,
    side_w,
    side_down,
    held,
    side_hidden,
    d_side,
    weight_sem,
    rows_sem,
    *sems,
):
    bf16, f32 = jnp.bfloat16, jnp.float32
    me = Place(layers)
    work = PairGather(me, layers, False, src.shape, held, sems)
    own_expert = me.row * layers + me.layer
    block, half = src.shape
    width = 2 * half
    few, slots = pick_ref.shape[5], pick_ref.shape[4]
    per_block = block // few
    count = 2 * per_block
    lanes = side_down.shape[0]
    step = pl.program_id(0)
    steps = 2 * layers
    weight_loads = [
        pltpu.make_async_copy(src_ref, dst_ref, weight_sem.at[i])
        for i, (src_ref, dst_ref) in enumerate(
            (
                (down_hbm, down_w),
                (side_down_hbm, side_down),
                (side_hbm, side_w),
                (gate_hbm, gate_w),
                (up_hbm, up_w),
            )
        )
    ]

    def relay(early):
        for turn in range(layers):
            at = nearest_first(layers, turn, me.layer)
            if early and turn > 0:

                @pl.when(step == max(1, 2 * turn - 2))
                def _():
                    work.second(at)

            if not early:

                @pl.when(step == (0, 2)[turn] if turn < 2 else step == 2 * turn - 1)
                def _():
                    work.third(at)

        for distance in range(2, layers):
            if not early:

                @pl.when(step == distance - 2)
                def _():
                    work.at_distance(distance, work.arrived)

    def prepare(which):
        layer = nearest_first(layers, which // 2, me.layer)

        @pl.when(lax.rem(which, 2) == 0)
        def _():
            work.from_core(0, layer).wait_recv()
            work.from_core(2, layer).wait_recv()

        @pl.when(lax.rem(which, 2) == 1)
        def _():
            work.from_core(1, layer).wait_recv()
            work.from_core(3, layer).wait_recv()

    @pl.when(step == 0)
    def _():
        own = pltpu.make_async_copy(src, work.piece(0, me.layer), rows_sem)
        own.start()
        for copy in weight_loads:
            copy.start()
        me.greet()
        own.wait()
        work.begin()
        for copy in weight_loads:
            copy.wait()

    far = lax.rem(step, 2)
    x_place = me.row // 2 * (1 - far) + (1 - me.row // 2) * far
    pair = x_place * layers + nearest_first(layers, step // 2, me.layer)
    rows = held.at[pl.ds(pl.multiple_of(pair * 2 * block, 16), 2 * block)]

    def spot(b):
        core, j = b // per_block, b % per_block
        return core, j, pl.ds(b * few, few), pl.ds(j * slots, slots)

    for b in range(count):
        core, j, _, here = spot(b)
        for c in range(2):
            slot_grads_ref[0, core, 0, here, c * half : (c + 1) * half] = dot_nn(
                pick_ref[0, core, 0, j], grads_ref[0, core, 0, c, j * few : (j + 1) * few, :]
            ).astype(bf16)
    join = lambda ref: jnp.concatenate([ref[0, core, 0] for core in range(2)], axis=0)
    d_raw = dot_nt(join(slot_grads_ref), down_w[...])
    side_grads = [
        jnp.concatenate([grads_ref[0, core, 0, c] for core in range(2)], axis=0) for c in range(2)
    ]
    d_side_hidden = sum(
        dot_nt(side_grads[c], side_down[:, c * half : (c + 1) * half]) for c in range(2)
    )

    relay(True)

    @pl.when(step == 0)
    def _():
        work.second(me.layer)
        if layers > 1:
            work.at_distance(1, work.arrived)
        prepare(step)


    side = dot_nt(rows[...], side_w[...])
    side_gate, side_up = side[:, :lanes], side[:, lanes:]
    lane = lax.broadcasted_iota(jnp.int32, side_gate.shape, 1)
    expert = lane - units
    is_expert = (expert >= 0) & (expert < experts)
    highest = jnp.max(jnp.where(is_expert, side_gate, -jnp.inf), axis=1, keepdims=True)
    words = join(words_ref)
    word = words[:, 0:1]
    for i in range(1, words.shape[1]):
        word = jnp.where(expert >= 16 * i, words[:, i : i + 1], word)
    picked = lax.shift_right_logical(
        jnp.broadcast_to(word, expert.shape), jnp.bitwise_and(expert, 15)
    )
    picked = is_expert & (jnp.bitwise_and(picked, 1) == 1)
    chosen = jnp.where(picked, jnp.exp(jnp.where(is_expert, side_gate - highest, 0.0)), 0.0)
    total = jnp.sum(chosen, axis=1, keepdims=True)
    own = jnp.sum(jnp.where(expert == own_expert, chosen, 0.0), axis=1, keepdims=True) / total

    def two_parts(value):
        high = value.astype(bf16).astype(f32)
        at = lax.broadcasted_iota(jnp.int32, (value.shape[0], lanes), 1)
        return jnp.where(at == 0, high, jnp.where(at == 1, value - high, 0.0)).astype(bf16)

    own_parts = two_parts(own)
    slot_gates = []
    for b in range(count):
        core, j, tokens, here = spot(b)
        pick = pick_ref[0, core, 0, j]
        slot_rows_ref[0, core, 0, here, :] = dot_nn(pick, rows[tokens, :]).astype(bf16)
        parts = dot_nn(pick, own_parts[b * few : (b + 1) * few])
        slot_gates.append(jnp.sum(parts, axis=1, keepdims=True))
    slot_gate = jnp.concatenate(slot_gates, axis=0)

    slot_rows = join(slot_rows_ref)
    gate_pre = dot_nt(slot_rows, gate_w[...])
    up_pre = dot_nt(slot_rows, up_w[...])
    sigmoid = 1.0 / (1.0 + jnp.exp(-gate_pre))
    silu = gate_pre * sigmoid
    hidden = (silu * up_pre).astype(bf16).astype(f32)
    d_gates = jnp.sum(d_raw * hidden, axis=1, keepdims=True)
    d_hidden = d_raw * slot_gate
    each = per_block * slots

    def keep(ref, value):
        for core in range(2):
            ref[0, core, 0] = value[core * each : (core + 1) * each]

    hidden = (hidden * slot_gate).astype(bf16)
    keep(hidden_ref, hidden)
    d_up = (d_hidden * silu).astype(bf16)
    keep(d_up_ref, d_up)
    d_gate = (d_hidden * up_pre * sigmoid * (1.0 + gate_pre * (1.0 - sigmoid))).astype(bf16)
    keep(d_gate_ref, d_gate)

    relay(False)

    @pl.when(step + 1 < steps)
    def _():
        prepare(step + 1)

    side_sigmoid = 1.0 / (1.0 + jnp.exp(-side_gate))
    side_silu = side_gate * side_sigmoid
    side_hidden[...] = (side_silu * side_up).astype(bf16)
    d_side[:, lanes:] = (d_side_hidden * side_silu).astype(bf16)
    d_side[:, :lanes] = (
        d_side_hidden * side_up * side_sigmoid * (1.0 + side_gate * (1.0 - side_sigmoid))
    ).astype(bf16)

    @pl.when(step == 0)
    def _():
        grad_side_ref[...] = jnp.zeros_like(grad_side_ref)
        grad_side_down_ref[...] = jnp.zeros_like(grad_side_down_ref)

    grad_side_ref[...] += dot_tn(d_side[...], rows[...])
    for c in range(2):
        grad_side_down_ref[:, c * half : (c + 1) * half] += dot_tn(side_hidden[...], side_grads[c])

    d_gate_parts = two_parts(d_gates)
    for b in range(count):
        core, j, tokens, _ = spot(b)
        there = pl.ds(j * few, few)
        back = dot_nn(spread_ref[0, core, 0, j], d_gate_parts[b * slots : (b + 1) * slots])
        d_gates_ref[0, core, 0, there, :] = jnp.sum(back, axis=1, keepdims=True)
        side_hidden_ref[0, core, 0, there, :] = side_hidden[tokens, :]
        d_side_ref[0, core, 0, there, :] = d_side[tokens, :]

    @pl.when(step == steps - 1)
    def _():
        at = (me.row // 2 * layers + me.layer) * 2 + me.core
        mine = held.at[pl.ds(pl.multiple_of(at * block, 16), block)]
        keep_rows = pltpu.make_async_copy(mine, own_rows_ref, rows_sem)
        keep_rows.start()
        work.finish()
        keep_rows.wait()


def expert_pass(layers, few, slots, units, experts, rows_own, grads, pick, spread, words, weights, side_w, side_down):
    block, half = rows_own.shape
    width = 2 * half
    hidden = weights[0].shape[0]
    per_block = block // few
    tokens = 4 * layers * block
    lanes = side_down.shape[0]

    def by_step(*tail):
        def place(step):
            row = lax.axis_index("row")
            layer = nearest_first(layers, step // 2, lax.axis_index("exp"))
            far = lax.rem(step, 2)
            x_place = row // 2 * (1 - far) + (1 - row // 2) * far
            return (x_place, 0, layer, *(0 for _ in tail))

        return pl.BlockSpec((1, 2, 1, *tail), place)

    shape = lambda *tail, kind=jnp.bfloat16: jax.ShapeDtypeStruct((2, 2, layers, *tail), kind)
    each = per_block * slots
    outs = pl.pallas_call(
        functools.partial(expert_body, layers, units, experts),
        grid=(2 * layers,),
        in_specs=[
            pl.BlockSpec(memory_space=pl.ANY),
            by_step(2, block, half),
            by_step(per_block, slots, few),
            by_step(per_block, few, slots),
            by_step(block, words.shape[1]),
            *[pl.BlockSpec(memory_space=pl.ANY)] * 5,
        ],
        out_specs=[
            pl.BlockSpec(memory_space=pl.ANY),
            by_step(each, width),
            by_step(each, width),
            by_step(each, hidden),
            by_step(each, hidden),
            by_step(each, hidden),
            by_step(block, 1),
            by_step(block, lanes),
            by_step(block, 2 * lanes),
            pl.BlockSpec((2 * lanes, width), lambda i: (0, 0)),
            pl.BlockSpec((lanes, width), lambda i: (0, 0)),
        ],
        out_shape=[
            jax.ShapeDtypeStruct((block, width), jnp.bfloat16),
            shape(each, width),
            shape(each, width),
            shape(each, hidden),
            shape(each, hidden),
            shape(each, hidden),
            shape(block, 1, kind=jnp.float32),
            shape(block, lanes),
            shape(block, 2 * lanes),
            jax.ShapeDtypeStruct((2 * lanes, width), jnp.float32),
            jax.ShapeDtypeStruct((lanes, width), jnp.float32),
        ],
        scratch_shapes=[
            *(pltpu.VMEM(w.shape, jnp.bfloat16) for w in (*weights, side_w, side_down)),
            pltpu.VMEM((tokens, width), jnp.bfloat16),
            pltpu.VMEM((2 * block, lanes), jnp.bfloat16),
            pltpu.VMEM((2 * block, 2 * lanes), jnp.bfloat16),
            pltpu.SemaphoreType.DMA((5,)),
            pltpu.SemaphoreType.DMA,
            *Gather.semaphores(layers),
        ],
        compiler_params=pltpu.CompilerParams(
            collective_id=3, has_side_effects=True, vmem_limit_bytes=62 * 1024 * 1024
        ),
    )(
        rows_own,
        grads.reshape(2, 2, layers, 2, block, half),
        pick.reshape(2, 2, layers, per_block, slots, few),
        spread.reshape(2, 2, layers, per_block, few, slots),
        words.reshape(2, 2, layers, block, -1),
        *weights,
        side_w,
        side_down,
    )
    return outs


def rotate(value, cosine, sine):
    half = value.shape[-1] // 2
    first, second = (value[..., :half], value[..., half:])
    return jnp.concatenate(
        [first * cosine - second * sine, first * sine + second * cosine], axis=-1
    )


def unrotate(value, cosine, sine):
    half = value.shape[-1] // 2
    first, second = (value[..., :half], value[..., half:])
    return jnp.concatenate(
        [first * cosine + second * sine, second * cosine - first * sine], axis=-1
    )


def sequence_layout(lengths_row, group):
    ends = jnp.cumsum(lengths_row)
    starts = ends - lengths_row
    index = jnp.arange(group, dtype=jnp.int32)
    seq_ids = jnp.sum((index[:, None] >= ends[None, :]).astype(jnp.int32), axis=1)
    member = seq_ids[:, None] == jnp.arange(lengths_row.shape[0], dtype=jnp.int32)[None, :]
    begins = jnp.sum(jnp.where(member, starts[None, :], 0), axis=1)
    return (seq_ids, index - begins)


def rotary_tables(places):
    half = ROPE // 2
    freqs = jnp.power(theta_base, -jnp.arange(half, dtype=jnp.float32) * (2.0 / ROPE))
    angle = places.astype(jnp.float32)[..., None] * freqs
    return (jnp.cos(angle), jnp.sin(angle))


def norm_back(value, factor, gain, grad, width):
    weighted = grad * gain
    inner = lax.psum(jnp.sum(weighted * value, axis=1), "col")
    d_value = (
        factor[:, None] * weighted - value * (factor * factor * factor * inner / width)[:, None]
    )
    d_gain = jnp.sum(grad * value * factor[:, None], axis=0)
    return (d_value, d_gain)


def masked_scores(query_block, keys, seq_ids, first, scale):
    size = query_block.shape[0]
    group = keys.shape[0]
    scored = (
        jnp.einsum("qhd,khd->hqk", query_block, keys, preferred_element_type=jnp.float32) * scale
    )
    query_index = first + jnp.arange(size, dtype=jnp.int32)
    key_index = jnp.arange(group, dtype=jnp.int32)
    allowed = (seq_ids[first : first + size][:, None] == seq_ids[None, :group]) & (
        key_index[None, :] <= query_index[:, None]
    )
    return jnp.where(allowed[None, :, :], scored, -1e30)


def own_slice(value, index, axis):
    size = value.shape[axis] // 2
    return lax.dynamic_slice_in_dim(value, index * size, size, axis)


def col_pair(mine, sent, axis):
    received = lax.ppermute(sent, "col", SWAP)
    first = lax.axis_index("col") == 0
    return jnp.where(
        first,
        jnp.concatenate([mine, received], axis=axis),
        jnp.concatenate([received, mine], axis=axis),
    )


def halves(value, split):
    col = lax.axis_index("col")
    return own_slice(value, col, split), own_slice(value, 1 - col, split)


def trade(value, split, join):
    return col_pair(*halves(value, split), join)


def routed_and_shared(
    tok_dev, capacity, layers, router, expert_weights, shared_own, normed_own, grads_own, words
):
    bf16 = jnp.bfloat16
    col_id = lax.axis_index("col")
    own_expert = lax.axis_index("row") * layers + lax.axis_index("exp")
    experts = router.shape[1]
    units = shared_own.shape[1]
    block, half_width = normed_own.shape
    tokens = words.shape[0]
    few = min(tok_dev, block)
    slots = -(-min(capacity, few) // 16) * 16
    blocks = tokens // few

    own_word = lax.dynamic_index_in_dim(words, own_expert // 16, 1, keepdims=False)
    own_pick = (jnp.bitwise_and(lax.shift_right_logical(own_word, own_expert % 16), 1) == 1).reshape(
        blocks, few
    )
    order = jnp.arange(few, dtype=jnp.int32)
    place = dot_nn(own_pick.astype(bf16), (order[:, None] < order[None, :]).astype(bf16)).astype(
        jnp.int32
    )
    places = jnp.arange(slots, dtype=jnp.int32)
    pick = ((place[:, None, :] == places[None, :, None]) & own_pick[:, None, :]).astype(bf16)
    spread = ((place[:, :, None] == places[None, None, :]) & own_pick[:, :, None]).astype(bf16)
    lanes = -(-(units + experts) // 128) * 128
    fill = lambda value, n: jnp.pad(value, ((0, n - value.shape[0]), (0, 0)))
    side_w = jnp.concatenate(
        [fill(jnp.concatenate([shared_own[0], router.T]), lanes), fill(shared_own[1], lanes)]
    )
    side_down = fill(shared_own[2], lanes)

    grads_all = lax.all_gather(grads_own, ("row", "exp", "col"), axis=0)
    grads_all = grads_all.reshape(experts, 2, block, half_width)
    (
        own_normed,
        slot_rows,
        slot_grads,
        hidden,
        d_gate,
        d_up,
        d_gates_all,
        side_hidden,
        d_side,
        grad_side,
        grad_side_down,
    ) = expert_pass(
        layers,
        few,
        slots,
        units,
        experts,
        normed_own,
        grads_all,
        pick,
        spread,
        words,
        expert_weights,
        side_w,
        side_down,
    )
    spread = spread.reshape(2, 2, layers, -1, few, slots)
    gate_weight, up_weight, down_weight = expert_weights
    (d_normed,) = made_scatter(
        (d_gate, d_up), (gate_weight, up_weight), spread, d_side, side_w, (), (), layers, 4
    )
    flat = lambda *values: tuple(value.reshape(-1, value.shape[-1]) for value in values)
    out_parts = (
        (hidden,),
        (down_weight,),
        spread,
        side_hidden,
        side_down,
        flat(d_gate, d_up, hidden),
        flat(slot_rows, slot_rows, slot_grads),
    )
    grad_shared = jnp.stack(
        [grad_side[:units], grad_side[lanes : lanes + units], grad_side_down[:units]]
    )

    d_gates = lax.psum(
        lax.all_to_all(
            d_gates_all.reshape(experts, block), ("row", "exp"), split_axis=0, concat_axis=0, tiled=True
        ),
        "col",
    ).T
    own_probs = jax.nn.softmax(dot_nn(own_normed, router), axis=1)
    own_words = lax.dynamic_slice_in_dim(words, own_expert * block, block, 0)
    numbers = jnp.arange(experts, dtype=jnp.int32)
    picks = (
        jnp.bitwise_and(
            lax.shift_right_logical(own_words[:, numbers // 16], (numbers % 16)[None, :]), 1
        )
        == 1
    )
    selected = jnp.where(picks, own_probs, 0.0)
    own_total = jnp.sum(selected, axis=1, keepdims=True)
    own_gates = selected / own_total
    d_selected = (d_gates - jnp.sum(d_gates * own_gates, axis=1, keepdims=True)) / own_total
    d_router_probs = jnp.where(picks, d_selected, 0.0)
    d_logits = own_probs * (
        d_router_probs - jnp.sum(own_probs * d_router_probs, axis=1, keepdims=True)
    )
    router_half = lax.dynamic_slice_in_dim(router, col_id * half_width, half_width, 0)
    grad_router = lax.dot_general(
        normed_own.astype(jnp.float32),
        d_logits,
        (((0,), (0,)), ((), ())),
        precision=lax.Precision.HIGHEST,
        preferred_element_type=jnp.float32,
    )
    d_normed = d_normed + lax.dot_general(
        d_logits,
        router_half.astype(jnp.float32),
        (((1,), (1,)), ((), ())),
        precision=lax.Precision.HIGHEST,
        preferred_element_type=jnp.float32,
    )
    return (d_normed, out_parts, (grad_shared, grad_router))


def per_device(
    layer_input,
    lengths,
    routes,
    norm1_gain,
    w_query,
    w_latent,
    latent_gain,
    w_kv,
    w_out,
    norm2_gain,
    shared_gate,
    shared_up,
    shared_down,
    router,
    expert_gate,
    expert_up,
    expert_down,
    cotangent,
):
    row_id = lax.axis_index("row")
    col_id = lax.axis_index("col")
    exp_id = lax.axis_index("exp")
    rows_n, cols_n, exps_n = (lax.axis_size(name) for name in ("row", "col", "exp"))
    experts = rows_n * exps_n
    own_expert = row_id * exps_n + exp_id
    tok_dev = routes.shape[1]
    topk_count = routes.shape[2]
    capacity = max(2, 3 * tok_dev * topk_count // (2 * experts))
    slots = -(-capacity // 16) * 16
    block, half_width = layer_input.shape
    width = half_width * cols_n
    group = block * rows_n
    tokens = group * exps_n
    heads_here = w_kv.shape[1] // (QK_NOPE + V_DIM)
    head_dim = QK_NOPE + ROPE
    scale = 1.0 / math.sqrt(head_dim)
    query_rows = group // 2
    bf16 = jnp.bfloat16

    query_halves, layer_input = lax.optimization_barrier((halves(w_query, 1), layer_input))
    w_query_own = col_pair(*query_halves, 0)
    seq_ids, places = sequence_layout(lengths[0], group)
    cosine, sine = rotary_tables(places)

    group_input, w_latent_all = gather_several((layer_input, w_latent[0].T), 1, 10, (False, True))
    latent_width, slab = w_latent.shape[2], w_latent.shape[1]
    w_latent_all = w_latent_all.reshape(rows_n, cols_n, latent_width, slab)
    w_latent_all = w_latent_all.transpose(2, 1, 0, 3).reshape(latent_width, width)
    group_input, w_out, cotangent = lax.optimization_barrier((group_input, w_out, cotangent))
    w_out_own = trade(w_out, 0, 1)
    group_input = group_input.astype(jnp.float32)
    factor_group = lax.rsqrt(jnp.mean(group_input * group_input, axis=1) + epsilon)
    normed_group = (group_input * factor_group[:, None] * norm1_gain).astype(bf16)
    query_pre = dot_nn(normed_group, w_query_own).reshape(group, heads_here, head_dim)
    queries = jnp.concatenate(
        [
            query_pre[..., :QK_NOPE],
            rotate(query_pre[..., QK_NOPE:], cosine[:, None, :], sine[:, None, :]),
        ],
        axis=2,
    ).astype(bf16)
    queries, shared_gate, shared_up, shared_down = lax.optimization_barrier(
        (queries, shared_gate, shared_up, shared_down)
    )
    units = shared_gate.shape[1] // (cols_n * exps_n)
    shared_parts = jnp.stack(
        [
            lax.dynamic_index_in_dim(
                part.reshape(cols_n, exps_n, units, half_width), exp_id, 1, keepdims=False
            )
            for part in (shared_gate.T, shared_up.T, shared_down)
        ]
    )
    shared_own = trade(shared_parts, 1, 3)[:, 0]

    latent = dot_nt(normed_group, w_latent_all)
    compressed_raw = latent[:, :KV_RANK]
    kv_factor = lax.rsqrt(jnp.mean(compressed_raw * compressed_raw, axis=1) + epsilon)
    compressed = (compressed_raw * kv_factor[:, None] * latent_gain).astype(bf16)
    rotary_key = rotate(latent[:, KV_RANK:], cosine, sine).astype(bf16)
    key_value = (
        dot_nn(compressed, w_kv).astype(bf16).reshape(group, heads_here, QK_NOPE + V_DIM)
    )
    keys = jnp.concatenate(
        [
            key_value[..., :QK_NOPE],
            jnp.broadcast_to(rotary_key[:, None, :], (group, heads_here, ROPE)),
        ],
        axis=2,
    )
    values = key_value[..., QK_NOPE:]
    block_outputs = []
    block_totals = []
    for first in range(0, group, query_rows):
        last = first + query_rows
        scores = masked_scores(queries[first:last], keys[:last], seq_ids, first, scale)
        highest = jnp.max(scores, axis=2, keepdims=True)
        log_total = highest + jnp.log(jnp.sum(jnp.exp(scores - highest), axis=2, keepdims=True))
        probs_low = jnp.exp(scores - log_total).astype(bf16)
        block_outputs.append(
            jnp.einsum(
                "hqk,khd->qhd", probs_low, values[:last], preferred_element_type=jnp.float32
            ).astype(bf16)
        )
        block_totals.append(log_total)
    attended = jnp.concatenate(block_outputs, axis=0).reshape(group, heads_here * V_DIM)

    input_wide = layer_input.astype(jnp.float32)
    hidden_state = input_wide + scatter(dot_nn(attended, w_out_own).astype(bf16), 1, 2)
    words_n = -(-experts // 16)
    word_of = jnp.arange(words_n, dtype=jnp.int32)[:, None, None]
    bits = jnp.where(routes // 16 == word_of, jnp.left_shift(1, routes % 16), 0)
    bits = jnp.sum(bits, axis=2).astype(jnp.float32)
    padded = -(-tok_dev // 128) * 128
    bits = jnp.pad(bits, ((0, 0), (0, padded - tok_dev)))
    is_here = jnp.arange(experts, dtype=jnp.int32) == own_expert
    bits = jnp.where(is_here[:, None, None], bits[None], 0.0).reshape(experts * words_n, padded)
    bits, hidden_state = lax.optimization_barrier((bits, hidden_state))
    bits = small_sum(bits, exps_n, 8).reshape(experts, words_n, cols_n, padded)[..., :tok_dev]
    words_all = bits.astype(jnp.int32).transpose(0, 2, 3, 1).reshape(tokens, words_n)

    gain_two = lax.dynamic_slice_in_dim(norm2_gain, col_id * half_width, half_width)
    square = lax.psum(jnp.sum(hidden_state * hidden_state, axis=1), "col")
    factor_two = lax.rsqrt(square / width + epsilon)
    normed_two = (hidden_state * factor_two[:, None] * gain_two).astype(bf16)
    pieces = max(1, exps_n // 4)
    feed = functools.partial(
        routed_and_shared,
        tok_dev,
        capacity,
        exps_n,
        router,
        (expert_gate[0].T, expert_up[0].T, expert_down[0].T),
        shared_own,
    )
    if pieces == 1:
        d_normed, out_parts, weight_grads = feed(normed_two, cotangent, words_all)
    else:
        piece_rows = block // pieces

        def one_piece(total, items):
            d_rows, out_parts, grads = feed(*items)
            *out_parts, job_a, job_b = out_parts
            (branch_rows,) = made_scatter(*out_parts, (), (), exps_n, 9)
            grads = (*grads, tuple(dot_tn(a, b) for a, b in zip(job_a, job_b)))
            return (jax.tree.map(jnp.add, total, grads), (d_rows, branch_rows))

        split = lambda value: value.reshape(pieces, piece_rows, half_width)
        word_pieces = words_all.reshape(experts, pieces, piece_rows, words_n)
        items = (
            split(normed_two),
            split(cotangent),
            word_pieces.transpose(1, 0, 2, 3).reshape(pieces, -1, words_n),
        )
        start = (
            jnp.zeros((3, units, width), jnp.float32),
            jnp.zeros((half_width, experts), jnp.float32),
            (jnp.zeros(expert_gate.shape[:0:-1], jnp.float32),) * 3,
        )
        weight_grads, (d_normed, branch) = lax.scan(one_piece, start, items)
        d_normed, branch = (v.reshape(block, half_width) for v in (d_normed, branch))
    grad_shared, grad_router = weight_grads[:2]
    expert_grads = weight_grads[2] if pieces > 1 else None
    grad_shared = trade(grad_shared.astype(bf16)[:, None], 3, 1)
    d_normed, grad_shared = lax.optimization_barrier((d_normed, grad_shared))
    grad_shared = lax.all_gather(grad_shared, "exp", axis=2, tiled=False)
    d_norm_two, grad_gain_two = norm_back(hidden_state, factor_two, gain_two, d_normed, width)
    d_hidden_state = cotangent.astype(jnp.float32) + d_norm_two

    d_branch = gather(d_hidden_state.astype(bf16), 1, 1)
    grad_w_out = trade(dot_tn(attended, d_branch).astype(bf16), 1, 0)
    d_attended = dot_nt(d_branch, w_out_own).astype(bf16).reshape(group, heads_here, V_DIM)
    d_query_blocks = []
    d_keys = jnp.zeros((group, heads_here, head_dim), jnp.float32)
    d_values = jnp.zeros((group, heads_here, V_DIM), jnp.float32)
    for number, first in enumerate(range(0, group, query_rows)):
        last = first + query_rows
        query_block = queries[first:last]
        d_block = d_attended[first:last]
        scores = masked_scores(query_block, keys[:last], seq_ids, first, scale)
        probs = jnp.exp(scores - block_totals[number])
        d_probs = jnp.einsum(
            "qhd,khd->hqk", d_block, values[:last], preferred_element_type=jnp.float32
        )
        delta = jnp.sum(probs * d_probs, axis=2, keepdims=True)
        d_scores = (probs * (d_probs - delta)).astype(bf16)
        d_query_blocks.append(
            jnp.einsum("hqk,khd->qhd", d_scores, keys[:last], preferred_element_type=jnp.float32)
            * scale
        )
        d_keys = d_keys.at[:last].add(
            jnp.einsum("hqk,qhd->khd", d_scores, query_block, preferred_element_type=jnp.float32)
            * scale
        )
        d_values = d_values.at[:last].add(
            jnp.einsum(
                "hqk,qhd->khd", probs.astype(bf16), d_block, preferred_element_type=jnp.float32
            )
        )
    d_query = jnp.concatenate(d_query_blocks, axis=0)
    d_query_pre = (
        jnp.concatenate(
            [
                d_query[..., :QK_NOPE],
                unrotate(d_query[..., QK_NOPE:], cosine[:, None, :], sine[:, None, :]),
            ],
            axis=2,
        )
        .astype(bf16)
        .reshape(group, heads_here * head_dim)
    )
    d_key_value = (
        jnp.concatenate([d_keys[..., :QK_NOPE], d_values], axis=2)
        .astype(bf16)
        .reshape(group, heads_here * (QK_NOPE + V_DIM))
    )
    grad_w_kv = dot_tn(compressed, d_key_value)
    d_latent_sum = scatter(
        jnp.concatenate(
            [dot_nt(d_key_value, w_kv), jnp.sum(d_keys[..., QK_NOPE:], axis=1)], axis=1
        ).astype(bf16),
        1,
        5,
        by_rows=True,
    )
    own_first = (row_id * cols_n + col_id) * (group // (rows_n * cols_n))

    def own_tokens(value):
        return lax.dynamic_slice_in_dim(value, own_first, group // (rows_n * cols_n), 0)

    raw_own, factor_own = own_tokens(compressed_raw), own_tokens(kv_factor)
    d_compressed = d_latent_sum[:, :KV_RANK]
    weighted = d_compressed * latent_gain
    grad_latent_gain = jnp.sum(d_compressed * raw_own * factor_own[:, None], axis=0)
    inner = jnp.sum(weighted * raw_own, axis=1)
    d_raw = (
        factor_own[:, None] * weighted
        - raw_own * (factor_own * factor_own * factor_own * inner / KV_RANK)[:, None]
    )
    d_latent = gather(
        jnp.concatenate(
            [d_raw, unrotate(d_latent_sum[:, KV_RANK:], own_tokens(cosine), own_tokens(sine))],
            axis=1,
        ).astype(bf16),
        1,
        6,
        by_rows=True,
    )
    slab = w_latent.shape[1]
    slab_start = col_id * half_width + row_id * slab
    normed_slab = lax.dynamic_slice_in_dim(normed_group, slab_start, slab, 1)
    grad_w_latent = dot_tn(d_latent, normed_slab)
    grad_w_query = trade(dot_tn(normed_group, d_query_pre).astype(bf16), 0, 1)
    d_gathered = dot_nt(d_query_pre, w_query_own)
    piece = lax.dynamic_slice_in_dim(d_gathered, slab_start, slab, 1) + dot_nt(
        d_latent, w_latent[0]
    )
    d_gathered = lax.dynamic_update_slice_in_dim(d_gathered, piece, slab_start, 1)
    d_first = scatter(d_gathered.astype(bf16), 1, 2)
    gain_one = lax.dynamic_slice_in_dim(norm1_gain, col_id * half_width, half_width)
    factor_one = lax.dynamic_slice_in_dim(factor_group, row_id * block, block)
    d_norm_one, grad_gain_one = norm_back(input_wide, factor_one, gain_one, d_first, width)
    input_grad = d_hidden_state + d_norm_one
    if pieces == 1:
        out_parts, input_grad = lax.optimization_barrier((out_parts, input_grad))
        branch, *expert_grads = made_scatter(*out_parts, exps_n, 9)
    output = (hidden_state + branch).astype(bf16)

    small = jnp.concatenate(
        [
            grad_gain_one[None],
            grad_gain_two[None],
            jnp.pad(grad_latent_gain, (0, half_width - KV_RANK))[None],
            grad_router.T,
        ],
        axis=0,
    )
    small = jnp.pad(small, ((0, -small.shape[0] % 8), (0, 0)))
    small = small_sum(small, exps_n, 7)
    summed_latent_gain = small[2, :KV_RANK] + small[2, half_width : half_width + KV_RANK]

    grad_shared, grad_w_query = lax.optimization_barrier((grad_shared, grad_w_query))
    grad_shared = grad_shared.reshape(3, cols_n * exps_n * units, half_width).astype(jnp.float32)
    summed = lax.psum(
        (grad_w_query, grad_w_latent.astype(bf16), grad_w_kv.astype(bf16), grad_w_out), "exp"
    )
    return (
        output,
        input_grad,
        small[0],
        summed[0].astype(jnp.float32),
        summed[1].T.astype(jnp.float32)[None],
        summed_latent_gain,
        summed[2].astype(jnp.float32),
        summed[3].astype(jnp.float32),
        small[1],
        grad_shared[0].T,
        grad_shared[1].T,
        grad_shared[2],
        small[3 : 3 + experts].T,
        *(grad.T[None] for grad in expert_grads),
    )


def solution(mesh):
    placed = (
        P(("row", "exp"), "col"),
        P("exp", None),
        P("col", ("row", "exp"), None),
        P(),
        P("col", "row"),
        P("col", "row", None),
        P(),
        P(None, ("row", "col")),
        P("row", "col"),
        P(),
        P("col", "row"),
        P("col", "row"),
        P("row", "col"),
        P(),
        P(("row", "exp"), None, "col"),
        P(("row", "exp"), None, "col"),
        P(("row", "exp"), None, "col"),
        P(("row", "exp"), "col"),
    )
    return jax.shard_map(
        per_device,
        mesh=mesh,
        in_specs=placed,
        out_specs=(
            P(("row", "exp"), "col"),
            P(("row", "exp"), "col"),
            P(),
            P("col", "row"),
            P("col", "row", None),
            P(),
            P(None, ("row", "col")),
            P("row", "col"),
            P(),
            P("col", "row"),
            P("col", "row"),
            P("row", "col"),
            P(),
            P(("row", "exp"), None, "col"),
            P(("row", "exp"), None, "col"),
            P(("row", "exp"), None, "col"),
        ),
        check_vma=False,
    )
```

```python
import functools
import math

import jax
import jax.numpy as jnp
from jax import lax
from jax.experimental import pallas as pl
from jax.experimental.pallas import tpu as pltpu
from jax.sharding import PartitionSpec as P

QK_NOPE = 128
ROPE = 64
KV_RANK = 512
V_DIM = 128

epsilon = 1e-06
theta_base = 10000.0
SWAP = [(0, 1), (1, 0)]


MESH = pl.DeviceIdType.MESH


class Place:
    def __init__(self, layers):
        self.layers = layers
        self.row, self.col = lax.axis_index("row"), lax.axis_index("col")
        self.layer = lax.axis_index("exp") if layers > 1 else 0
        self.core = lax.rem(self.row, 2)
        self.x_row = lax.rem(self.row + 2, 4)
        self.core_row = self.row + 1 - 2 * self.core
        self.y_col = 1 - self.col
        self.to_x = {"row": self.x_row}
        self.to_y = {"col": self.y_col}
        self.to_core = {"row": self.core_row}
        self.above = {"exp": self.layer + 1}
        self.below = {"exp": self.layer - 1}

    def greet(self):
        barrier = pltpu.get_barrier_semaphore()
        for target in (self.to_x, self.to_y, self.to_core):
            pl.semaphore_signal(barrier, inc=1, device_id=target, device_id_type=MESH)
        if self.layers > 1:

            @pl.when(self.layer > 0)
            def _():
                pl.semaphore_signal(barrier, inc=1, device_id=self.below, device_id_type=MESH)

            @pl.when(self.layer < self.layers - 1)
            def _():
                pl.semaphore_signal(barrier, inc=1, device_id=self.above, device_id_type=MESH)

        peers = 3
        if self.layers > 1:
            peers = peers + jnp.where(self.layer > 0, 1, 0) + jnp.where(self.layer < self.layers - 1, 1, 0)
        pl.semaphore_wait(barrier, peers)


def remote(src, dst, send, recv, target):
    return pltpu.make_async_remote_copy(
        src_ref=src, dst_ref=dst, send_sem=send, recv_sem=recv, device_id=target, device_id_type=MESH
    )


def first_part(rows):
    return (rows // 2 + 15) // 16 * 16


def piece_of(where, layers, shape, by_rows, row, col, layer, span=None):
    rows, width = shape
    start, size = (0, rows) if span is None else span
    if by_rows == "lanes":
        first = pl.multiple_of((col * 4 + row) * width, 128)
        return where.at[pl.ds(start, size), pl.ds(first, width)]
    if by_rows:
        first = pl.multiple_of((row * 2 + col) * rows + start, 16)
        return where.at[pl.ds(first, size)]
    first = pl.multiple_of((row * layers + layer) * rows + start, 16)
    return where.at[pl.ds(first, size), pl.ds(pl.multiple_of(col * width, 128), width)]


class Gather:
    def __init__(self, me, layers, by_rows, shape, held, sems):
        self.me, self.layers, self.by_rows, self.shape, self.held = me, layers, by_rows, shape, held
        self.up_send, self.down_send, self.z_recv = sems[:3]
        self.send, self.recv, self.diag_send, self.diag_recv = sems[3:]
        part = first_part(shape[0])
        self.spans = ((0, part), (part, shape[0] - part))
        self.owners = (
            (me.row, me.col),
            (me.x_row, me.col),
            (me.row, me.y_col),
            (me.x_row, me.y_col),
        )
        self.sides = (me.to_x, me.to_y)

    @staticmethod
    def semaphores(layers):
        dma = pltpu.SemaphoreType.DMA
        line = [dma((layers,)) for _ in range(3)]
        return [*line, dma((5, 4, layers)), dma((5, 4, layers)), dma((2, layers)), dma((2, layers))]

    def area(self, where, row, col, layer, span=None):
        return piece_of(where, self.layers, self.shape, self.by_rows, row, col, layer, span)

    def piece(self, kind, layer, span=None):
        return self.area(self.held, *self.owners[kind], layer, span)

    def partner_piece(self, where, kind, layer):
        row, col = self.owners[kind]
        return self.area(where, row + 1 - 2 * self.me.core, col, layer)

    def to_core(self, kind, layer):
        piece = self.piece(kind, layer)
        sems = (4, kind, layer)
        return remote(piece, piece, self.send.at[sems], self.recv.at[sems], self.me.to_core)

    def from_core(self, kind, layer):
        piece = self.partner_piece(self.held, kind, layer)
        sems = (4, kind, layer)
        return remote(piece, piece, self.send.at[sems], self.recv.at[sems], self.me.to_core)

    def beside(self, axis, half, layer, incoming=False):
        piece = self.piece(axis + 1 if incoming else 0, layer, self.spans[half])
        sems = (2 * axis + half, 0, layer)
        return remote(piece, piece, self.send.at[sems], self.recv.at[sems], self.sides[axis])

    def corner(self, axis, layer, incoming=False):
        piece = self.piece(3 if incoming else axis + 1, layer, self.spans[axis])
        sems = (axis, layer)
        return remote(
            piece, piece, self.diag_send.at[sems], self.diag_recv.at[sems], self.sides[1 - axis]
        )

    def along(self, up, layer):
        piece = self.piece(0, layer)
        return remote(
            piece,
            piece,
            (self.up_send if up else self.down_send).at[layer],
            self.z_recv.at[layer],
            self.me.above if up else self.me.below,
        )

    def pass_on(self, up, layer):
        me = self.me

        @pl.when((me.layer < self.layers - 1) if up else (me.layer > 0))
        def _():
            self.along(up, layer).start()

    def spread(self, layer):
        self.beside(0, 0, layer).start()
        self.beside(1, 1, layer).start()
        self.beside(0, 1, layer).start()
        self.beside(1, 0, layer).start()
        self.to_core(0, layer).start()

    def begin(self):
        if self.layers > 1:
            self.pass_on(True, self.me.layer)
            self.pass_on(False, self.me.layer)
        self.spread(self.me.layer)

    def at_distance(self, distance, act):
        me = self.me
        if distance == 0:
            act(me.layer, None)
            return

        @pl.when(me.layer >= distance)
        def _():
            act(me.layer - distance, True)

        @pl.when(me.layer + distance < self.layers)
        def _():
            act(me.layer + distance, False)

    def arrived(self, layer, upward):
        self.along(upward, layer).wait_recv()
        self.pass_on(upward, layer)
        self.spread(layer)

    def second(self, layer):
        for axis in (0, 1):
            self.beside(axis, axis, layer, True).wait_recv()
            self.corner(axis, layer).start()
        for axis in (0, 1):
            self.beside(axis, 1 - axis, layer, True).wait_recv()
            self.to_core(axis + 1, layer).start()

    def third(self, layer):
        for axis in (0, 1):
            self.corner(axis, layer, True).wait_recv()
        self.to_core(3, layer).start()

    def finish(self):
        me, layers = self.me, self.layers
        for layer in range(layers):
            for kind in range(4):
                self.to_core(kind, layer).wait_send()
            for axis in (0, 1):
                for half in (0, 1):
                    self.beside(axis, half, layer).wait_send()
                self.corner(axis, layer).wait_send()
        if layers > 1:
            for layer in range(layers):

                @pl.when((me.layer < layers - 1) & (layer <= me.layer))
                def _():
                    self.along(True, layer).wait_send()

                @pl.when((me.layer > 0) & (layer >= me.layer))
                def _():
                    self.along(False, layer).wait_send()


def gather_body(layers, by_rows, *refs):
    count = len(by_rows)
    me = Place(layers)
    srcs, outs, refs = refs[:count], refs[count : 2 * count], refs[2 * count :]
    works, stores = [], []
    for i in range(count):
        held, store_sem, *sems = refs[9 * i : 9 * i + 9]
        works.append(Gather(me, layers, by_rows[i], srcs[i].shape, held, sems))

        def store(kind, layer, partner, work=works[i], out=outs[i], store_sem=store_sem):
            if partner:
                pair = (
                    work.partner_piece(work.held, kind, layer),
                    work.partner_piece(out, kind, layer),
                )
            else:
                pair = (work.piece(kind, layer), work.area(out, *work.owners[kind], layer))
            return pltpu.make_async_copy(*pair, store_sem.at[1 if partner else 0, kind, layer])

        stores.append(store)
    own = [
        pltpu.make_async_copy(src, work.piece(0, me.layer), refs[9 * i + 1].at[0, 0, me.layer])
        for i, (src, work) in enumerate(zip(srcs, works))
    ]
    for copy in own:
        copy.start()
    me.greet()
    for copy, work, store in zip(own, works, stores):
        copy.wait()
        work.begin()
        store(0, me.layer, False).start()

    def arrived(layer, upward):
        for work, store in zip(works, stores):
            work.arrived(layer, upward)
            store(0, layer, False).start()

    def second(layer, upward):
        for work, store in zip(works, stores):
            work.second(layer)
            for kind in (1, 2):
                store(kind, layer, False).start()

    def third(layer, upward):
        for work, store in zip(works, stores):
            work.third(layer)
            store(3, layer, False).start()
            for kind in range(4):
                work.from_core(kind, layer).wait_recv()
                store(kind, layer, True).start()

    for step in range(1, layers + 2):
        if step < layers:
            works[0].at_distance(step, arrived)
        if step - 1 < layers:
            works[0].at_distance(step - 1, second)
        if 0 <= step - 2 < layers:
            works[0].at_distance(step - 2, third)
    for work, store in zip(works, stores):
        for layer in range(layers):
            for kind in range(4):
                store(kind, layer, False).wait()
                store(kind, layer, True).wait()
        work.finish()


def gather(value, layers, collective_id, by_rows=False):
    return gather_several((value,), layers, collective_id, (by_rows,))[0]


def gather_several(values, layers, collective_id, by_rows):
    dma = pltpu.SemaphoreType.DMA
    shapes, scratch = [], []
    for value, rows_only in zip(values, by_rows):
        rows, width = value.shape
        if rows_only == "lanes":
            shapes.append((rows, 8 * width))
        else:
            shapes.append((8 * rows, width) if rows_only else (4 * layers * rows, 2 * width))
        scratch += [
            pltpu.VMEM(shapes[-1], value.dtype),
            dma((2, 4, layers)),
            *Gather.semaphores(layers),
        ]
    in_hbm = pl.BlockSpec(memory_space=pl.ANY)
    return pl.pallas_call(
        functools.partial(gather_body, layers, by_rows),
        out_shape=[
            jax.ShapeDtypeStruct(shape, value.dtype) for shape, value in zip(shapes, values)
        ],
        in_specs=[in_hbm] * len(values),
        out_specs=[in_hbm] * len(values),
        scratch_shapes=scratch,
        compiler_params=pltpu.CompilerParams(
            collective_id=collective_id,
            has_side_effects=True,
            vmem_limit_bytes=56 * 1024 * 1024,
        ),
    )(*values)


def scatter_body(
    layers,
    by_rows,
    src,
    out,
    acc,
    core_in,
    diag_a,
    diag_b,
    side_in,
    line_in,
    load_sem,
    core_send,
    core_recv,
    diag_send,
    diag_recv,
    side_send,
    side_recv,
    line_send,
    line_recv,
):
    me = Place(layers)
    rows, width = out.shape
    part = first_part(rows)
    owners = (
        (me.row, me.col),
        (me.x_row, me.col),
        (me.row, me.y_col),
        (me.x_row, me.y_col),
    )

    def layer_at(step):
        if layers == 1:
            return 0
        found = 0
        for layer in range(layers):
            order = sorted(range(layers), key=lambda other: (-abs(other - layer), -other))
            found = found + jnp.where(me.layer == layer, order[step], 0)
        return found

    layer_of = [layer_at(step) for step in range(layers)]

    def area(row, col, layer):
        return piece_of(src, layers, (rows, width), by_rows, row, col, layer)

    def load(step, kind):
        return pltpu.make_async_copy(
            area(*owners[kind], layer_of[step]), acc.at[step, kind], load_sem.at[step, kind]
        )

    def to_core(step, kind):
        row, col = owners[kind]
        return remote(
            area(row + 1 - 2 * me.core, col, layer_of[step]),
            core_in.at[step, kind],
            core_send.at[step, kind],
            core_recv.at[step, kind],
            me.to_core,
        )

    def diag(step, axis):
        start, size = ((0, part), (part, rows - part))[axis]
        return remote(
            acc.at[step, 3, pl.ds(start, size)],
            (diag_a, diag_b)[axis].at[step],
            diag_send.at[axis, step],
            diag_recv.at[axis, step],
            (me.to_y, me.to_x)[axis],
        )

    def side(step, axis):
        return remote(
            acc.at[step, axis + 1],
            side_in.at[axis, step],
            side_send.at[axis, step],
            side_recv.at[axis, step],
            (me.to_x, me.to_y)[axis],
        )

    def line(step, up):
        layer = layer_of[step]
        way = 0 if up else 1
        return remote(
            acc.at[step, 0],
            line_in.at[way, layer],
            line_send.at[step],
            line_recv.at[way, layer],
            me.above if up else me.below,
        )

    lanes = 32 if part % 32 == 0 and rows % 32 == 0 else 16

    def add(target, others, start=0, size=rows, into=None):
        def step(i, carry):
            first = pl.multiple_of(i * lanes, 16)
            total = target[pl.ds(start + first, lanes), :].astype(jnp.float32)
            for other in others:
                total = total + other[pl.ds(first, lanes), :].astype(jnp.float32)
            if into is None:
                target[pl.ds(start + first, lanes), :] = total.astype(target.dtype)
            else:
                into[pl.ds(first, lanes), :] = total.astype(into.dtype)
            return carry

        lax.fori_loop(0, size // lanes, step, 0)

    me.greet()
    kinds = (3, 1, 2, 0)
    for step in range(layers):
        for kind in kinds:
            to_core(step, kind).start()
            load(step, kind).start()

    def ready(step, kind):
        load(step, kind).wait()
        to_core(step, kind).wait_recv()

    def stage_a(step):
        ready(step, 3)
        add(acc.at[step, 3], [core_in.at[step, 3]])
        diag(step, 0).start()
        diag(step, 1).start()

    def stage_b(step):
        for axis, buffer, start, size in (
            (0, diag_a, 0, part),
            (1, diag_b, part, rows - part),
        ):
            kind = axis + 1
            ready(step, kind)
            add(acc.at[step, kind], [core_in.at[step, kind]])
            diag(step, axis).wait_recv()
            add(acc.at[step, kind], [buffer.at[step]], start, size)
            side(step, axis).start()

    def stage_c(step):
        ready(step, 0)
        side(step, 0).wait_recv()
        side(step, 1).wait_recv()
        parts = [core_in.at[step, 0], side_in.at[0, step], side_in.at[1, step]]
        if layers == 1:
            add(acc.at[step, 0], parts, into=out)
            return
        add(acc.at[step, 0], parts)
        layer = layer_of[step]
        if step < layers - 1:

            @pl.when((layer > me.layer) & (me.layer > 0))
            def _():
                line(step, True).wait_recv()
                add(acc.at[step, 0], [line_in.at[0, layer]])

            @pl.when((layer < me.layer) & (me.layer < layers - 1))
            def _():
                line(step, False).wait_recv()
                add(acc.at[step, 0], [line_in.at[1, layer]])

            @pl.when(layer > me.layer)
            def _():
                line(step, True).start()

            @pl.when(layer < me.layer)
            def _():
                line(step, False).start()
        else:
            inner = (me.layer > 0) & (me.layer < layers - 1)

            @pl.when(me.layer > 0)
            def _():
                line(step, True).wait_recv()

            @pl.when(me.layer < layers - 1)
            def _():
                line(step, False).wait_recv()

            @pl.when(inner)
            def _():
                add(acc.at[step, 0], [line_in.at[0, layer], line_in.at[1, layer]], into=out)

            @pl.when(me.layer == 0)
            def _():
                add(acc.at[step, 0], [line_in.at[1, layer]], into=out)

            @pl.when(me.layer == layers - 1)
            def _():
                add(acc.at[step, 0], [line_in.at[0, layer]], into=out)

    for step in range(layers + 2):
        if step < layers:
            stage_a(step)
        if 0 <= step - 1 < layers:
            stage_b(step - 1)
        if 0 <= step - 2 < layers:
            stage_c(step - 2)
    for step in range(layers):
        for kind in kinds:
            to_core(step, kind).wait_send()
        for axis in (0, 1):
            diag(step, axis).wait_send()
            side(step, axis).wait_send()
        if step < layers - 1:

            @pl.when(layer_of[step] > me.layer)
            def _():
                line(step, True).wait_send()

            @pl.when(layer_of[step] < me.layer)
            def _():
                line(step, False).wait_send()


def scatter(value, layers, collective_id, by_rows=False):
    if by_rows:
        rows, width = value.shape[0] // 8, value.shape[1]
    else:
        rows, width = value.shape[0] // (4 * layers), value.shape[1] // 2
    part = first_part(rows)
    dma = pltpu.SemaphoreType.DMA
    buffer = lambda *lead: pltpu.VMEM((*lead, rows, width), value.dtype)
    return pl.pallas_call(
        functools.partial(scatter_body, layers, by_rows),
        out_shape=jax.ShapeDtypeStruct((rows, width), jnp.float32),
        in_specs=[pl.BlockSpec(memory_space=pl.ANY)],
        out_specs=pl.BlockSpec(memory_space=pltpu.VMEM),
        scratch_shapes=[
            buffer(layers, 4),
            buffer(layers, 4),
            pltpu.VMEM((layers, part, width), value.dtype),
            pltpu.VMEM((layers, rows - part, width), value.dtype),
            buffer(2, layers),
            buffer(2, layers),
            dma((layers, 4)),
            dma((layers, 4)),
            dma((layers, 4)),
            dma((2, layers)),
            dma((2, layers)),
            dma((2, layers)),
            dma((2, layers)),
            dma((layers,)),
            dma((2, layers)),
        ],
        compiler_params=pltpu.CompilerParams(
            collective_id=collective_id,
            has_side_effects=True,
            vmem_limit_bytes=56 * 1024 * 1024,
        ),
    )(value)


def dot_nn(left, right):
    return jnp.dot(left, right, preferred_element_type=jnp.float32)


def dot_nt(left, right):
    return lax.dot_general(
        left, right, (((1,), (1,)), ((), ())), preferred_element_type=jnp.float32
    )


def dot_tn(left, right):
    return lax.dot_general(
        left, right, (((0,), (0,)), ((), ())), preferred_element_type=jnp.float32
    )


def made_scatter_body(layers, parts, jobs, *refs):
    slots_hbm, refs = refs[:parts], refs[parts:]
    weights_hbm, refs = refs[:parts], refs[parts:]
    spread_hbm, side_hbm, side_w_hbm, refs = *refs[:3], refs[3:]
    job_a, job_b, refs = refs[:jobs], refs[jobs : 2 * jobs], refs[2 * jobs :]
    out, job_out, refs = refs[0], refs[1 : 1 + jobs], refs[1 + jobs :]
    if jobs:
        job_acc, a_in, b_in, job_sem, flush_sem, refs = *refs[:5], refs[5:]
    slots_in, refs = refs[:parts], refs[parts:]
    weights, refs = refs[:parts], refs[parts:]
    spread_in, side_in, side_w, slot_rows, refs = *refs[:4], refs[4:]
    core_out, acc, core_in, diag_a, diag_b, beside_in, line_in, refs = *refs[:7], refs[7:]
    in_sem, weight_sem, core_send, core_recv, diag_send, diag_recv, side_send, side_recv = refs[:8]
    line_send, line_recv = refs[8:]
    me = Place(layers)
    rows, width = out.shape
    part = first_part(rows)
    f32 = jnp.float32
    per_block, few, slots = spread_in.shape[2:]
    x_mine = me.row // 2

    def layer_at(step):
        return nearest_first(layers, layers - 1 - step, me.layer)

    def loads(unit):
        step, own = unit // 2, lax.rem(unit, 2)
        core = me.core * own + (1 - me.core) * (1 - own)
        slot = lax.rem(unit, 2)
        layer = layer_at(step)
        pairs = [*zip(slots_hbm, slots_in), (spread_hbm, spread_in), (side_hbm, side_in)]
        return [
            pltpu.make_async_copy(
                src.at[x_mine if x == 0 else 1 - x_mine, core, layer],
                dst.at[slot, x],
                in_sem.at[slot, i, x],
            )
            for i, (src, dst) in enumerate(pairs)
            for x in range(2)
        ]

    def weight_loads():
        pairs = [*zip(weights_hbm, weights), (side_w_hbm, side_w)]
        copies = []
        for i, (src, dst) in enumerate(pairs):
            for at, col in enumerate((me.col, me.y_col)):
                copies.append(
                    pltpu.make_async_copy(
                        src.at[:, pl.ds(pl.multiple_of(col * width, 128), width)],
                        dst.at[:, pl.ds(at * width, width)],
                        weight_sem.at[i, at],
                    )
                )
        return copies

    def make(unit, put):
        for copy in loads(unit):
            copy.wait()

        @pl.when(unit + 1 < 2 * layers)
        def _():
            for copy in loads(unit + 1):
                copy.start()

        slot = lax.rem(unit, 2)
        total = sum(
            dot_nn(value[slot].reshape(-1, value.shape[-1]), weight[...])
            for value, weight in zip(slots_in, weights)
        )
        slot_rows[...] = total.astype(slot_rows.dtype)
        for x in range(2):
            for j in range(per_block):
                there = pl.ds(j * few, few)
                here = pl.ds((x * per_block + j) * slots, slots)
                made = dot_nn(spread_in[slot, x, j], slot_rows[here, :]) + dot_nn(
                    side_in[slot, x, there, :], side_w[...]
                )
                put(x, there, made[:, :width].astype(acc.dtype))
                put(x + 2, there, made[:, width:].astype(acc.dtype))

    def to_core(step, kind):
        return remote(
            core_out.at[lax.rem(step, 2), kind],
            core_in.at[step, kind],
            core_send.at[step, kind],
            core_recv.at[step, kind],
            me.to_core,
        )

    def diag(step, axis):
        start, size = ((0, part), (part, rows - part))[axis]
        return remote(
            acc.at[step, 3, pl.ds(start, size)],
            (diag_a, diag_b)[axis].at[step],
            diag_send.at[axis, step],
            diag_recv.at[axis, step],
            (me.to_y, me.to_x)[axis],
        )

    def side(step, axis):
        return remote(
            acc.at[step, axis + 1],
            beside_in.at[axis, step],
            side_send.at[axis, step],
            side_recv.at[axis, step],
            (me.to_x, me.to_y)[axis],
        )

    def line(step, up):
        layer = layer_at(step)
        way = 0 if up else 1
        return remote(
            acc.at[step, 0],
            line_in.at[way, layer],
            line_send.at[step],
            line_recv.at[way, layer],
            me.above if up else me.below,
        )

    lanes = 32 if part % 32 == 0 and rows % 32 == 0 else 16

    def add(target, others, start=0, size=rows, into=None):
        def step(i, carry):
            first = pl.multiple_of(i * lanes, 16)
            total = target[pl.ds(start + first, lanes), :].astype(f32)
            for other in others:
                total = total + other[pl.ds(first, lanes), :].astype(f32)
            if into is None:
                target[pl.ds(start + first, lanes), :] = total.astype(target.dtype)
            else:
                into[pl.ds(first, lanes), :] = total.astype(into.dtype)
            return carry

        lax.fori_loop(0, size // lanes, step, 0)

    turns = layers + 2
    chunk = a_in.shape[1] if jobs else 0
    chunks = job_a[0].shape[0] // chunk if jobs else 0

    def job_loads(unit, job):
        slot = lax.rem(unit, 2)
        here = pl.ds(pl.multiple_of(lax.rem(unit, turns) * chunk, 16), chunk)
        return [
            pltpu.make_async_copy(src.at[here], dst.at[slot], job_sem.at[slot, i])
            for i, (src, dst) in enumerate(((job_a[job], a_in), (job_b[job], b_in)))
        ]

    def start_job_loads(unit):
        for job in range(jobs):

            @pl.when((unit // turns == job) & (lax.rem(unit, turns) < chunks))
            def _():
                for copy in job_loads(unit, job):
                    copy.start()

    def flush(job):
        return pltpu.make_async_copy(job_acc, job_out[job], flush_sem)

    def job_turn(unit):
        if not jobs:
            return
        at = lax.rem(unit, turns)
        slot = lax.rem(unit, 2)

        @pl.when(unit + 1 < jobs * turns)
        def _():
            start_job_loads(unit + 1)

        @pl.when((at == 0) & (unit > 0))
        def _():
            flush(0).wait()

        @pl.when(at == 0)
        def _():
            job_acc[...] = jnp.zeros_like(job_acc)

        @pl.when(at < chunks)
        def _():
            for copy in job_loads(unit, 0):
                copy.wait()
            left = a_in[slot].T
            for first in range(0, 2 * width, width // 2):
                here = pl.ds(first, width // 2)
                job_acc[:, here] += dot_nn(left, b_in[slot, :, here])

        for job in range(jobs):

            @pl.when((at == chunks - 1) & (unit // turns == job))
            def _():
                flush(job).start()

    for copy in (*weight_loads(), *loads(0)):
        copy.start()
    if jobs:
        start_job_loads(0)
    me.greet()
    for copy in weight_loads():
        copy.wait()

    def produce(step):
        @pl.when(step >= 2)
        def _():
            for kind in range(4):
                to_core(step - 2, kind).wait_send()

        half = lax.rem(step, 2)

        def to_other(kind, there, value):
            core_out[half, kind, there, :] = value

        make(2 * step, to_other)
        for kind in (3, 1, 2, 0):
            to_core(step, kind).start()

        def to_own(kind, there, value):
            acc[step, kind, there, :] = value

        make(2 * step + 1, to_own)

    def stage_a(step):
        to_core(step, 3).wait_recv()
        add(acc.at[step, 3], [core_in.at[step, 3]])
        diag(step, 0).start()
        diag(step, 1).start()

    def stage_b(step):
        for axis, buffer, start, size in (
            (0, diag_a, 0, part),
            (1, diag_b, part, rows - part),
        ):
            kind = axis + 1
            to_core(step, kind).wait_recv()
            add(acc.at[step, kind], [core_in.at[step, kind]])
            diag(step, axis).wait_recv()
            add(acc.at[step, kind], [buffer.at[step]], start, size)
            side(step, axis).start()

    def stage_c(step):
        to_core(step, 0).wait_recv()
        side(step, 0).wait_recv()
        side(step, 1).wait_recv()
        add(acc.at[step, 0], [core_in.at[step, 0], beside_in.at[0, step], beside_in.at[1, step]])
        layer = layer_at(step)

        @pl.when((layer > me.layer) & (me.layer > 0))
        def _():
            line(step, True).wait_recv()
            add(acc.at[step, 0], [line_in.at[0, layer]])

        @pl.when((layer < me.layer) & (me.layer < layers - 1))
        def _():
            line(step, False).wait_recv()
            add(acc.at[step, 0], [line_in.at[1, layer]])

        @pl.when(layer > me.layer)
        def _():
            line(step, True).start()

        @pl.when(layer < me.layer)
        def _():
            line(step, False).start()

    def stages(step, carry):
        @pl.when(step < layers)
        def _():
            produce(step)
            stage_a(step)

        job_turn(3 * step)

        @pl.when((step >= 1) & (step <= layers))
        def _():
            stage_b(step - 1)

        job_turn(3 * step + 1)

        @pl.when(step >= 2)
        def _():
            stage_c(step - 2)

        job_turn(3 * step + 2)
        return carry

    lax.fori_loop(0, layers + 2, stages, 0)
    last = layers - 1

    @pl.when(me.layer > 0)
    def _():
        line(last, True).wait_recv()

    @pl.when(me.layer < last)
    def _():
        line(last, False).wait_recv()

    @pl.when((me.layer > 0) & (me.layer < last))
    def _():
        add(acc.at[last, 0], [line_in.at[0, me.layer], line_in.at[1, me.layer]], into=out)

    @pl.when(me.layer == 0)
    def _():
        add(acc.at[last, 0], [line_in.at[1, me.layer]], into=out)

    @pl.when(me.layer == last)
    def _():
        add(acc.at[last, 0], [line_in.at[0, me.layer]], into=out)

    if jobs:
        flush(0).wait()
    for step in range(layers):
        if step >= layers - 2:
            for kind in range(4):
                to_core(step, kind).wait_send()
        for axis in (0, 1):
            diag(step, axis).wait_send()
            side(step, axis).wait_send()
        if step < last:

            @pl.when(layer_at(step) > me.layer)
            def _():
                line(step, True).wait_send()

            @pl.when(layer_at(step) < me.layer)
            def _():
                line(step, False).wait_send()


def made_scatter(slots_in, weights, spread, side, side_w, job_a, job_b, layers, collective_id):
    block, width = side.shape[3], side_w.shape[1] // 2
    bf16, f32 = jnp.bfloat16, jnp.float32
    parts, jobs = len(weights), len(job_a)
    part = first_part(block)
    dma = pltpu.SemaphoreType.DMA
    buffer = lambda *lead: pltpu.VMEM((*lead, block, width), bf16)
    ahead = lambda value: pltpu.VMEM((2, 2, *value.shape[3:]), bf16)
    in_hbm = pl.BlockSpec(memory_space=pl.ANY)
    job_shapes, job_scratch = [], []
    if jobs:
        rows, tall, wide = *job_a[0].shape, job_b[0].shape[1]
        chunks = max(n for n in range(1, layers + 3) if rows % (16 * n) == 0)
        job_shapes = [jax.ShapeDtypeStruct((tall, wide), f32)] * jobs
        job_scratch = [
            pltpu.VMEM((tall, wide), f32),
            pltpu.VMEM((2, rows // chunks, tall), bf16),
            pltpu.VMEM((2, rows // chunks, wide), bf16),
            dma((2, 2)),
            dma,
        ]
    return pl.pallas_call(
        functools.partial(made_scatter_body, layers, parts, jobs),
        out_shape=[jax.ShapeDtypeStruct((block, width), f32), *job_shapes],
        in_specs=[in_hbm] * (2 * parts + 3 + 2 * jobs),
        out_specs=[pl.BlockSpec(memory_space=pltpu.VMEM), *[in_hbm] * jobs],
        scratch_shapes=[
            *job_scratch,
            *(ahead(value) for value in slots_in),
            *(pltpu.VMEM(value.shape, bf16) for value in weights),
            ahead(spread),
            ahead(side),
            pltpu.VMEM(side_w.shape, bf16),
            pltpu.VMEM((2 * slots_in[0].shape[3], 2 * width), bf16),
            buffer(2, 4),
            buffer(layers, 4),
            buffer(layers, 4),
            pltpu.VMEM((layers, part, width), bf16),
            pltpu.VMEM((layers, block - part, width), bf16),
            buffer(2, layers),
            buffer(2, layers),
            dma((2, parts + 2, 2)),
            dma((parts + 1, 2)),
            dma((layers, 4)),
            dma((layers, 4)),
            dma((2, layers)),
            dma((2, layers)),
            dma((2, layers)),
            dma((2, layers)),
            dma((layers,)),
            dma((2, layers)),
        ],
        compiler_params=pltpu.CompilerParams(
            collective_id=collective_id,
            has_side_effects=True,
            vmem_limit_bytes=62 * 1024 * 1024,
        ),
    )(*slots_in, *weights, spread, side, side_w, *job_a, *job_b)


def small_sum_body(layers, src, out, core_in, mid, x_in, near, line_in, total, send, recv, line_send, line_recv):
    me = Place(layers)
    width = src.shape[1]
    barrier = pltpu.get_barrier_semaphore()
    for target in (me.to_x, me.to_y, me.to_core):
        pl.semaphore_signal(barrier, inc=1, device_id=target, device_id_type=MESH)
    for step in range(1, layers):
        other = {"exp": lax.rem(me.layer + step, layers)}
        pl.semaphore_signal(barrier, inc=1, device_id=other, device_id_type=MESH)
    pl.semaphore_wait(barrier, 3 + layers - 1)
    swap = remote(src, core_in, send.at[0], recv.at[0], me.to_core)
    swap.start()
    swap.wait()
    mid[...] = src[...] + core_in[...]
    swap = remote(mid, x_in, send.at[1], recv.at[1], me.to_x)
    swap.start()
    swap.wait()
    near[...] = mid[...] + x_in[...]
    line_in[me.layer] = near[...]

    def along(step, incoming):
        layer = lax.rem(me.layer + (layers - step if incoming else 0), layers)
        return remote(
            near,
            line_in.at[layer],
            line_send.at[step],
            line_recv.at[step],
            {"exp": lax.rem(me.layer + step, layers)},
        )

    for step in range(1, layers):
        along(step, False).start()
    for step in range(1, layers):
        along(step, True).wait_recv()
    summed = line_in[0]
    for layer in range(1, layers):
        summed = summed + line_in[layer]
    total[...] = summed
    mine = pl.ds(pl.multiple_of(me.col * width, 128), width)
    theirs = pl.ds(pl.multiple_of(me.y_col * width, 128), width)
    out[:, mine] = summed
    remote(total, out.at[:, mine], send.at[2], recv.at[2], me.to_y).start()
    remote(total, out.at[:, theirs], send.at[2], recv.at[2], me.to_y).wait()
    for step in range(1, layers):
        along(step, False).wait_send()


def small_sum(value, layers, collective_id):
    rows, width = value.shape
    dma = pltpu.SemaphoreType.DMA
    buffer = lambda *lead: pltpu.VMEM((*lead, rows, width), value.dtype)
    in_vmem = pl.BlockSpec(memory_space=pltpu.VMEM)
    return pl.pallas_call(
        functools.partial(small_sum_body, layers),
        out_shape=jax.ShapeDtypeStruct((rows, 2 * width), value.dtype),
        in_specs=[in_vmem],
        out_specs=in_vmem,
        scratch_shapes=[
            buffer(),
            buffer(),
            buffer(),
            buffer(),
            buffer(layers),
            buffer(),
            dma((3,)),
            dma((3,)),
            dma((layers,)),
            dma((layers,)),
        ],
        compiler_params=pltpu.CompilerParams(
            collective_id=collective_id,
            has_side_effects=True,
            vmem_limit_bytes=32 * 1024 * 1024,
        ),
    )(value)


class PairGather(Gather):
    def area(self, where, row, col, layer, span=None):
        rows, width = self.shape
        start, size = (0, rows) if span is None else span
        at = (row // 2 * self.layers + layer) * 2 + lax.rem(row, 2)
        first = pl.multiple_of(at * rows + start, 16)
        return where.at[pl.ds(first, size), pl.ds(pl.multiple_of(col * width, 128), width)]


def nearest_first(layers, turn, layer):
    found = 0
    for here in range(layers):
        order = sorted(range(layers), key=lambda other: (abs(other - here), other))
        for at in range(layers):
            found = found + jnp.where((layer == here) & (turn == at), order[at], 0)
    return found


def expert_body(
    layers,
    units,
    experts,
    src,
    grads_ref,
    pick_ref,
    spread_ref,
    words_ref,
    gate_hbm,
    up_hbm,
    down_hbm,
    side_hbm,
    side_down_hbm,
    own_rows_ref,
    slot_rows_ref,
    slot_grads_ref,
    hidden_ref,
    d_gate_ref,
    d_up_ref,
    d_gates_ref,
    side_hidden_ref,
    d_side_ref,
    grad_side_ref,
    grad_side_down_ref,
    gate_w,
    up_w,
    down_w,
    side_w,
    side_down,
    held,
    side_hidden,
    d_side,
    weight_sem,
    rows_sem,
    *sems,
):
    bf16, f32 = jnp.bfloat16, jnp.float32
    me = Place(layers)
    work = PairGather(me, layers, False, src.shape, held, sems)
    own_expert = me.row * layers + me.layer
    block, half = src.shape
    width = 2 * half
    few, slots = pick_ref.shape[5], pick_ref.shape[4]
    per_block = block // few
    count = 2 * per_block
    lanes = side_down.shape[0]
    step = pl.program_id(0)
    steps = 2 * layers
    weight_loads = [
        pltpu.make_async_copy(src_ref, dst_ref, weight_sem.at[i])
        for i, (src_ref, dst_ref) in enumerate(
            (
                (down_hbm, down_w),
                (side_down_hbm, side_down),
                (side_hbm, side_w),
                (gate_hbm, gate_w),
                (up_hbm, up_w),
            )
        )
    ]

    def relay(early):
        for turn in range(layers):
            at = nearest_first(layers, turn, me.layer)
            if early and turn > 0:

                @pl.when(step == max(1, 2 * turn - 2))
                def _():
                    work.second(at)

            if not early:

                @pl.when(step == (0, 2)[turn] if turn < 2 else step == 2 * turn - 1)
                def _():
                    work.third(at)

        for distance in range(2, layers):
            if not early:

                @pl.when(step == distance - 2)
                def _():
                    work.at_distance(distance, work.arrived)

    def prepare(which):
        layer = nearest_first(layers, which // 2, me.layer)

        @pl.when(lax.rem(which, 2) == 0)
        def _():
            work.from_core(0, layer).wait_recv()
            work.from_core(2, layer).wait_recv()

        @pl.when(lax.rem(which, 2) == 1)
        def _():
            work.from_core(1, layer).wait_recv()
            work.from_core(3, layer).wait_recv()

    @pl.when(step == 0)
    def _():
        own = pltpu.make_async_copy(src, work.piece(0, me.layer), rows_sem)
        own.start()
        for copy in weight_loads:
            copy.start()
        me.greet()
        own.wait()
        work.begin()
        for copy in weight_loads:
            copy.wait()

    far = lax.rem(step, 2)
    x_place = me.row // 2 * (1 - far) + (1 - me.row // 2) * far
    pair = x_place * layers + nearest_first(layers, step // 2, me.layer)
    rows = held.at[pl.ds(pl.multiple_of(pair * 2 * block, 16), 2 * block)]

    def spot(b):
        core, j = b // per_block, b % per_block
        return core, j, pl.ds(b * few, few), pl.ds(j * slots, slots)

    for b in range(count):
        core, j, _, here = spot(b)
        for c in range(2):
            slot_grads_ref[0, core, 0, here, c * half : (c + 1) * half] = dot_nn(
                pick_ref[0, core, 0, j], grads_ref[0, core, 0, c, j * few : (j + 1) * few, :]
            ).astype(bf16)
    join = lambda ref: jnp.concatenate([ref[0, core, 0] for core in range(2)], axis=0)
    d_raw = dot_nt(join(slot_grads_ref), down_w[...])
    side_grads = [
        jnp.concatenate([grads_ref[0, core, 0, c] for core in range(2)], axis=0) for c in range(2)
    ]
    d_side_hidden = sum(
        dot_nt(side_grads[c], side_down[:, c * half : (c + 1) * half]) for c in range(2)
    )

    relay(True)

    @pl.when(step == 0)
    def _():
        work.second(me.layer)
        if layers > 1:
            work.at_distance(1, work.arrived)
        prepare(step)


    side = dot_nt(rows[...], side_w[...])
    side_gate, side_up = side[:, :lanes], side[:, lanes:]
    lane = lax.broadcasted_iota(jnp.int32, side_gate.shape, 1)
    expert = lane - units
    is_expert = (expert >= 0) & (expert < experts)
    highest = jnp.max(jnp.where(is_expert, side_gate, -jnp.inf), axis=1, keepdims=True)
    words = join(words_ref)
    word = words[:, 0:1]
    for i in range(1, words.shape[1]):
        word = jnp.where(expert >= 16 * i, words[:, i : i + 1], word)
    picked = lax.shift_right_logical(
        jnp.broadcast_to(word, expert.shape), jnp.bitwise_and(expert, 15)
    )
    picked = is_expert & (jnp.bitwise_and(picked, 1) == 1)
    chosen = jnp.where(picked, jnp.exp(jnp.where(is_expert, side_gate - highest, 0.0)), 0.0)
    total = jnp.sum(chosen, axis=1, keepdims=True)
    own = jnp.sum(jnp.where(expert == own_expert, chosen, 0.0), axis=1, keepdims=True) / total

    def two_parts(value):
        high = value.astype(bf16).astype(f32)
        at = lax.broadcasted_iota(jnp.int32, (value.shape[0], lanes), 1)
        return jnp.where(at == 0, high, jnp.where(at == 1, value - high, 0.0)).astype(bf16)

    own_parts = two_parts(own)
    slot_gates = []
    for b in range(count):
        core, j, tokens, here = spot(b)
        pick = pick_ref[0, core, 0, j]
        slot_rows_ref[0, core, 0, here, :] = dot_nn(pick, rows[tokens, :]).astype(bf16)
        parts = dot_nn(pick, own_parts[b * few : (b + 1) * few])
        slot_gates.append(jnp.sum(parts, axis=1, keepdims=True))
    slot_gate = jnp.concatenate(slot_gates, axis=0)

    slot_rows = join(slot_rows_ref)
    gate_pre = dot_nt(slot_rows, gate_w[...])
    up_pre = dot_nt(slot_rows, up_w[...])
    sigmoid = 1.0 / (1.0 + jnp.exp(-gate_pre))
    silu = gate_pre * sigmoid
    hidden = (silu * up_pre).astype(bf16).astype(f32)
    d_gates = jnp.sum(d_raw * hidden, axis=1, keepdims=True)
    d_hidden = d_raw * slot_gate
    each = per_block * slots

    def keep(ref, value):
        for core in range(2):
            ref[0, core, 0] = value[core * each : (core + 1) * each]

    hidden = (hidden * slot_gate).astype(bf16)
    keep(hidden_ref, hidden)
    d_up = (d_hidden * silu).astype(bf16)
    keep(d_up_ref, d_up)
    d_gate = (d_hidden * up_pre * sigmoid * (1.0 + gate_pre * (1.0 - sigmoid))).astype(bf16)
    keep(d_gate_ref, d_gate)

    relay(False)

    @pl.when(step + 1 < steps)
    def _():
        prepare(step + 1)

    side_sigmoid = 1.0 / (1.0 + jnp.exp(-side_gate))
    side_silu = side_gate * side_sigmoid
    side_hidden[...] = (side_silu * side_up).astype(bf16)
    d_side[:, lanes:] = (d_side_hidden * side_silu).astype(bf16)
    d_side[:, :lanes] = (
        d_side_hidden * side_up * side_sigmoid * (1.0 + side_gate * (1.0 - side_sigmoid))
    ).astype(bf16)

    @pl.when(step == 0)
    def _():
        grad_side_ref[...] = jnp.zeros_like(grad_side_ref)
        grad_side_down_ref[...] = jnp.zeros_like(grad_side_down_ref)

    grad_side_ref[...] += dot_tn(d_side[...], rows[...])
    for c in range(2):
        grad_side_down_ref[:, c * half : (c + 1) * half] += dot_tn(side_hidden[...], side_grads[c])

    d_gate_parts = two_parts(d_gates)
    for b in range(count):
        core, j, tokens, _ = spot(b)
        there = pl.ds(j * few, few)
        back = dot_nn(spread_ref[0, core, 0, j], d_gate_parts[b * slots : (b + 1) * slots])
        d_gates_ref[0, core, 0, there, :] = jnp.sum(back, axis=1, keepdims=True)
        side_hidden_ref[0, core, 0, there, :] = side_hidden[tokens, :]
        d_side_ref[0, core, 0, there, :] = d_side[tokens, :]

    @pl.when(step == steps - 1)
    def _():
        at = (me.row // 2 * layers + me.layer) * 2 + me.core
        mine = held.at[pl.ds(pl.multiple_of(at * block, 16), block)]
        keep_rows = pltpu.make_async_copy(mine, own_rows_ref, rows_sem)
        keep_rows.start()
        work.finish()
        keep_rows.wait()


def expert_pass(layers, few, slots, units, experts, rows_own, grads, pick, spread, words, weights, side_w, side_down):
    block, half = rows_own.shape
    width = 2 * half
    hidden = weights[0].shape[0]
    per_block = block // few
    tokens = 4 * layers * block
    lanes = side_down.shape[0]

    def by_step(*tail):
        def place(step):
            row = lax.axis_index("row")
            layer = nearest_first(layers, step // 2, lax.axis_index("exp"))
            far = lax.rem(step, 2)
            x_place = row // 2 * (1 - far) + (1 - row // 2) * far
            return (x_place, 0, layer, *(0 for _ in tail))

        return pl.BlockSpec((1, 2, 1, *tail), place)

    shape = lambda *tail, kind=jnp.bfloat16: jax.ShapeDtypeStruct((2, 2, layers, *tail), kind)
    each = per_block * slots
    outs = pl.pallas_call(
        functools.partial(expert_body, layers, units, experts),
        grid=(2 * layers,),
        in_specs=[
            pl.BlockSpec(memory_space=pl.ANY),
            by_step(2, block, half),
            by_step(per_block, slots, few),
            by_step(per_block, few, slots),
            by_step(block, words.shape[1]),
            *[pl.BlockSpec(memory_space=pl.ANY)] * 5,
        ],
        out_specs=[
            pl.BlockSpec(memory_space=pl.ANY),
            by_step(each, width),
            by_step(each, width),
            by_step(each, hidden),
            by_step(each, hidden),
            by_step(each, hidden),
            by_step(block, 1),
            by_step(block, lanes),
            by_step(block, 2 * lanes),
            pl.BlockSpec((2 * lanes, width), lambda i: (0, 0)),
            pl.BlockSpec((lanes, width), lambda i: (0, 0)),
        ],
        out_shape=[
            jax.ShapeDtypeStruct((block, width), jnp.bfloat16),
            shape(each, width),
            shape(each, width),
            shape(each, hidden),
            shape(each, hidden),
            shape(each, hidden),
            shape(block, 1, kind=jnp.float32),
            shape(block, lanes),
            shape(block, 2 * lanes),
            jax.ShapeDtypeStruct((2 * lanes, width), jnp.float32),
            jax.ShapeDtypeStruct((lanes, width), jnp.float32),
        ],
        scratch_shapes=[
            *(pltpu.VMEM(w.shape, jnp.bfloat16) for w in (*weights, side_w, side_down)),
            pltpu.VMEM((tokens, width), jnp.bfloat16),
            pltpu.VMEM((2 * block, lanes), jnp.bfloat16),
            pltpu.VMEM((2 * block, 2 * lanes), jnp.bfloat16),
            pltpu.SemaphoreType.DMA((5,)),
            pltpu.SemaphoreType.DMA,
            *Gather.semaphores(layers),
        ],
        compiler_params=pltpu.CompilerParams(
            collective_id=3, has_side_effects=True, vmem_limit_bytes=62 * 1024 * 1024
        ),
    )(
        rows_own,
        grads.reshape(2, 2, layers, 2, block, half),
        pick.reshape(2, 2, layers, per_block, slots, few),
        spread.reshape(2, 2, layers, per_block, few, slots),
        words.reshape(2, 2, layers, block, -1),
        *weights,
        side_w,
        side_down,
    )
    return outs


def rotate(value, cosine, sine):
    half = value.shape[-1] // 2
    first, second = (value[..., :half], value[..., half:])
    return jnp.concatenate(
        [first * cosine - second * sine, first * sine + second * cosine], axis=-1
    )


def unrotate(value, cosine, sine):
    half = value.shape[-1] // 2
    first, second = (value[..., :half], value[..., half:])
    return jnp.concatenate(
        [first * cosine + second * sine, second * cosine - first * sine], axis=-1
    )


def sequence_layout(lengths_row, group):
    ends = jnp.cumsum(lengths_row)
    starts = ends - lengths_row
    index = jnp.arange(group, dtype=jnp.int32)
    seq_ids = jnp.sum((index[:, None] >= ends[None, :]).astype(jnp.int32), axis=1)
    member = seq_ids[:, None] == jnp.arange(lengths_row.shape[0], dtype=jnp.int32)[None, :]
    begins = jnp.sum(jnp.where(member, starts[None, :], 0), axis=1)
    return (seq_ids, index - begins)


def rotary_tables(places):
    half = ROPE // 2
    freqs = jnp.power(theta_base, -jnp.arange(half, dtype=jnp.float32) * (2.0 / ROPE))
    angle = places.astype(jnp.float32)[..., None] * freqs
    return (jnp.cos(angle), jnp.sin(angle))


def norm_back(value, factor, gain, grad, width):
    weighted = grad * gain
    inner = lax.psum(jnp.sum(weighted * value, axis=1), "col")
    d_value = (
        factor[:, None] * weighted - value * (factor * factor * factor * inner / width)[:, None]
    )
    d_gain = jnp.sum(grad * value * factor[:, None], axis=0)
    return (d_value, d_gain)


def masked_scores(query_block, keys, seq_ids, first, scale):
    size = query_block.shape[0]
    group = keys.shape[0]
    scored = (
        jnp.einsum("qhd,khd->hqk", query_block, keys, preferred_element_type=jnp.float32) * scale
    )
    query_index = first + jnp.arange(size, dtype=jnp.int32)
    key_index = jnp.arange(group, dtype=jnp.int32)
    allowed = (seq_ids[first : first + size][:, None] == seq_ids[None, :group]) & (
        key_index[None, :] <= query_index[:, None]
    )
    return jnp.where(allowed[None, :, :], scored, -1e30)


def own_slice(value, index, axis):
    size = value.shape[axis] // 2
    return lax.dynamic_slice_in_dim(value, index * size, size, axis)


def col_pair(mine, sent, axis):
    received = lax.ppermute(sent, "col", SWAP)
    first = lax.axis_index("col") == 0
    return jnp.where(
        first,
        jnp.concatenate([mine, received], axis=axis),
        jnp.concatenate([received, mine], axis=axis),
    )


def halves(value, split):
    col = lax.axis_index("col")
    return own_slice(value, col, split), own_slice(value, 1 - col, split)


def trade(value, split, join):
    return col_pair(*halves(value, split), join)


def routed_and_shared(
    tok_dev, capacity, layers, router, expert_weights, shared_own, normed_own, grads_own, words
):
    bf16 = jnp.bfloat16
    col_id = lax.axis_index("col")
    own_expert = lax.axis_index("row") * layers + lax.axis_index("exp")
    experts = router.shape[1]
    units = shared_own.shape[1]
    block, half_width = normed_own.shape
    tokens = words.shape[0]
    few = min(tok_dev, block)
    slots = -(-min(capacity, few) // 16) * 16
    blocks = tokens // few

    own_word = lax.dynamic_index_in_dim(words, own_expert // 16, 1, keepdims=False)
    own_pick = (jnp.bitwise_and(lax.shift_right_logical(own_word, own_expert % 16), 1) == 1).reshape(
        blocks, few
    )
    order = jnp.arange(few, dtype=jnp.int32)
    place = dot_nn(own_pick.astype(bf16), (order[:, None] < order[None, :]).astype(bf16)).astype(
        jnp.int32
    )
    places = jnp.arange(slots, dtype=jnp.int32)
    pick = ((place[:, None, :] == places[None, :, None]) & own_pick[:, None, :]).astype(bf16)
    spread = ((place[:, :, None] == places[None, None, :]) & own_pick[:, :, None]).astype(bf16)
    lanes = -(-(units + experts) // 128) * 128
    fill = lambda value, n: jnp.pad(value, ((0, n - value.shape[0]), (0, 0)))
    side_w = jnp.concatenate(
        [fill(jnp.concatenate([shared_own[0], router.T]), lanes), fill(shared_own[1], lanes)]
    )
    side_down = fill(shared_own[2], lanes)

    grads_all = lax.all_gather(grads_own, ("row", "exp", "col"), axis=0)
    grads_all = grads_all.reshape(experts, 2, block, half_width)
    (
        own_normed,
        slot_rows,
        slot_grads,
        hidden,
        d_gate,
        d_up,
        d_gates_all,
        side_hidden,
        d_side,
        grad_side,
        grad_side_down,
    ) = expert_pass(
        layers,
        few,
        slots,
        units,
        experts,
        normed_own,
        grads_all,
        pick,
        spread,
        words,
        expert_weights,
        side_w,
        side_down,
    )
    spread = spread.reshape(2, 2, layers, -1, few, slots)
    gate_weight, up_weight, down_weight = expert_weights
    (d_normed,) = made_scatter(
        (d_gate, d_up), (gate_weight, up_weight), spread, d_side, side_w, (), (), layers, 4
    )
    flat = lambda *values: tuple(value.reshape(-1, value.shape[-1]) for value in values)
    out_parts = (
        (hidden,),
        (down_weight,),
        spread,
        side_hidden,
        side_down,
        flat(d_gate, d_up, hidden),
        flat(slot_rows, slot_rows, slot_grads),
    )
    grad_shared = jnp.stack(
        [grad_side[:units], grad_side[lanes : lanes + units], grad_side_down[:units]]
    )

    d_gates = lax.psum(
        lax.all_to_all(
            d_gates_all.reshape(experts, block), ("row", "exp"), split_axis=0, concat_axis=0, tiled=True
        ),
        "col",
    ).T
    own_probs = jax.nn.softmax(dot_nn(own_normed, router), axis=1)
    own_words = lax.dynamic_slice_in_dim(words, own_expert * block, block, 0)
    numbers = jnp.arange(experts, dtype=jnp.int32)
    picks = (
        jnp.bitwise_and(
            lax.shift_right_logical(own_words[:, numbers // 16], (numbers % 16)[None, :]), 1
        )
        == 1
    )
    selected = jnp.where(picks, own_probs, 0.0)
    own_total = jnp.sum(selected, axis=1, keepdims=True)
    own_gates = selected / own_total
    d_selected = (d_gates - jnp.sum(d_gates * own_gates, axis=1, keepdims=True)) / own_total
    d_router_probs = jnp.where(picks, d_selected, 0.0)
    d_logits = own_probs * (
        d_router_probs - jnp.sum(own_probs * d_router_probs, axis=1, keepdims=True)
    )
    router_half = lax.dynamic_slice_in_dim(router, col_id * half_width, half_width, 0)
    grad_router = lax.dot_general(
        normed_own.astype(jnp.float32),
        d_logits,
        (((0,), (0,)), ((), ())),
        precision=lax.Precision.HIGHEST,
        preferred_element_type=jnp.float32,
    )
    d_normed = d_normed + lax.dot_general(
        d_logits,
        router_half.astype(jnp.float32),
        (((1,), (1,)), ((), ())),
        precision=lax.Precision.HIGHEST,
        preferred_element_type=jnp.float32,
    )
    return (d_normed, out_parts, (grad_shared, grad_router))


def per_device(
    layer_input,
    lengths,
    routes,
    norm1_gain,
    w_query,
    w_latent,
    latent_gain,
    w_kv,
    w_out,
    norm2_gain,
    shared_gate,
    shared_up,
    shared_down,
    router,
    expert_gate,
    expert_up,
    expert_down,
    cotangent,
):
    row_id = lax.axis_index("row")
    col_id = lax.axis_index("col")
    exp_id = lax.axis_index("exp")
    rows_n, cols_n, exps_n = (lax.axis_size(name) for name in ("row", "col", "exp"))
    experts = rows_n * exps_n
    own_expert = row_id * exps_n + exp_id
    tok_dev = routes.shape[1]
    topk_count = routes.shape[2]
    capacity = max(2, 3 * tok_dev * topk_count // (2 * experts))
    slots = -(-capacity // 16) * 16
    block, half_width = layer_input.shape
    width = half_width * cols_n
    group = block * rows_n
    tokens = group * exps_n
    heads_here = w_kv.shape[1] // (QK_NOPE + V_DIM)
    head_dim = QK_NOPE + ROPE
    scale = 1.0 / math.sqrt(head_dim)
    query_rows = group // 2
    bf16 = jnp.bfloat16

    query_halves, layer_input = lax.optimization_barrier((halves(w_query, 1), layer_input))
    w_query_own = col_pair(*query_halves, 0)
    seq_ids, places = sequence_layout(lengths[0], group)
    cosine, sine = rotary_tables(places)

    group_input, w_latent_all = gather_several(
        (layer_input, w_latent[0].T), 1, 10, (False, "lanes")
    )
    group_input, w_out, cotangent = lax.optimization_barrier((group_input, w_out, cotangent))
    w_out_own = trade(w_out, 0, 1)
    group_input = group_input.astype(jnp.float32)
    factor_group = lax.rsqrt(jnp.mean(group_input * group_input, axis=1) + epsilon)
    normed_group = (group_input * factor_group[:, None] * norm1_gain).astype(bf16)
    query_pre = dot_nn(normed_group, w_query_own).reshape(group, heads_here, head_dim)
    queries = jnp.concatenate(
        [
            query_pre[..., :QK_NOPE],
            rotate(query_pre[..., QK_NOPE:], cosine[:, None, :], sine[:, None, :]),
        ],
        axis=2,
    ).astype(bf16)
    queries, shared_gate, shared_up, shared_down = lax.optimization_barrier(
        (queries, shared_gate, shared_up, shared_down)
    )
    units = shared_gate.shape[1] // (cols_n * exps_n)
    shared_parts = jnp.stack(
        [
            lax.dynamic_index_in_dim(
                part.reshape(cols_n, exps_n, units, half_width), exp_id, 1, keepdims=False
            )
            for part in (shared_gate.T, shared_up.T, shared_down)
        ]
    )
    shared_own = trade(shared_parts, 1, 3)[:, 0]

    latent = dot_nt(normed_group, w_latent_all)
    compressed_raw = latent[:, :KV_RANK]
    kv_factor = lax.rsqrt(jnp.mean(compressed_raw * compressed_raw, axis=1) + epsilon)
    compressed = (compressed_raw * kv_factor[:, None] * latent_gain).astype(bf16)
    rotary_key = rotate(latent[:, KV_RANK:], cosine, sine).astype(bf16)
    key_value = (
        dot_nn(compressed, w_kv).astype(bf16).reshape(group, heads_here, QK_NOPE + V_DIM)
    )
    keys = jnp.concatenate(
        [
            key_value[..., :QK_NOPE],
            jnp.broadcast_to(rotary_key[:, None, :], (group, heads_here, ROPE)),
        ],
        axis=2,
    )
    values = key_value[..., QK_NOPE:]
    block_outputs = []
    block_totals = []
    for first in range(0, group, query_rows):
        last = first + query_rows
        scores = masked_scores(queries[first:last], keys[:last], seq_ids, first, scale)
        highest = jnp.max(scores, axis=2, keepdims=True)
        log_total = highest + jnp.log(jnp.sum(jnp.exp(scores - highest), axis=2, keepdims=True))
        probs_low = jnp.exp(scores - log_total).astype(bf16)
        block_outputs.append(
            jnp.einsum(
                "hqk,khd->qhd", probs_low, values[:last], preferred_element_type=jnp.float32
            ).astype(bf16)
        )
        block_totals.append(log_total)
    attended = jnp.concatenate(block_outputs, axis=0).reshape(group, heads_here * V_DIM)

    input_wide = layer_input.astype(jnp.float32)
    hidden_state = input_wide + scatter(dot_nn(attended, w_out_own).astype(bf16), 1, 2)
    words_n = -(-experts // 16)
    word_of = jnp.arange(words_n, dtype=jnp.int32)[:, None, None]
    bits = jnp.where(routes // 16 == word_of, jnp.left_shift(1, routes % 16), 0)
    bits = jnp.sum(bits, axis=2).astype(jnp.float32)
    padded = -(-tok_dev // 128) * 128
    bits = jnp.pad(bits, ((0, 0), (0, padded - tok_dev)))
    is_here = jnp.arange(experts, dtype=jnp.int32) == own_expert
    bits = jnp.where(is_here[:, None, None], bits[None], 0.0).reshape(experts * words_n, padded)
    bits, hidden_state = lax.optimization_barrier((bits, hidden_state))
    bits = small_sum(bits, exps_n, 8).reshape(experts, words_n, cols_n, padded)[..., :tok_dev]
    words_all = bits.astype(jnp.int32).transpose(0, 2, 3, 1).reshape(tokens, words_n)

    gain_two = lax.dynamic_slice_in_dim(norm2_gain, col_id * half_width, half_width)
    square = lax.psum(jnp.sum(hidden_state * hidden_state, axis=1), "col")
    factor_two = lax.rsqrt(square / width + epsilon)
    normed_two = (hidden_state * factor_two[:, None] * gain_two).astype(bf16)
    pieces = max(1, exps_n // 4)
    feed = functools.partial(
        routed_and_shared,
        tok_dev,
        capacity,
        exps_n,
        router,
        (expert_gate[0].T, expert_up[0].T, expert_down[0].T),
        shared_own,
    )
    if pieces == 1:
        d_normed, out_parts, weight_grads = feed(normed_two, cotangent, words_all)
    else:
        piece_rows = block // pieces

        def one_piece(total, items):
            d_rows, out_parts, grads = feed(*items)
            *out_parts, job_a, job_b = out_parts
            (branch_rows,) = made_scatter(*out_parts, (), (), exps_n, 9)
            grads = (*grads, tuple(dot_tn(a, b) for a, b in zip(job_a, job_b)))
            return (jax.tree.map(jnp.add, total, grads), (d_rows, branch_rows))

        split = lambda value: value.reshape(pieces, piece_rows, half_width)
        word_pieces = words_all.reshape(experts, pieces, piece_rows, words_n)
        items = (
            split(normed_two),
            split(cotangent),
            word_pieces.transpose(1, 0, 2, 3).reshape(pieces, -1, words_n),
        )
        start = (
            jnp.zeros((3, units, width), jnp.float32),
            jnp.zeros((half_width, experts), jnp.float32),
            (jnp.zeros(expert_gate.shape[:0:-1], jnp.float32),) * 3,
        )
        weight_grads, (d_normed, branch) = lax.scan(one_piece, start, items)
        d_normed, branch = (v.reshape(block, half_width) for v in (d_normed, branch))
    grad_shared, grad_router = weight_grads[:2]
    expert_grads = weight_grads[2] if pieces > 1 else None
    grad_shared = trade(grad_shared.astype(bf16)[:, None], 3, 1)
    d_normed, grad_shared = lax.optimization_barrier((d_normed, grad_shared))
    grad_shared = lax.all_gather(grad_shared, "exp", axis=2, tiled=False)
    d_norm_two, grad_gain_two = norm_back(hidden_state, factor_two, gain_two, d_normed, width)
    d_hidden_state = cotangent.astype(jnp.float32) + d_norm_two

    d_branch = gather(d_hidden_state.astype(bf16), 1, 1)
    grad_w_out = trade(dot_tn(attended, d_branch).astype(bf16), 1, 0)
    d_attended = dot_nt(d_branch, w_out_own).astype(bf16).reshape(group, heads_here, V_DIM)
    d_query_blocks = []
    d_keys = jnp.zeros((group, heads_here, head_dim), jnp.float32)
    d_values = jnp.zeros((group, heads_here, V_DIM), jnp.float32)
    for number, first in enumerate(range(0, group, query_rows)):
        last = first + query_rows
        query_block = queries[first:last]
        d_block = d_attended[first:last]
        scores = masked_scores(query_block, keys[:last], seq_ids, first, scale)
        probs = jnp.exp(scores - block_totals[number])
        d_probs = jnp.einsum(
            "qhd,khd->hqk", d_block, values[:last], preferred_element_type=jnp.float32
        )
        delta = jnp.sum(probs * d_probs, axis=2, keepdims=True)
        d_scores = (probs * (d_probs - delta)).astype(bf16)
        d_query_blocks.append(
            jnp.einsum("hqk,khd->qhd", d_scores, keys[:last], preferred_element_type=jnp.float32)
            * scale
        )
        d_keys = d_keys.at[:last].add(
            jnp.einsum("hqk,qhd->khd", d_scores, query_block, preferred_element_type=jnp.float32)
            * scale
        )
        d_values = d_values.at[:last].add(
            jnp.einsum(
                "hqk,qhd->khd", probs.astype(bf16), d_block, preferred_element_type=jnp.float32
            )
        )
    d_query = jnp.concatenate(d_query_blocks, axis=0)
    d_query_pre = (
        jnp.concatenate(
            [
                d_query[..., :QK_NOPE],
                unrotate(d_query[..., QK_NOPE:], cosine[:, None, :], sine[:, None, :]),
            ],
            axis=2,
        )
        .astype(bf16)
        .reshape(group, heads_here * head_dim)
    )
    d_key_value = (
        jnp.concatenate([d_keys[..., :QK_NOPE], d_values], axis=2)
        .astype(bf16)
        .reshape(group, heads_here * (QK_NOPE + V_DIM))
    )
    grad_w_kv = dot_tn(compressed, d_key_value)
    d_latent_sum = scatter(
        jnp.concatenate(
            [dot_nt(d_key_value, w_kv), jnp.sum(d_keys[..., QK_NOPE:], axis=1)], axis=1
        ).astype(bf16),
        1,
        5,
        by_rows=True,
    )
    own_first = (row_id * cols_n + col_id) * (group // (rows_n * cols_n))

    def own_tokens(value):
        return lax.dynamic_slice_in_dim(value, own_first, group // (rows_n * cols_n), 0)

    raw_own, factor_own = own_tokens(compressed_raw), own_tokens(kv_factor)
    d_compressed = d_latent_sum[:, :KV_RANK]
    weighted = d_compressed * latent_gain
    grad_latent_gain = jnp.sum(d_compressed * raw_own * factor_own[:, None], axis=0)
    inner = jnp.sum(weighted * raw_own, axis=1)
    d_raw = (
        factor_own[:, None] * weighted
        - raw_own * (factor_own * factor_own * factor_own * inner / KV_RANK)[:, None]
    )
    d_latent = gather(
        jnp.concatenate(
            [d_raw, unrotate(d_latent_sum[:, KV_RANK:], own_tokens(cosine), own_tokens(sine))],
            axis=1,
        ).astype(bf16),
        1,
        6,
        by_rows=True,
    )
    slab = w_latent.shape[1]
    slab_start = col_id * half_width + row_id * slab
    normed_slab = lax.dynamic_slice_in_dim(normed_group, slab_start, slab, 1)
    grad_w_latent = dot_tn(d_latent, normed_slab)
    grad_w_query = trade(dot_tn(normed_group, d_query_pre).astype(bf16), 0, 1)
    d_gathered = dot_nt(d_query_pre, w_query_own)
    piece = lax.dynamic_slice_in_dim(d_gathered, slab_start, slab, 1) + dot_nt(
        d_latent, w_latent[0]
    )
    d_gathered = lax.dynamic_update_slice_in_dim(d_gathered, piece, slab_start, 1)
    d_first = scatter(d_gathered.astype(bf16), 1, 2)
    gain_one = lax.dynamic_slice_in_dim(norm1_gain, col_id * half_width, half_width)
    factor_one = lax.dynamic_slice_in_dim(factor_group, row_id * block, block)
    d_norm_one, grad_gain_one = norm_back(input_wide, factor_one, gain_one, d_first, width)
    input_grad = d_hidden_state + d_norm_one
    if pieces == 1:
        out_parts, input_grad = lax.optimization_barrier((out_parts, input_grad))
        branch, *expert_grads = made_scatter(*out_parts, exps_n, 9)
    output = (hidden_state + branch).astype(bf16)

    small = jnp.concatenate(
        [
            grad_gain_one[None],
            grad_gain_two[None],
            jnp.pad(grad_latent_gain, (0, half_width - KV_RANK))[None],
            grad_router.T,
        ],
        axis=0,
    )
    small = jnp.pad(small, ((0, -small.shape[0] % 8), (0, 0)))
    small = small_sum(small, exps_n, 7)
    summed_latent_gain = small[2, :KV_RANK] + small[2, half_width : half_width + KV_RANK]

    grad_shared, grad_w_query = lax.optimization_barrier((grad_shared, grad_w_query))
    grad_shared = grad_shared.reshape(3, cols_n * exps_n * units, half_width).astype(jnp.float32)
    summed = lax.psum(
        (grad_w_query, grad_w_latent.astype(bf16), grad_w_kv.astype(bf16), grad_w_out), "exp"
    )
    return (
        output,
        input_grad,
        small[0],
        summed[0].astype(jnp.float32),
        summed[1].T.astype(jnp.float32)[None],
        summed_latent_gain,
        summed[2].astype(jnp.float32),
        summed[3].astype(jnp.float32),
        small[1],
        grad_shared[0].T,
        grad_shared[1].T,
        grad_shared[2],
        small[3 : 3 + experts].T,
        *(grad.T[None] for grad in expert_grads),
    )


def solution(mesh):
    placed = (
        P(("row", "exp"), "col"),
        P("exp", None),
        P("col", ("row", "exp"), None),
        P(),
        P("col", "row"),
        P("col", "row", None),
        P(),
        P(None, ("row", "col")),
        P("row", "col"),
        P(),
        P("col", "row"),
        P("col", "row"),
        P("row", "col"),
        P(),
        P(("row", "exp"), None, "col"),
        P(("row", "exp"), None, "col"),
        P(("row", "exp"), None, "col"),
        P(("row", "exp"), "col"),
    )
    return jax.shard_map(
        per_device,
        mesh=mesh,
        in_specs=placed,
        out_specs=(
            P(("row", "exp"), "col"),
            P(("row", "exp"), "col"),
            P(),
            P("col", "row"),
            P("col", "row", None),
            P(),
            P(None, ("row", "col")),
            P("row", "col"),
            P(),
            P("col", "row"),
            P("col", "row"),
            P("row", "col"),
            P(),
            P(("row", "exp"), None, "col"),
            P(("row", "exp"), None, "col"),
            P(("row", "exp"), None, "col"),
        ),
        check_vma=False,
    )
```
